32 devices in a mesh: section: 2 (over core), fsdp: 8 (over z, x), tp: 2 (over y).
Axes of the slice: x: 2, y: 2, z: 4, core: 2. Of those that a mesh axis runs over, the one named last changes fastest.
Arguments:
- inputs: bfloat16 [8, 2, 512, 2048], P('fsdp', None, 'tp'), may hold values from -6 to 6
- cotangent: bfloat16 [8, 2, 512, 2048], P('fsdp', None, 'tp'), may hold values from -6 to 6
- norm_gain: bfloat16 [2, 2048], P('section', 'fsdp'), may hold values from 0.5 to 1.5
- w_zx: bfloat16 [2, 2048, 2, 4096], P('section', 'fsdp', None, 'tp'), may hold values from -1 to 1
- w_bc: bfloat16 [2, 2048, 256], P('section', 'fsdp'), may hold values from -0.125 to 0.125
- w_dt: bfloat16 [2, 2048, 64], P('section', 'fsdp', 'tp'), may hold values from -0.125 to 0.125
- conv_x: float32 [2, 4, 4096], P('section', None, 'tp'), may hold values from -3 to 3
- conv_xb: float32 [2, 4096], P('section', 'tp'), may hold values from -0.5 to 0.5
- conv_bc: float32 [2, 4, 256], P('section'), may hold values from -3 to 3
- conv_bcb: float32 [2, 256], P('section'), may hold values from -0.5 to 0.5
- dt_bias: float32 [2, 64], P('section', 'tp'), may hold values from -5 to -1
- a_log: float32 [2, 64], P('section', 'tp'), may hold values from 0 to 2.77
- d_skip: float32 [2, 64], P('section', 'tp'), may hold values from 0.5 to 2
- gate_gain: float32 [2, 4096], P('section', 'tp'), may hold values from 0.5 to 1.5
- w_out: bfloat16 [2, 2048, 4096], P('section', 'fsdp', 'tp'), may hold values from -0.09375 to 0.09375
Outputs:
- outputs: float32 [8, 2, 512, 2048], P('fsdp', 'section', 'tp')
- grad_inputs: float32 [8, 2, 512, 2048], P('fsdp', 'section', 'tp')
- grad_norm_gain: float32 [2, 2048], P('section', 'fsdp')
- grad_w_zx: float32 [2, 2048, 2, 4096], P('section', 'fsdp', None, 'tp')
- grad_w_bc: float32 [2, 2048, 256], P('section', 'fsdp')
- grad_w_dt: float32 [2, 2048, 64], P('section', 'fsdp', 'tp')
- grad_conv_x: float32 [2, 4, 4096], P('section', None, 'tp')
- grad_conv_xb: float32 [2, 4096], P('section', 'tp')
- grad_conv_bc: float32 [2, 4, 256], P('section')
- grad_conv_bcb: float32 [2, 256], P('section')
- grad_dt_bias: float32 [2, 64], P('section', 'tp')
- grad_a_log: float32 [2, 64], P('section', 'tp')
- grad_d_skip: float32 [2, 64], P('section', 'tp')
- grad_gate_gain: float32 [2, 4096], P('section', 'tp')
- grad_w_out: float32 [2, 2048, 4096], P('section', 'fsdp', 'tp')
The draws below stay inside these ranges and needn't reach their ends.
All inputs are finite; a program needn't handle non-finite values.
Results may differ from the reference program's by a relative error of at most 0.015.
Values may be sent and summed in bfloat16 or wider, within the bound.
A program may use at most 320 MiB of HBM per device.

```python
import jax
import jax.numpy as jnp
from jax import lax

D = 2048
H = 64
NS = 128
CONV = 4
BLOCK = 256
MB_TOK = 512
MICRO = 2
DI = 4096
SEQS = 8
LAYERS = 2


def draw_w_zx(key, part):
    key = jax.random.fold_in(key, 11)
    channel_pos = jnp.arange(DI, dtype=jnp.float32) / (DI - 1)
    spread_row = 0.5 * 4.0 ** channel_pos
    values = jax.random.truncated_normal(key, -3.0, 3.0, (LAYERS, D, 2, DI), jnp.float32)
    scales = jnp.stack([jnp.ones((DI,), jnp.float32), spread_row])
    return (values * scales[None, None] / D ** 0.5).astype(jnp.bfloat16)


def raised(drawn, rng, source, target, blocks, factor):
    owner, partner = [(jnp.arange(drawn.shape[dim]) // (drawn.shape[dim] // blocks)).reshape([-1 if axis == dim else 1 for axis in range(drawn.ndim)]) for dim in (source, target)]
    chosen = jax.random.permutation(rng, blocks)[partner]
    strong = (owner == chosen) | (owner == (partner + blocks // 2) % blocks)
    return jnp.where(strong, factor * drawn, drawn)


def steps_of(rng, dims, split, least, top_value):
    def one(dim, blocks):
        draws = jax.random.uniform(jax.random.fold_in(jax.random.fold_in(rng, 6), dim), (blocks,), jnp.float32, least / len(split), top_value / len(split))
        return jnp.repeat(jnp.exp(draws), dims[dim] // blocks).reshape((-1,) + (1,) * (len(dims) - dim - 1))

    gain = one(*split[0])
    for cut in split[1:]:
        gain = gain * one(*cut)
    return gain


def centred(stream_key, shape, spread, reach, cuts=(), held_as=jnp.bfloat16):
    array = spread * jax.random.normal(stream_key, shape, jnp.float32)
    if cuts:
        array = array * steps_of(stream_key, shape, cuts, -0.22, 0.18)
    return jnp.clip(array, -reach, reach).astype(held_as)


def bell_draw_with(rng, shape, width, reach, cuts, heavy, held_as=jnp.bfloat16):
    array = width * jax.random.normal(rng, shape, jnp.float32)
    if cuts:
        array = array * steps_of(rng, shape, cuts, -0.22, 0.18)
    return jnp.clip(raised(array, jax.random.fold_in(rng, 3), *heavy), -reach, reach).astype(held_as)


def setup_inputs(seed: int = 0) -> dict:
    seeds = jax.random.split(jax.random.key(seed), 16)
    inputs = centred(seeds[0], (SEQS, MICRO, MB_TOK, D), 1.0, 6.0, ((0, 8), (2, 2)))
    cotangent = bell_draw_with(seeds[1], (SEQS, MICRO, MB_TOK, D), 1.0, 6.0, ((0, 8), (2, 2)), (0, 3, 8, 2.0))
    norm_gain = jnp.clip(1.0 + 0.1 * jax.random.normal(seeds[2], (LAYERS, D), jnp.float32), 0.5, 1.5).astype(jnp.bfloat16)
    w_zx = draw_w_zx(jax.random.fold_in(seeds[15], 71), 0)
    w_bc = centred(seeds[4], (LAYERS, D, 2 * NS), D ** -0.5, 0.125, ((0, 2), (1, 8)))
    w_dt = centred(seeds[5], (LAYERS, D, H), D ** -0.5, 0.125, ((0, 2), (1, 8), (2, 2)))
    conv_x = centred(seeds[6], (LAYERS, CONV, DI), CONV ** -0.5, 3.0, ((0, 2), (2, 2)), jnp.float32)
    conv_xb = jnp.clip(jax.random.uniform(seeds[7], (LAYERS, DI), jnp.float32, -0.5, 0.5) * steps_of(seeds[7], (LAYERS, DI), ((0, 2), (1, 2)), -0.4, 0.0), -0.5, 0.5)
    conv_bc = centred(seeds[8], (LAYERS, CONV, 2 * NS), CONV ** -0.5, 3.0, ((0, 2),), jnp.float32)
    conv_bcb = jnp.clip(jax.random.uniform(seeds[9], (LAYERS, 2 * NS), jnp.float32, -0.5, 0.5) * steps_of(seeds[9], (LAYERS, 2 * NS), ((0, 2),), -0.4, 0.0), -0.5, 0.5)
    dt_bias = jnp.clip(-5.0 + 4.0 * jax.random.uniform(seeds[10], (LAYERS, H), jnp.float32) ** steps_of(seeds[10], (LAYERS, H), ((0, 2), (1, 2)), -0.2, 0.2), -5.0, -1.0)
    a_log = jnp.clip(2.77 * jax.random.uniform(seeds[11], (LAYERS, H), jnp.float32) ** steps_of(seeds[11], (LAYERS, H), ((0, 2), (1, 2)), -0.2, 0.2), 0.0, 2.77)
    d_skip = jnp.clip(0.5 + 1.5 * jax.random.uniform(seeds[12], (LAYERS, H), jnp.float32) ** steps_of(seeds[12], (LAYERS, H), ((0, 2), (1, 2)), -0.2, 0.2), 0.5, 2.0)
    gate_gain = jnp.clip(1.0 + 0.1 * jax.random.normal(seeds[13], (LAYERS, DI), jnp.float32), 0.5, 1.5)
    w_out = centred(seeds[14], (LAYERS, D, DI), DI ** -0.5, 0.09375, ((0, 2), (1, 8), (2, 2)))
    return {"inputs": inputs, "cotangent": cotangent, "norm_gain": norm_gain, "w_zx": w_zx, "w_bc": w_bc, "w_dt": w_dt, "conv_x": conv_x, "conv_xb": conv_xb, "conv_bc": conv_bc, "conv_bcb": conv_bcb, "dt_bias": dt_bias, "a_log": a_log, "d_skip": d_skip, "gate_gain": gate_gain, "w_out": w_out}


NORM_EPSILON = 1e-05
HIGHEST_PRECISION = lax.Precision.HIGHEST

@jax.custom_vjp
def low(v):
    return lax.optimization_barrier(v.astype(jnp.bfloat16)).astype(jnp.float32)

@jax.custom_vjp
def low_back(v):
    return v

def low_keep(v):
    return (low(v), None)

def low_pass(kept, grad):
    return (grad,)

def back_keep(v):
    return (v, None)

def back_low(kept, grad):
    return (low(grad),)
low.defvjp(low_keep, low_pass)
low_back.defvjp(back_keep, back_low)

def causal_conv(pre_rows, carried_rows, kernel, offset):
    kernel_width = kernel.shape[0]
    length = pre_rows.shape[0]
    padded = jnp.concatenate([carried_rows, pre_rows], axis=0)
    result = offset[None, :] + kernel[kernel_width - 1][None, :] * padded[kernel_width - 1:]
    for offset_step in range(kernel_width - 1):
        result = result + kernel[offset_step][None, :] * padded[offset_step:offset_step + length]
    return (result, padded[length:])

def scan_heads(head_inputs, step_sizes, decay_rates, in_map, out_map, carried, block_len):
    length = head_inputs.shape[0]
    log_decay = step_sizes * decay_rates[None, :]
    positions = jnp.arange(block_len)
    causal = positions[:, None] >= positions[None, :]
    pieces = []
    for number in range(length // block_len):
        first_row = number * block_len
        scaled_inputs = head_inputs[first_row:first_row + block_len] * step_sizes[first_row:first_row + block_len][:, :, None]
        block_in = in_map[first_row:first_row + block_len]
        block_out = out_map[first_row:first_row + block_len]
        cumulative = jnp.cumsum(log_decay[first_row:first_row + block_len], axis=0)
        by_head = cumulative.T
        log_gaps = by_head[:, :, None] - by_head[:, None, :]
        weights = jnp.exp(jnp.where(causal[None], log_gaps, -10000.0))
        scores = jnp.dot(block_out, block_in.T, precision=HIGHEST_PRECISION)
        within = jnp.einsum('hij,jhp->ihp', weights * scores[None], scaled_inputs, precision=HIGHEST_PRECISION)
        entering = jnp.einsum('in,hpn->ihp', block_out, carried, precision=HIGHEST_PRECISION) * jnp.exp(cumulative)[:, :, None]
        pieces.append(within + entering)
        remaining = jnp.exp(cumulative[-1:] - cumulative)
        carried = carried * jnp.exp(cumulative[-1])[:, None, None] + jnp.einsum('jhp,jn->hpn', scaled_inputs * remaining[:, :, None], block_in, precision=HIGHEST_PRECISION)
    return (jnp.concatenate(pieces, axis=0), carried)

def mix_tokens(pre_zx, pre_bc, pre_dt, head_params, carried, tail_x, tail_bc):
    conv_x, conv_xb, conv_bc, conv_bcb, dt_bias, a_log, d_skip = head_params
    head_count = pre_dt.shape[1]
    state_size = pre_bc.shape[1] // 2
    length = pre_zx.shape[0]
    conv_rows_x, tail_x = causal_conv(pre_zx[:, 1], tail_x, conv_x, conv_xb)
    conv_rows_bc, tail_bc = causal_conv(pre_bc, tail_bc, conv_bc, conv_bcb)
    head_inputs = jax.nn.silu(conv_rows_x).reshape(length, head_count, -1)
    shared = jax.nn.silu(conv_rows_bc)
    step_sizes = jax.nn.softplus(pre_dt + dt_bias[None, :])
    decay_rates = -jnp.exp(a_log)
    outputs, carried = scan_heads(head_inputs, step_sizes, decay_rates, shared[:, :state_size], shared[:, state_size:], carried, BLOCK)
    outputs = outputs + d_skip[None, :, None] * head_inputs
    gated_rows = outputs.reshape(length, -1) * jax.nn.silu(pre_zx[:, 0])
    return (gated_rows, lax.optimization_barrier(jnp.sum(gated_rows * gated_rows, axis=1)), carried, tail_x, tail_bc)

def norm_rows(residual, gain_row):
    scale_rows = lax.rsqrt(lax.optimization_barrier(jnp.mean(residual * residual, axis=1, keepdims=True)) + NORM_EPSILON)
    return residual * scale_rows * gain_row[None, :]

def gate_norm(gated_rows, squares, gain_row):
    return gated_rows * lax.rsqrt(squares[:, None] / DI + NORM_EPSILON) * gain_row[None, :]

def one_layer(residual, weights):
    norm_gain, w_zx, w_bc, w_dt, conv_x, conv_xb, conv_bc, conv_bcb, dt_bias, a_log, d_skip, gate_gain, w_out = weights
    normed = low(norm_rows(residual, norm_gain))
    pre_zx = low_back(jnp.einsum('td,dkc->tkc', normed, w_zx, precision=HIGHEST_PRECISION))
    pre_bc = low_back(jnp.dot(normed, w_bc, precision=HIGHEST_PRECISION))
    pre_dt = low_back(jnp.dot(normed, w_dt, precision=HIGHEST_PRECISION))
    head_count = pre_dt.shape[1]
    carried = jnp.zeros((head_count, pre_zx.shape[2] // head_count, pre_bc.shape[1] // 2), jnp.float32)
    tail_x = jnp.zeros((CONV - 1, pre_zx.shape[2]), jnp.float32)
    tail_bc = jnp.zeros((CONV - 1, pre_bc.shape[1]), jnp.float32)
    head_params = (conv_x, conv_xb, conv_bc, conv_bcb, dt_bias, a_log, d_skip)
    gated_rows, squares, unused_state, unused_tail_x, unused_tail_bc = mix_tokens(pre_zx, pre_bc, pre_dt, head_params, carried, tail_x, tail_bc)
    mixed_rows = low(gate_norm(gated_rows, squares, gate_gain))
    branch = low_back(jnp.einsum('tc,dc->td', mixed_rows, w_out, precision=HIGHEST_PRECISION))
    return residual + branch

def reference(inputs, cotangent, norm_gain, w_zx, w_bc, w_dt, conv_x, conv_xb, conv_bc, conv_bcb, dt_bias, a_log, d_skip, gate_gain, w_out):
    weights = tuple((tensor.astype(jnp.float32) for tensor in (norm_gain, w_zx, w_bc, w_dt, conv_x, conv_xb, conv_bc, conv_bcb, dt_bias, a_log, d_skip, gate_gain, w_out)))
    start_rows = inputs.astype(jnp.float32)
    checked_layer = jax.checkpoint(one_layer)

    def one_sequence(sequence, layer_weights):
        hidden = sequence
        for layer_index in range(LAYERS):
            hidden = checked_layer(hidden, tuple((tensor[layer_index] for tensor in layer_weights)))
        return hidden

    def forward(start_values, layer_weights):
        grouped = start_values.reshape(SEQS // 2, 2, MICRO * MB_TOK, D)

        def advance(carry_value, group_rows):
            return (carry_value, jax.vmap(one_sequence, in_axes=(0, None))(group_rows, layer_weights))
        unused_carry, results = lax.scan(advance, jnp.zeros((), jnp.float32), grouped)
        return results.reshape(start_values.shape)
    outputs, pullback = jax.vjp(forward, start_rows, weights)
    grad_inputs, grad_weights = pullback(cotangent.astype(jnp.float32))
    return (outputs, grad_inputs, grad_weights[0], grad_weights[1], grad_weights[2], grad_weights[3], grad_weights[4], grad_weights[5], grad_weights[6], grad_weights[7], grad_weights[8], grad_weights[9], grad_weights[10], grad_weights[11], grad_weights[12])
```

```python
import jax
import jax.numpy as jnp
from jax import lax
from jax.experimental import pallas as pl
from jax.experimental.pallas import tpu as pltpu
from jax.sharding import PartitionSpec as P

CONV = 4
DI = 4096
EPS = 1e-05
CHUNK = 128
LANES = 128
HALO = 8
NEG = -10000.0
HIGHEST = lax.Precision.HIGHEST
F32 = jnp.float32
BF16 = jnp.bfloat16
VMEM_LIMIT = 56 * 1024 * 1024


def sigmoid(v):
    return 0.5 * jnp.tanh(0.5 * v) + 0.5


def dot_nn(a, b):
    return lax.dot_general(a, b, (((1,), (0,)), ((), ())), preferred_element_type=F32)


def dot_nt(a, b):
    return lax.dot_general(a, b, (((1,), (1,)), ((), ())), preferred_element_type=F32)


def dot_exact(a, b):
    return lax.dot_general(
        a, b, (((1,), (0,)), ((), ())), preferred_element_type=F32, precision=HIGHEST
    )


def split(a):
    high = a.astype(BF16)
    return high, (a - high.astype(F32)).astype(BF16)


def dot3(a, b, dot=dot_nn):
    return dot(a[0], b[0]) + (dot(a[1], b[0]) + dot(a[0], b[1]))


def tri(shape, keep):
    rows = lax.broadcasted_iota(jnp.int32, shape, 0)
    cols = lax.broadcasted_iota(jnp.int32, shape, 1)
    return keep(rows, cols)


def expand(columns, spread, heads):
    high = columns.astype(BF16).astype(F32)
    rest = columns - high
    packed = high + pltpu.roll(rest, heads, 1)
    return dot_nn(packed.astype(BF16), spread)


def step_terms(pre_dt, slab, channels, heads, spread):
    lane = lax.broadcasted_iota(jnp.int32, pre_dt.shape, 1)
    live = lane < heads
    arg = pre_dt + slab[5:6, channels : channels + LANES]
    dt = jnp.where(live, jnp.maximum(arg, 0.0) + jnp.log1p(jnp.exp(-jnp.abs(arg))), 0.0)
    decay = slab[6:7, channels : channels + LANES]
    lower = tri((CHUNK, CHUNK), lambda r, c: r >= c).astype(F32)
    cum = dot_exact(lower, dt * decay)
    last = cum[CHUNK - 1 : CHUNK, :]
    grown = jnp.where(live, jnp.exp(cum), 0.0)
    left = jnp.where(live, jnp.exp(last - cum), 0.0)
    wide = expand(jnp.concatenate([dt, grown, left], axis=0), spread, heads)
    return arg, dt, decay, cum, wide[:CHUNK], wide[CHUNK : 2 * CHUNK], wide[2 * CHUNK :]


def conv_rows(buffer, slab):
    out = slab[4:5, :] + slab[CONV - 1 : CONV, :] * buffer[HALO : HALO + CHUNK, :]
    for k in range(CONV - 1):
        first = HALO - (CONV - 1) + k
        out = out + slab[k : k + 1, :] * buffer[first : first + CHUNK, :]
    return out


def forward_kernel(
    pre, tail, start, slab, spread, u, sq, y, entering, leaving, state, buffer, *, channels, heads
):
    step = pl.program_id(0)
    size = channels + 2 * LANES

    @pl.when(step == 0)
    def _():
        state[...] = start[...]
        buffer[0:HALO, :] = tail[...]

    @pl.when(step > 0)
    def _():
        buffer[0:HALO, :] = buffer[CHUNK : CHUNK + HALO, :]

    buffer[HALO:, :] = pre[:, channels : channels + size]
    entering[0] = state[...]
    conv = conv_rows(buffer, slab)
    act = conv * sigmoid(conv)
    xs = act[:, :channels]
    in_map = act[:, channels : channels + LANES]
    out_map = act[:, channels + LANES :]
    arg, dt, decay, cum, dt_w, grown_w, left_w = step_terms(
        pre[:, channels + size :], slab, channels, heads, spread[...]
    )
    cum_t = cum.T
    xt = xs * dt_w
    xt_s = split(xt)
    out_s = split(out_map)
    scores = dot3(out_s, split(in_map), dot_nt)
    held = state[...]
    base = grown_w * dot3(out_s, split(held)) + slab[6:7, :channels] * xs
    state[...] = held * grown_w[CHUNK - 1 : CHUNK, :] + dot3(
        split(in_map.T), split(xt * left_w)
    )
    causal = tri((CHUNK, CHUNK), lambda r, c: r >= c)
    first_half = lax.broadcasted_iota(jnp.int32, (CHUNK, LANES), 1) < LANES // 2
    zero = jnp.zeros((CHUNK, LANES), BF16)
    for pair in range(channels // LANES):
        cols = slice(pair * LANES, (pair + 1) * LANES)
        mats = []
        for h in (2 * pair, 2 * pair + 1):
            gap = cum[:, h : h + 1] - cum_t[h : h + 1, :]
            mats.append(scores * jnp.exp(jnp.where(causal, gap, NEG)))
        stacked = tuple(
            jnp.concatenate(
                [jnp.where(first_half, xp[:, cols], zero), jnp.where(first_half, zero, xp[:, cols])],
                axis=0,
            )
            for xp in xt_s
        )
        y[:, cols] = base[:, cols] + dot3(split(jnp.concatenate(mats, axis=1)), stacked)
    z = pre[:, :channels]
    gated = y[...] * (z * sigmoid(z))
    sq[...] = jnp.sum(gated * gated, axis=1, keepdims=True)
    u[...] = (gated * slab[5:6, :channels]).astype(BF16)

    @pl.when(step == pl.num_programs(0) - 1)
    def _():
        leaving[...] = state[...]


def backward_kernel(
    q,
    kappa,
    pre,
    before,
    tail,
    y,
    entering,
    grad_start,
    e_start,
    slab,
    spread,
    gather,
    gpre,
    grad_leaving,
    e_leaving,
    sums,
    grad,
    buffer,
    e_buffer,
    *,
    channels,
    heads,
):
    step = pl.program_id(0)
    steps = pl.num_programs(0)
    size = channels + 2 * LANES

    @pl.when(step == 0)
    def _():
        grad[...] = grad_start[...]
        e_buffer[CHUNK:, :] = e_start[...]
        sums[...] = jnp.zeros_like(sums)

    @pl.when(step > 0)
    def _():
        e_buffer[CHUNK:, :] = e_buffer[0:HALO, :]

    @pl.when(step == steps - 1)
    def _():
        buffer[0:HALO, :] = tail[...]

    @pl.when(step < steps - 1)
    def _():
        buffer[0:HALO, :] = before[:, channels : channels + size]

    buffer[HALO:, :] = pre[:, channels : channels + size]
    conv = conv_rows(buffer, slab)
    sig = sigmoid(conv)
    act = conv * sig
    d_act = sig * (1.0 + conv * (1.0 - sig))
    xs = act[:, :channels]
    in_map = act[:, channels : channels + LANES]
    out_map = act[:, channels + LANES :]
    arg, dt, decay, cum, dt_w, grown_w, left_w = step_terms(
        pre[:, channels + size :], slab, channels, heads, spread[...]
    )
    cum_t = cum.T

    z = pre[:, :channels]
    sig_z = sigmoid(z)
    silu_z = z * sig_z
    yv = y[...]
    gated = yv * silu_z
    qv = q[...]
    sums[5:6, :channels] += jnp.sum(qv * gated, axis=0, keepdims=True)
    g_gated = qv * slab[5:6, :channels] - gated * kappa[...]
    gpre[:, :channels] = (g_gated * yv * (sig_z * (1.0 + z * (1.0 - sig_z)))).astype(BF16)
    gy = g_gated * silu_z
    gy_b = gy.astype(BF16)
    sums[6:7, :channels] += jnp.sum(gy * xs, axis=0, keepdims=True)

    xt = xs * dt_w
    xt_b = xt.astype(BF16)
    in_b = in_map.astype(BF16)
    out_b = out_map.astype(BF16)
    held = entering[0]
    held_b = held.astype(BF16)
    g_state = grad[...]
    g_state_b = g_state.astype(BF16)
    grown_last = grown_w[CHUNK - 1 : CHUNK, :]

    from_state = grown_w * dot_nn(out_b, held_b)
    ge_b = (grown_w * gy).astype(BF16)
    g_out_map = dot_nt(ge_b, held_b)
    g_xt = left_w * dot_nn(in_b, g_state_b)
    g_in_map = dot_nt((xt * left_w).astype(BF16), g_state_b)
    through = jnp.sum(g_state * held, axis=0, keepdims=True) * grown_last
    grad[...] = g_state * grown_last + dot_nn(out_map.T.astype(BF16), ge_b)
    row_terms = gy * from_state
    col_terms = xt * g_xt

    scores_t = dot3(split(in_map), split(out_map), dot_nt)
    later = tri((CHUNK, CHUNK), lambda r, c: c >= r)
    first_half = lax.broadcasted_iota(jnp.int32, (CHUNK, LANES), 1) < LANES // 2
    lane = lax.broadcasted_iota(jnp.int32, (CHUNK, LANES), 1)
    zero = jnp.zeros((CHUNK, LANES), BF16)
    g_scores_t = jnp.zeros((CHUNK, CHUNK), F32)
    gap_rows = []
    gap_cols = jnp.zeros((CHUNK, LANES), F32)
    g_xt_parts = []
    for pair in range(channels // LANES):
        cols = slice(pair * LANES, (pair + 1) * LANES)
        gp = gy_b[:, cols]
        stacked = jnp.concatenate(
            [jnp.where(first_half, gp, zero), jnp.where(first_half, zero, gp)], axis=0
        )
        g_mats = dot_nt(xt_b[:, cols], stacked)
        mats = []
        for number in range(2):
            h = 2 * pair + number
            gap = cum_t[h : h + 1, :] - cum[:, h : h + 1]
            weight = jnp.exp(jnp.where(later, gap, NEG))
            mats.append((scores_t * weight).astype(BF16))
            g_score = g_mats[:, number * CHUNK : (number + 1) * CHUNK] * weight
            g_scores_t = g_scores_t + g_score
            g_gap = g_score * scores_t
            gap_rows.append(jnp.sum(g_gap, axis=0, keepdims=True))
            gap_cols = jnp.where(lane == h, jnp.sum(g_gap, axis=1, keepdims=True), gap_cols)
        g_xt_parts.append(g_xt[:, cols] + dot_nn(jnp.concatenate(mats, axis=1), stacked))
    g_xt = jnp.concatenate(g_xt_parts, axis=1)
    g_scores_b = g_scores_t.astype(BF16)
    g_in_map = g_in_map + dot_nn(g_scores_b, out_b)
    g_out_map = g_out_map + dot_nn(g_scores_t.T.astype(BF16), in_b)
    g_xs = slab[6:7, :channels] * gy + dt_w * g_xt

    pad = jnp.zeros((CHUNK - heads, CHUNK), F32)
    gap_rows_t = jnp.concatenate(gap_rows + [pad], axis=0).T
    packed = jnp.concatenate(
        [xs * g_xt, row_terms, col_terms, jnp.broadcast_to(through, (HALO, channels))], axis=0
    )
    high, rest = split(packed)
    grouped = dot_nn(high, gather[...]) + dot_nn(rest, gather[...])
    direct = grouped[:CHUNK]
    row_sum = grouped[CHUNK : 2 * CHUNK]
    col_sum = grouped[2 * CHUNK : 3 * CHUNK]
    through_sum = grouped[3 * CHUNK : 3 * CHUNK + 1]
    upper = tri((CHUNK, CHUNK), lambda r, c: c >= r).astype(F32)
    below = tri((CHUNK, CHUNK), lambda r, c: r > c).astype(F32)
    g_log = (
        dot_exact(upper, gap_rows_t - gap_cols + row_sum) + dot_exact(below, col_sum) + through_sum
    )
    g_dt = direct + g_log * decay
    g_dtin = jnp.where(lane < heads, g_dt * sigmoid(arg), 0.0)
    sums[5:6, channels : channels + LANES] += jnp.sum(g_dtin, axis=0, keepdims=True)
    sums[6:7, channels : channels + LANES] += decay * jnp.sum(dt * g_log, axis=0, keepdims=True)

    e = jnp.concatenate([g_xs, g_in_map, g_out_map], axis=1) * d_act
    e_buffer[0:CHUNK, :] = e
    sums[4:5, :] += jnp.sum(e, axis=0, keepdims=True)
    for k in range(CONV):
        first = HALO - (CONV - 1) + k
        sums[k : k + 1, :] += jnp.sum(e * buffer[first : first + CHUNK, :], axis=0, keepdims=True)
    g_pre = slab[CONV - 1 : CONV, :] * e
    for k in range(CONV - 1):
        first = CONV - 1 - k
        g_pre = g_pre + slab[k : k + 1, :] * e_buffer[first : first + CHUNK, :]
    gpre[:, channels : channels + size] = g_pre.astype(BF16)
    gpre[:, channels + size :] = g_dtin.astype(BF16)

    @pl.when(step == steps - 1)
    def _():
        grad_leaving[...] = grad[...]
        e_leaving[...] = e_buffer[0:HALO, :]


def fixed(shape):
    return pl.BlockSpec(shape, lambda i: (0,) * len(shape))


def mixer_forward(pre, tail, start, slab, spread, heads):
    rows, width = pre.shape
    state_size, channels = start.shape
    size = channels + 2 * LANES
    steps = rows // CHUNK
    by_row = lambda cols: pl.BlockSpec((CHUNK, cols), lambda i: (i, 0))
    shape = jax.ShapeDtypeStruct

    def body(*refs):
        forward_kernel(*refs, channels=channels, heads=heads)

    return pl.pallas_call(
        body,
        grid=(steps,),
        in_specs=[
            by_row(width),
            fixed((HALO, size)),
            fixed(start.shape),
            fixed(slab.shape),
            fixed(spread.shape),
        ],
        out_specs=[
            by_row(channels),
            by_row(1),
            by_row(channels),
            pl.BlockSpec((1, state_size, channels), lambda i: (i, 0, 0)),
            fixed(start.shape),
        ],
        out_shape=[
            shape((rows, channels), BF16),
            shape((rows, 1), F32),
            shape((rows, channels), F32),
            shape((steps, state_size, channels), F32),
            shape(start.shape, F32),
        ],
        scratch_shapes=[
            pltpu.VMEM((state_size, channels), F32),
            pltpu.VMEM((CHUNK + HALO, size), F32),
        ],
        compiler_params=pltpu.CompilerParams(
            dimension_semantics=("arbitrary",), vmem_limit_bytes=VMEM_LIMIT
        ),
        cost_estimate=pl.CostEstimate(
            flops=rows * channels * 2 * 600, bytes_accessed=rows * channels * 24, transcendentals=0
        ),
        name="mixer_forward",
    )(pre, tail, start, slab, spread)


def mixer_backward(q, kappa, pre, tail, y, entering, grad, e_rows, slab, spread, gather, heads):
    rows, width = pre.shape
    state_size, channels = grad.shape
    size = channels + 2 * LANES
    steps = rows // CHUNK
    by_row = lambda cols: pl.BlockSpec((CHUNK, cols), lambda i: (steps - 1 - i, 0))
    shape = jax.ShapeDtypeStruct
    groups = CHUNK // HALO

    def body(*refs):
        backward_kernel(*refs, channels=channels, heads=heads)

    return pl.pallas_call(
        body,
        grid=(steps,),
        in_specs=[
            by_row(channels),
            by_row(1),
            by_row(width),
            pl.BlockSpec(
                (HALO, width), lambda i: (jnp.maximum((steps - 1 - i) * groups - 1, 0), 0)
            ),
            fixed((HALO, size)),
            by_row(channels),
            pl.BlockSpec((1, state_size, channels), lambda i: (steps - 1 - i, 0, 0)),
            fixed(grad.shape),
            fixed(e_rows.shape),
            fixed(slab.shape),
            fixed(spread.shape),
            fixed(gather.shape),
        ],
        out_specs=[by_row(width), fixed(grad.shape), fixed(e_rows.shape), fixed(slab.shape)],
        out_shape=[
            shape((rows, width), BF16),
            shape(grad.shape, F32),
            shape(e_rows.shape, F32),
            shape(slab.shape, F32),
        ],
        scratch_shapes=[
            pltpu.VMEM((state_size, channels), F32),
            pltpu.VMEM((CHUNK + HALO, size), F32),
            pltpu.VMEM((CHUNK + HALO, size), F32),
        ],
        compiler_params=pltpu.CompilerParams(
            dimension_semantics=("arbitrary",), vmem_limit_bytes=VMEM_LIMIT
        ),
        cost_estimate=pl.CostEstimate(
            flops=rows * channels * 2 * 1800, bytes_accessed=rows * channels * 32, transcendentals=0
        ),
        name="mixer_backward",
    )(q, kappa, pre, pre, tail, y, entering, grad, e_rows, slab, spread, gather)


SWAP = [(0, 1), (1, 0)]


def swap_core(value):
    return lax.ppermute(value, "section", SWAP)


def swap_tp(value):
    return lax.ppermute(value, "tp", SWAP)


def by_index(index, own, other):
    first = index == 0
    return jnp.stack([jnp.where(first, own, other), jnp.where(first, other, own)])


def pick(pair, index):
    return lax.dynamic_index_in_dim(pair, index, 0, keepdims=False)


def gather_tokens(own, core, half):
    both = by_index(half, own, swap_tp(own))
    whole = by_index(core, both, swap_core(both))
    whole = jnp.moveaxis(whole, 0, 1)
    return whole.reshape((4 * own.shape[0],) + own.shape[1:])


def scatter_tokens(part, core, half):
    rows = part.shape[0] // 4
    split = part.reshape((2, 2, rows) + part.shape[1:])
    mine = lax.dynamic_index_in_dim(split, core, 1, keepdims=False)
    theirs = lax.dynamic_index_in_dim(split, 1 - core, 1, keepdims=False)
    total = mine + swap_core(theirs)
    sent = pick(total, 1 - half)
    if part.ndim > 1:
        sent = sent.astype(BF16)
    return pick(total, half) + swap_tp(sent).astype(F32)


def local(
    inputs,
    cotangent,
    norm_gain,
    w_zx,
    w_bc,
    w_dt,
    conv_x,
    conv_xb,
    conv_bc,
    conv_bcb,
    dt_bias,
    a_log,
    d_skip,
    gate_gain,
    w_out,
):
    cores = lax.axis_size("section")
    core = lax.axis_index("section")
    half = lax.axis_index("tp")
    micros = inputs.shape[1]
    rows = inputs.shape[2] // cores
    channels = w_zx.shape[3] // cores
    heads = w_dt.shape[2] // cores
    width = channels // heads
    shared = w_bc.shape[2]
    depth = w_zx.shape[1]
    in_width = 2 * channels + shared + LANES
    gain_pair = by_index(core, norm_gain[0], swap_core(norm_gain[0]))
    gains = lax.all_gather(gain_pair, "fsdp", axis=1, tiled=True).astype(F32)

    def cut(tensor, index, size):
        return lax.dynamic_slice_in_dim(tensor, index * size, size, tensor.ndim - 1)

    def weight_shard(index):
        zx = cut(w_zx[0], index, channels).reshape(depth, 2 * channels)
        steps = jnp.pad(cut(w_dt[0], index, heads), ((0, 0), (0, LANES - heads)))
        return jnp.concatenate([zx, w_bc[0], steps, cut(w_out[0], index, channels)], axis=1)

    def slab_of(index):
        pad = jnp.zeros((LANES - heads,), F32)
        steps = jnp.concatenate([cut(dt_bias[0], index, heads), pad])
        decay = jnp.concatenate([-jnp.exp(cut(a_log[0], index, heads)), pad])
        skip = jnp.repeat(cut(d_skip[0], index, heads), width)
        rest = jnp.zeros((shared - LANES,), F32)
        taps = jnp.concatenate([cut(conv_x[0], index, channels), conv_bc[0]], axis=1)
        bias = jnp.concatenate([cut(conv_xb[0], index, channels), conv_bcb[0]])
        return jnp.concatenate(
            [
                taps,
                bias[None],
                jnp.concatenate([cut(gate_gain[0], index, channels), steps, rest])[None],
                jnp.concatenate([skip, decay, rest])[None],
                jnp.zeros((1, channels + shared), F32),
            ]
        )

    own_shard = weight_shard(core)
    got_shard = swap_core(weight_shard(1 - core))
    own_slab = slab_of(core)
    got_slab = swap_core(slab_of(1 - core))
    projections, slabs = [], []
    for layer in range(2):
        shard = jnp.where(core == layer, own_shard, got_shard)
        projections.append(
            (
                lax.all_gather(shard[:, :in_width], "fsdp", axis=0, tiled=True),
                lax.all_gather(shard[:, in_width:], "fsdp", axis=0, tiled=True),
            )
        )
        slabs.append(jnp.where(core == layer, own_slab, got_slab))

    lane = jnp.arange(LANES)
    head_of = jnp.arange(channels) // width
    spread = ((lane[:, None] % heads == head_of[None, :]) & (lane[:, None] < 2 * heads)).astype(BF16)
    gather = (head_of[:, None] == lane[None, :]).astype(BF16)

    def own_rows(tensor):
        return [
            lax.dynamic_slice_in_dim(tensor[0, m], core * rows, rows, 0).astype(F32)
            for m in range(micros)
        ]

    hidden = own_rows(inputs)
    size = channels + shared
    saved = []
    for layer in range(2):
        w_in, w_back = projections[layer]
        slab = slabs[layer]
        state = jnp.zeros((shared // 2, channels), F32)
        tail = jnp.zeros((HALO, size), F32)
        kept = []
        next_hidden = []
        for m in range(micros):
            h = hidden[m]
            scale = lax.rsqrt(jnp.mean(h * h, axis=1, keepdims=True) + EPS)
            normed = gather_tokens((h * scale * gains[layer][None]).astype(BF16), core, half)
            pre = dot_nn(normed, w_in)
            u, squares, y, entering, state = mixer_forward(pre, tail, state, slab, spread, heads)
            part = dot_nt(u, w_back)
            total = scatter_tokens(part, core, half)
            squares = scatter_tokens(squares[:, 0], core, half)
            r = lax.rsqrt(squares / DI + EPS)[:, None]
            branch = r * total
            next_hidden.append(h + branch)
            kept.append((h, scale, normed, pre, tail, y, u, entering, r, branch))
            tail = pre[-HALO:, channels : channels + size]
        saved.append(kept)
        hidden = next_hidden

    grads = own_rows(cotangent)
    reduced = [None, None]
    small = [None, None]
    for layer in (1, 0):
        w_in, w_back = projections[layer]
        slab = slabs[layer]
        state = jnp.zeros((shared // 2, channels), F32)
        e_rows = jnp.zeros((HALO, size), F32)
        next_grads = [None] * micros
        gpres = [None] * micros
        backs = [None] * micros
        totals = jnp.zeros(slab.shape, F32)
        gain_total = jnp.zeros((w_out.shape[1] * lax.axis_size("fsdp"),), F32)
        for m in reversed(range(micros)):
            h, scale, normed, pre, tail, y, u, entering, r, branch = saved[layer][m]
            g = grads[m]
            kappa = r * r * jnp.sum(g * branch, axis=1, keepdims=True) / DI
            back = gather_tokens((g * r).astype(BF16), core, half)
            kappa = gather_tokens(kappa[:, 0], core, half)[:, None]
            q = dot_nn(back, w_back)
            gpre, state, e_rows, sums = mixer_backward(
                q, kappa, pre, tail, y, entering, state, e_rows, slab, spread, gather, heads
            )
            g_norm = scatter_tokens(dot_nt(gpre, w_in), core, half)
            gain_total = gain_total + jnp.sum(g_norm * (h * scale), axis=0)
            g_norm = g_norm * gains[layer][None]
            mean = jnp.mean(g_norm * h, axis=1, keepdims=True)
            next_grads[m] = g + scale * g_norm - h * (scale * scale * scale) * mean
            gpres[m] = gpre
            backs[m] = back
            totals = totals + sums
        grads = next_grads
        normed_all = jnp.concatenate([saved[layer][m][2] for m in range(micros)])
        u_all = jnp.concatenate([saved[layer][m][6] for m in range(micros)])
        over_tokens = (((0,), (0,)), ((), ()))
        grad_back = lax.dot_general(
            jnp.concatenate(backs), u_all, over_tokens, preferred_element_type=F32
        ).astype(BF16)
        grad_in = lax.dot_general(
            normed_all, jnp.concatenate(gpres), over_tokens, preferred_element_type=F32
        ).astype(BF16)
        reduced[layer] = (
            lax.psum_scatter(grad_in, "fsdp", scatter_dimension=0, tiled=True),
            lax.psum_scatter(grad_back, "fsdp", scatter_dimension=0, tiled=True),
        )
        small[layer] = jnp.concatenate([totals.reshape(-1), gain_total])

    small_sums = jnp.stack(small)
    devices = lax.axis_size("fsdp")
    if devices & (devices - 1) == 0:
        bit = 1
        while bit < devices:
            small_sums = small_sums + lax.ppermute(
                small_sums, "fsdp", [(i, i ^ bit) for i in range(devices)]
            )
            bit *= 2
    else:
        small_sums = lax.psum(small_sums, "fsdp")
    own = pick(small_sums, core)
    got = swap_core(pick(small_sums, 1 - core))
    count = slabs[0].size
    halves = by_index(core, own[:count], got[:count]).reshape((2,) + slabs[0].shape)
    both = own + got
    common = jnp.concatenate(
        [both[:count].reshape(slabs[0].shape)[:5, channels:].reshape(-1), both[count:]]
    )
    common = common + swap_tp(common)
    conv_sum = common[: 5 * shared].reshape(5, shared)
    gain_sum = lax.dynamic_slice_in_dim(
        common[5 * shared :], lax.axis_index("fsdp") * depth, depth, 0
    )
    wide = jnp.concatenate([halves[0, :7, :channels], halves[1, :7, :channels]], axis=1)
    narrow = jnp.concatenate(
        [halves[j, 5:7, channels : channels + heads] for j in range(2)], axis=1
    )
    skip_sum = wide[6].reshape(2 * heads, width).sum(axis=1)

    mine = [jnp.where(core == 0, reduced[0][i], reduced[1][i]) for i in range(2)]
    theirs = [jnp.where(core == 0, reduced[1][i], reduced[0][i]) for i in range(2)]
    got = [swap_core(v) for v in theirs]
    in_pair = by_index(core, mine[0], got[0]).astype(F32)
    back_pair = by_index(core, mine[1], got[1]).astype(F32)
    g_zx = jnp.concatenate(
        [in_pair[j, :, : 2 * channels].reshape(depth, 2, channels) for j in range(2)], axis=2
    )
    g_bc = in_pair[:, :, 2 * channels : 2 * channels + shared].sum(axis=0)
    g_dt = jnp.concatenate(
        [in_pair[j, :, 2 * channels + shared : 2 * channels + shared + heads] for j in range(2)],
        axis=1,
    )
    g_back = jnp.concatenate([back_pair[0], back_pair[1]], axis=1)
    g_bc = g_bc + swap_tp(g_bc)

    def placed_rows(parts):
        own = jnp.where(core == 0, parts[0], parts[1])
        other = jnp.where(core == 0, parts[1], parts[0])
        return by_index(core, own, swap_core(other)).reshape(1, 1, 2 * rows, -1)

    return (
        placed_rows(hidden),
        placed_rows(grads),
        gain_sum[None],
        g_zx[None],
        g_bc[None],
        g_dt[None],
        wide[:4][None],
        wide[4][None],
        conv_sum[:4][None],
        conv_sum[4][None],
        narrow[0][None],
        narrow[1][None],
        skip_sum[None],
        wide[5][None],
        g_back[None],
    )


def solution(mesh):
    placed = (
        P("fsdp", None, "tp", None),
        P("fsdp", None, "tp", None),
        P("section", "fsdp"),
        P("section", "fsdp", None, "tp"),
        P("section", "fsdp", None),
        P("section", "fsdp", "tp"),
        P("section", None, "tp"),
        P("section", "tp"),
        P("section", None, None),
        P("section", None),
        P("section", "tp"),
        P("section", "tp"),
        P("section", "tp"),
        P("section", "tp"),
        P("section", "fsdp", "tp"),
    )
    return jax.shard_map(
        local,
        mesh=mesh,
        in_specs=placed,
        out_specs=(
            P("fsdp", "section", "tp", None),
            P("fsdp", "section", "tp", None),
        )
        + placed[2:],
        check_vma=False,
    )
```

```python
import functools

import jax
import jax.numpy as jnp
from jax import lax
from jax.experimental import pallas as pl
from jax.experimental.pallas import tpu as pltpu
from jax.sharding import PartitionSpec as P

CONV = 4
DI = 4096
EPS = 1e-05
CHUNK = 128
LANES = 128
HALO = 8
NEG = -10000.0
HIGHEST = lax.Precision.HIGHEST
F32 = jnp.float32
BF16 = jnp.bfloat16
VMEM_LIMIT = 56 * 1024 * 1024


def sigmoid(v):
    return 0.5 * jnp.tanh(0.5 * v) + 0.5


def dot_nn(a, b):
    return lax.dot_general(a, b, (((1,), (0,)), ((), ())), preferred_element_type=F32)


def dot_nt(a, b):
    return lax.dot_general(a, b, (((1,), (1,)), ((), ())), preferred_element_type=F32)


def dot_exact(a, b):
    return lax.dot_general(
        a, b, (((1,), (0,)), ((), ())), preferred_element_type=F32, precision=HIGHEST
    )


def split(a):
    high = a.astype(BF16)
    return high, (a - high.astype(F32)).astype(BF16)


def dot3(a, b, dot=dot_nn):
    return dot(a[0], b[0]) + (dot(a[1], b[0]) + dot(a[0], b[1]))


def tri(shape, keep):
    rows = lax.broadcasted_iota(jnp.int32, shape, 0)
    cols = lax.broadcasted_iota(jnp.int32, shape, 1)
    return keep(rows, cols)


def expand(columns, spread, heads):
    high = columns.astype(BF16).astype(F32)
    rest = columns - high
    packed = high + pltpu.roll(rest, heads, 1)
    return dot_nn(packed.astype(BF16), spread)


def step_terms(pre_dt, slab, channels, heads, spread):
    lane = lax.broadcasted_iota(jnp.int32, pre_dt.shape, 1)
    live = lane < heads
    arg = pre_dt + slab[5:6, channels : channels + LANES]
    dt = jnp.where(live, jnp.maximum(arg, 0.0) + jnp.log1p(jnp.exp(-jnp.abs(arg))), 0.0)
    decay = slab[6:7, channels : channels + LANES]
    lower = tri((CHUNK, CHUNK), lambda r, c: r >= c).astype(F32)
    cum = dot_exact(lower, dt * decay)
    last = cum[CHUNK - 1 : CHUNK, :]
    grown = jnp.where(live, jnp.exp(cum), 0.0)
    left = jnp.where(live, jnp.exp(last - cum), 0.0)
    wide = expand(jnp.concatenate([dt, grown, left], axis=0), spread, heads)
    return arg, dt, decay, cum, wide[:CHUNK], wide[CHUNK : 2 * CHUNK], wide[2 * CHUNK :]


def conv_rows(buffer, slab):
    out = slab[4:5, :] + slab[CONV - 1 : CONV, :] * buffer[HALO : HALO + CHUNK, :]
    for k in range(CONV - 1):
        first = HALO - (CONV - 1) + k
        out = out + slab[k : k + 1, :] * buffer[first : first + CHUNK, :]
    return out


def forward_kernel(
    pre, tail, start, slab, spread, u, sq, y, entering, leaving, state, buffer, *, channels, heads
):
    step = pl.program_id(0)
    size = channels + 2 * LANES

    @pl.when(step == 0)
    def _():
        state[...] = start[...]
        buffer[0:HALO, :] = tail[...]

    @pl.when(step > 0)
    def _():
        buffer[0:HALO, :] = buffer[CHUNK : CHUNK + HALO, :]

    buffer[HALO:, :] = pre[:, channels : channels + size]
    entering[0] = state[...]
    conv = conv_rows(buffer, slab)
    act = conv * sigmoid(conv)
    xs = act[:, :channels]
    in_map = act[:, channels : channels + LANES]
    out_map = act[:, channels + LANES :]
    arg, dt, decay, cum, dt_w, grown_w, left_w = step_terms(
        pre[:, channels + size :], slab, channels, heads, spread[...]
    )
    cum_t = cum.T
    xt = xs * dt_w
    xt_s = split(xt)
    out_s = split(out_map)
    scores = dot3(out_s, split(in_map), dot_nt)
    held = state[...]
    base = grown_w * dot3(out_s, split(held)) + slab[6:7, :channels] * xs
    state[...] = held * grown_w[CHUNK - 1 : CHUNK, :] + dot3(
        split(in_map.T), split(xt * left_w)
    )
    causal = tri((CHUNK, CHUNK), lambda r, c: r >= c)
    first_half = lax.broadcasted_iota(jnp.int32, (CHUNK, LANES), 1) < LANES // 2
    zero = jnp.zeros((CHUNK, LANES), BF16)
    for pair in range(channels // LANES):
        cols = slice(pair * LANES, (pair + 1) * LANES)
        mats = []
        for h in (2 * pair, 2 * pair + 1):
            gap = cum[:, h : h + 1] - cum_t[h : h + 1, :]
            mats.append(scores * jnp.exp(jnp.where(causal, gap, NEG)))
        stacked = tuple(
            jnp.concatenate(
                [jnp.where(first_half, xp[:, cols], zero), jnp.where(first_half, zero, xp[:, cols])],
                axis=0,
            )
            for xp in xt_s
        )
        y[:, cols] = base[:, cols] + dot3(split(jnp.concatenate(mats, axis=1)), stacked)
    z = pre[:, :channels]
    gated = y[...] * (z * sigmoid(z))
    sq[...] = jnp.sum(gated * gated, axis=1, keepdims=True)
    u[...] = (gated * slab[5:6, :channels]).astype(BF16)

    @pl.when(step == pl.num_programs(0) - 1)
    def _():
        leaving[...] = state[...]


def backward_kernel(
    q,
    kappa,
    pre,
    before,
    tail,
    y,
    entering,
    grad_start,
    e_start,
    slab,
    spread,
    gather,
    gpre,
    grad_leaving,
    e_leaving,
    sums,
    grad,
    buffer,
    e_buffer,
    *,
    channels,
    heads,
):
    step = pl.program_id(0)
    steps = pl.num_programs(0)
    size = channels + 2 * LANES

    @pl.when(step == 0)
    def _():
        grad[...] = grad_start[...]
        e_buffer[CHUNK:, :] = e_start[...]
        sums[...] = jnp.zeros_like(sums)

    @pl.when(step > 0)
    def _():
        e_buffer[CHUNK:, :] = e_buffer[0:HALO, :]

    @pl.when(step == steps - 1)
    def _():
        buffer[0:HALO, :] = tail[...]

    @pl.when(step < steps - 1)
    def _():
        buffer[0:HALO, :] = before[:, channels : channels + size]

    buffer[HALO:, :] = pre[:, channels : channels + size]
    conv = conv_rows(buffer, slab)
    sig = sigmoid(conv)
    act = conv * sig
    d_act = sig * (1.0 + conv * (1.0 - sig))
    xs = act[:, :channels]
    in_map = act[:, channels : channels + LANES]
    out_map = act[:, channels + LANES :]
    arg, dt, decay, cum, dt_w, grown_w, left_w = step_terms(
        pre[:, channels + size :], slab, channels, heads, spread[...]
    )
    cum_t = cum.T

    z = pre[:, :channels]
    sig_z = sigmoid(z)
    silu_z = z * sig_z
    yv = y[...]
    gated = yv * silu_z
    qv = q[...]
    sums[5:6, :channels] += jnp.sum(qv * gated, axis=0, keepdims=True)
    g_gated = qv * slab[5:6, :channels] - gated * kappa[...]
    gpre[:, :channels] = (g_gated * yv * (sig_z * (1.0 + z * (1.0 - sig_z)))).astype(BF16)
    gy = g_gated * silu_z
    gy_b = gy.astype(BF16)
    sums[6:7, :channels] += jnp.sum(gy * xs, axis=0, keepdims=True)

    xt = xs * dt_w
    xt_b = xt.astype(BF16)
    in_b = in_map.astype(BF16)
    out_b = out_map.astype(BF16)
    held = entering[0]
    held_b = held.astype(BF16)
    g_state = grad[...]
    g_state_b = g_state.astype(BF16)
    grown_last = grown_w[CHUNK - 1 : CHUNK, :]

    from_state = grown_w * dot_nn(out_b, held_b)
    ge_b = (grown_w * gy).astype(BF16)
    g_out_map = dot_nt(ge_b, held_b)
    g_xt = left_w * dot_nn(in_b, g_state_b)
    g_in_map = dot_nt((xt * left_w).astype(BF16), g_state_b)
    through = jnp.sum(g_state * held, axis=0, keepdims=True) * grown_last
    grad[...] = g_state * grown_last + dot_nn(out_map.T.astype(BF16), ge_b)
    row_terms = gy * from_state
    col_terms = xt * g_xt

    scores_t = dot3(split(in_map), split(out_map), dot_nt)
    later = tri((CHUNK, CHUNK), lambda r, c: c >= r)
    first_half = lax.broadcasted_iota(jnp.int32, (CHUNK, LANES), 1) < LANES // 2
    lane = lax.broadcasted_iota(jnp.int32, (CHUNK, LANES), 1)
    zero = jnp.zeros((CHUNK, LANES), BF16)
    g_scores_t = jnp.zeros((CHUNK, CHUNK), F32)
    gap_rows = []
    gap_cols = jnp.zeros((CHUNK, LANES), F32)
    g_xt_parts = []
    for pair in range(channels // LANES):
        cols = slice(pair * LANES, (pair + 1) * LANES)
        gp = gy_b[:, cols]
        stacked = jnp.concatenate(
            [jnp.where(first_half, gp, zero), jnp.where(first_half, zero, gp)], axis=0
        )
        g_mats = dot_nt(xt_b[:, cols], stacked)
        mats = []
        for number in range(2):
            h = 2 * pair + number
            gap = cum_t[h : h + 1, :] - cum[:, h : h + 1]
            weight = jnp.exp(jnp.where(later, gap, NEG))
            mats.append((scores_t * weight).astype(BF16))
            g_score = g_mats[:, number * CHUNK : (number + 1) * CHUNK] * weight
            g_scores_t = g_scores_t + g_score
            g_gap = g_score * scores_t
            gap_rows.append(jnp.sum(g_gap, axis=0, keepdims=True))
            gap_cols = jnp.where(lane == h, jnp.sum(g_gap, axis=1, keepdims=True), gap_cols)
        g_xt_parts.append(g_xt[:, cols] + dot_nn(jnp.concatenate(mats, axis=1), stacked))
    g_xt = jnp.concatenate(g_xt_parts, axis=1)
    g_scores_b = g_scores_t.astype(BF16)
    g_in_map = g_in_map + dot_nn(g_scores_b, out_b)
    g_out_map = g_out_map + dot_nn(g_scores_t.T.astype(BF16), in_b)
    g_xs = slab[6:7, :channels] * gy + dt_w * g_xt

    pad = jnp.zeros((CHUNK - heads, CHUNK), F32)
    gap_rows_t = jnp.concatenate(gap_rows + [pad], axis=0).T
    packed = jnp.concatenate(
        [xs * g_xt, row_terms, col_terms, jnp.broadcast_to(through, (HALO, channels))], axis=0
    )
    high, rest = split(packed)
    grouped = dot_nn(high, gather[...]) + dot_nn(rest, gather[...])
    direct = grouped[:CHUNK]
    row_sum = grouped[CHUNK : 2 * CHUNK]
    col_sum = grouped[2 * CHUNK : 3 * CHUNK]
    through_sum = grouped[3 * CHUNK : 3 * CHUNK + 1]
    upper = tri((CHUNK, CHUNK), lambda r, c: c >= r).astype(F32)
    below = tri((CHUNK, CHUNK), lambda r, c: r > c).astype(F32)
    g_log = (
        dot_exact(upper, gap_rows_t - gap_cols + row_sum) + dot_exact(below, col_sum) + through_sum
    )
    g_dt = direct + g_log * decay
    g_dtin = jnp.where(lane < heads, g_dt * sigmoid(arg), 0.0)
    sums[5:6, channels : channels + LANES] += jnp.sum(g_dtin, axis=0, keepdims=True)
    sums[6:7, channels : channels + LANES] += decay * jnp.sum(dt * g_log, axis=0, keepdims=True)

    e = jnp.concatenate([g_xs, g_in_map, g_out_map], axis=1) * d_act
    e_buffer[0:CHUNK, :] = e
    sums[4:5, :] += jnp.sum(e, axis=0, keepdims=True)
    for k in range(CONV):
        first = HALO - (CONV - 1) + k
        sums[k : k + 1, :] += jnp.sum(e * buffer[first : first + CHUNK, :], axis=0, keepdims=True)
    g_pre = slab[CONV - 1 : CONV, :] * e
    for k in range(CONV - 1):
        first = CONV - 1 - k
        g_pre = g_pre + slab[k : k + 1, :] * e_buffer[first : first + CHUNK, :]
    gpre[:, channels : channels + size] = g_pre.astype(BF16)
    gpre[:, channels + size :] = g_dtin.astype(BF16)

    @pl.when(step == steps - 1)
    def _():
        grad_leaving[...] = grad[...]
        e_leaving[...] = e_buffer[0:HALO, :]


def fixed(shape):
    return pl.BlockSpec(shape, lambda i: (0,) * len(shape))


def mixer_forward(pre, tail, start, slab, spread, heads):
    rows, width = pre.shape
    state_size, channels = start.shape
    size = channels + 2 * LANES
    steps = rows // CHUNK
    by_row = lambda cols: pl.BlockSpec((CHUNK, cols), lambda i: (i, 0))
    shape = jax.ShapeDtypeStruct

    def body(*refs):
        forward_kernel(*refs, channels=channels, heads=heads)

    return pl.pallas_call(
        body,
        grid=(steps,),
        in_specs=[
            by_row(width),
            fixed((HALO, size)),
            fixed(start.shape),
            fixed(slab.shape),
            fixed(spread.shape),
        ],
        out_specs=[
            by_row(channels),
            by_row(1),
            by_row(channels),
            pl.BlockSpec((1, state_size, channels), lambda i: (i, 0, 0)),
            fixed(start.shape),
        ],
        out_shape=[
            shape((rows, channels), BF16),
            shape((rows, 1), F32),
            shape((rows, channels), F32),
            shape((steps, state_size, channels), F32),
            shape(start.shape, F32),
        ],
        scratch_shapes=[
            pltpu.VMEM((state_size, channels), F32),
            pltpu.VMEM((CHUNK + HALO, size), F32),
        ],
        compiler_params=pltpu.CompilerParams(
            dimension_semantics=("arbitrary",), vmem_limit_bytes=VMEM_LIMIT
        ),
        cost_estimate=pl.CostEstimate(flops=1000, bytes_accessed=1000, transcendentals=0),
        name="mixer_forward",
    )(pre, tail, start, slab, spread)


def mixer_backward(q, kappa, pre, tail, y, entering, grad, e_rows, slab, spread, gather, heads):
    rows, width = pre.shape
    state_size, channels = grad.shape
    size = channels + 2 * LANES
    steps = rows // CHUNK
    by_row = lambda cols: pl.BlockSpec((CHUNK, cols), lambda i: (steps - 1 - i, 0))
    shape = jax.ShapeDtypeStruct
    groups = CHUNK // HALO

    def body(*refs):
        backward_kernel(*refs, channels=channels, heads=heads)

    return pl.pallas_call(
        body,
        grid=(steps,),
        in_specs=[
            by_row(channels),
            by_row(1),
            by_row(width),
            pl.BlockSpec(
                (HALO, width), lambda i: (jnp.maximum((steps - 1 - i) * groups - 1, 0), 0)
            ),
            fixed((HALO, size)),
            by_row(channels),
            pl.BlockSpec((1, state_size, channels), lambda i: (steps - 1 - i, 0, 0)),
            fixed(grad.shape),
            fixed(e_rows.shape),
            fixed(slab.shape),
            fixed(spread.shape),
            fixed(gather.shape),
        ],
        out_specs=[by_row(width), fixed(grad.shape), fixed(e_rows.shape), fixed(slab.shape)],
        out_shape=[
            shape((rows, width), BF16),
            shape(grad.shape, F32),
            shape(e_rows.shape, F32),
            shape(slab.shape, F32),
        ],
        scratch_shapes=[
            pltpu.VMEM((state_size, channels), F32),
            pltpu.VMEM((CHUNK + HALO, size), F32),
            pltpu.VMEM((CHUNK + HALO, size), F32),
        ],
        compiler_params=pltpu.CompilerParams(
            dimension_semantics=("arbitrary",), vmem_limit_bytes=VMEM_LIMIT
        ),
        cost_estimate=pl.CostEstimate(flops=1000, bytes_accessed=1000, transcendentals=0),
        name="mixer_backward",
    )(q, kappa, pre, pre, tail, y, entering, grad, e_rows, slab, spread, gather)


MESH = pl.DeviceIdType.MESH
DEEP = 4


def place_in_line():
    core, line, half = lax.axis_index("section"), lax.axis_index("fsdp"), lax.axis_index("tp")
    deep, side = line // 2, line % 2

    def device(z, x):
        return (core, z * 2 + x, half)

    return deep, side, device


def greet_all():
    core, line, half = lax.axis_index("section"), lax.axis_index("fsdp"), lax.axis_index("tp")
    barrier = pltpu.get_barrier_semaphore()

    def greet(target):
        pl.semaphore_signal(barrier, inc=1, device_id=target, device_id_type=MESH)

    greet((core, line, 1 - half))
    greet((1 - core, line, half))
    for step in range(1, 2 * DEEP):
        greet((core, (line + step) % (2 * DEEP), half))
    pl.semaphore_wait(barrier, 2 * DEEP + 1)


def start_kernel(*refs, count, micros):
    shards, (gain, own) = refs[:count], refs[count : count + 2]
    outs = refs[count + 2 :]
    wholes, (gains, normed) = outs[:count], outs[count : count + 2]
    scratch = outs[count + 2 :]
    local_sem, x_send, x_recv, up_send, up_recv, down_send, down_recv = scratch[:7]
    gain_send, gain_recv, own_sem, y_send, y_recv, core_send, core_recv, rows_out = scratch[7:]
    deep, side, device = place_in_line()
    core, line, half = lax.axis_index("section"), lax.axis_index("fsdp"), lax.axis_index("tp")
    lines = 2 * DEEP

    greet_all()
    across_tp, across_core = (core, line, 1 - half), (1 - core, line, half)

    def send_gain(step):
        return pltpu.make_async_remote_copy(
            src_ref=gain,
            dst_ref=gains.at[line],
            send_sem=gain_send.at[step],
            recv_sem=gain_recv.at[step],
            device_id=(core, (line + step) % lines, half),
            device_id_type=MESH,
        )

    for step in range(1, lines):
        send_gain(step).start()

    def rows(i, z, x):
        size = shards[i].shape[0]
        return wholes[i].at[pl.ds((z * 2 + x) * size, size)]

    def move(i, z, source, send, recv, target):
        return pltpu.make_async_remote_copy(
            src_ref=rows(i, z, side) if source is None else source,
            dst_ref=rows(i, z, side),
            send_sem=send,
            recv_sem=recv,
            device_id=target,
            device_id_type=MESH,
        )

    def across(i, z, source=None):
        return move(i, z, source, x_send.at[i, z], x_recv.at[i, z], device(deep, 1 - side))

    def upward(i, k, source=None):
        above = jnp.minimum(deep + 1, DEEP - 1)
        return move(i, deep - k, source, up_send.at[i, k], up_recv.at[i, k], device(above, side))

    def downward(i, k, source=None):
        below = jnp.maximum(deep - 1, 0)
        return move(i, deep + k, source, down_send.at[i, k], down_recv.at[i, k], device(below, side))

    has_above, has_below = deep < DEEP - 1, deep > 0
    for i in range(count):
        pltpu.make_async_copy(shards[i], rows(i, deep, side), local_sem.at[i]).start()

        @pl.when(has_above)
        def _(i=i):
            upward(i, 0, shards[i]).start()

        @pl.when(has_below)
        def _(i=i):
            downward(i, 0, shards[i]).start()

        across(i, deep, shards[i]).start()

    gains[line] = gain[...]
    for step in range(1, lines):
        send_gain(step).wait()
    gain_row = jnp.concatenate(
        [gains[f, j : j + 1, :] for f in range(lines) for j in range(gain.shape[0] // 4)], axis=1
    )
    tokens = own.shape[0] // micros
    h = own[...].astype(F32)
    scale = lax.rsqrt(jnp.mean(h * h, axis=1, keepdims=True) + EPS)
    rows_out[...] = (h * scale * gain_row).astype(BF16)

    def token_copies(m):
        source = rows_out.at[pl.ds(m * tokens, tokens)]
        place = normed.at[m, half, core]
        later = normed.at[m, 1 - half, core]
        remote = functools.partial(pltpu.make_async_remote_copy, device_id_type=MESH)
        return (
            pltpu.make_async_copy(source, place, own_sem.at[m]),
            remote(source, place, y_send.at[m], y_recv.at[m], device_id=across_tp),
            remote(source, place, core_send.at[m], core_recv.at[m], device_id=across_core),
            remote(later, later, core_send.at[micros + m], core_recv.at[micros + m], device_id=across_core),
        )

    for m in range(micros):
        for copy in token_copies(m)[:3]:
            copy.start()
    for m in range(micros):
        token_copies(m)[1].wait_recv()
        token_copies(m)[3].start()

    for k in range(1, DEEP):
        for i in range(count):

            @pl.when(deep >= k)
            def _(i=i, k=k):
                arrived = move(
                    i, deep - k, None, up_send.at[i, k - 1], up_recv.at[i, k - 1], device(deep, side)
                )
                arrived.wait_recv()

                @pl.when(has_above)
                def _():
                    upward(i, k).start()

                across(i, deep - k).start()

            @pl.when(deep + k <= DEEP - 1)
            def _(i=i, k=k):
                arrived = move(
                    i, deep + k, None, down_send.at[i, k - 1], down_recv.at[i, k - 1], device(deep, side)
                )
                arrived.wait_recv()

                @pl.when(has_below)
                def _():
                    downward(i, k).start()

                across(i, deep + k).start()

    for i in range(count):
        pltpu.make_async_copy(shards[i], rows(i, deep, side), local_sem.at[i]).wait()
        for z in range(DEEP):
            other = pltpu.make_async_remote_copy(
                src_ref=rows(i, z, side),
                dst_ref=rows(i, z, 1 - side),
                send_sem=x_send.at[i, z],
                recv_sem=x_recv.at[i, z],
                device_id=device(deep, 1 - side),
                device_id_type=MESH,
            )
            other.wait_send()
            other.wait_recv()
        for k in range(DEEP - 1):

            @pl.when(has_above & (deep >= k))
            def _(i=i, k=k):
                upward(i, k).wait_send()

            @pl.when(has_below & (deep + k <= DEEP - 1))
            def _(i=i, k=k):
                downward(i, k).wait_send()

    for m in range(micros):
        own_copy, y_copy, core_copy, core_later = token_copies(m)
        own_copy.wait()
        y_copy.wait_send()
        core_copy.wait()
        core_later.wait()


def start_gather(shards, gain, own, micros):
    count = len(shards)
    lines = 2 * DEEP
    pairs = pltpu.SemaphoreType.DMA((count, DEEP))
    dma = lambda n: pltpu.SemaphoreType.DMA((n,))
    shape = jax.ShapeDtypeStruct
    anywhere = pl.BlockSpec(memory_space=pl.ANY)
    vmem = pl.BlockSpec(memory_space=pltpu.VMEM)
    rows, width = own.shape
    sizes = sum(v.size for v in shards)
    return pl.pallas_call(
        functools.partial(start_kernel, count=count, micros=micros),
        out_shape=[shape((v.shape[0] * lines, v.shape[1]), v.dtype) for v in shards]
        + [
            shape((lines,) + gain.shape, F32),
            shape((micros, 2, 2, rows // micros, width), BF16),
        ],
        in_specs=[anywhere] * count + [vmem] * 2,
        out_specs=[anywhere] * count + [vmem, anywhere],
        scratch_shapes=[dma(count)]
        + [pairs] * 6
        + [dma(lines)] * 2
        + [dma(micros)] * 3
        + [dma(2 * micros)] * 2
        + [pltpu.VMEM(own.shape, BF16)],
        compiler_params=pltpu.CompilerParams(
            collective_id=1, has_side_effects=True, vmem_limit_bytes=VMEM_LIMIT
        ),
        cost_estimate=pl.CostEstimate(flops=1000, bytes_accessed=1000, transcendentals=0),
        name="start_gather",
    )(*shards, gain, own)


def add_rows(out, *parts):
    rows = out.shape[0]
    step = 32

    def body(n, _):
        at = pl.ds(pl.multiple_of(n * step, step), step)
        total = parts[0][at].astype(F32)
        for part in parts[1:]:
            total = total + part[at].astype(F32)
        out[at] = total.astype(out.dtype)
        return 0

    lax.fori_loop(0, rows // step, body, 0)


X_ORDER = ((3, 2, 1, 0), (3, 0, 2, 1), (0, 3, 1, 2), (0, 1, 2, 3))


def reduce_kernel(*refs, count):
    parts, small, results = refs[:count], refs[count], refs[count + 1 : 2 * count + 1]
    own_small, next_small, both_small = refs[2 * count + 1 : 2 * count + 4]
    scratch = refs[2 * count + 4 :]
    held, crossed, from_below, from_above = (
        scratch[n * count : (n + 1) * count] for n in range(4)
    )
    load_sem, x_send, x_recv, up_send, up_recv, down_send, down_recv = scratch[4 * count : -3]
    small_buffer, small_send, small_recv = scratch[-3:]
    deep, side, device = place_in_line()
    core, line, half = lax.axis_index("section"), lax.axis_index("fsdp"), lax.axis_index("tp")
    greet_all()
    across_core = (1 - core, line, half)
    partners = [
        device(deep, 1 - side),
        device(deep + 1 - 2 * (deep % 2), side),
        device((deep + 2) % DEEP, side),
        (core, line, 1 - half),
        across_core,
        across_core,
    ]

    def swap_small(n, source, target):
        return pltpu.make_async_remote_copy(
            src_ref=source,
            dst_ref=target,
            send_sem=small_send.at[n],
            recv_sem=small_recv.at[n],
            device_id=partners[n],
            device_id_type=MESH,
        )

    def sum_small():
        for n in range(3):
            copy = swap_small(n, small if n == 0 else small_buffer.at[n - 1], small_buffer.at[3 + n])
            if n > 0:
                copy.start()
            copy.wait()
            value = small[...] if n == 0 else small_buffer[n - 1]
            small_buffer[n] = value + small_buffer[3 + n]
        over_tp = swap_small(3, small_buffer.at[2], small_buffer.at[6])
        over_core = swap_small(4, small_buffer.at[2], next_small)
        over_tp.start()
        over_core.start()
        own_small[...] = small_buffer[2]
        over_tp.wait()
        small_buffer[7] = small_buffer[2] + small_buffer[6]
        last = swap_small(5, small_buffer.at[7], small_buffer.at[8])
        last.start()
        last.wait()
        both_small[...] = small_buffer[7] + small_buffer[8]
        over_core.wait()

    def rows(i, z, x):
        size = results[i].shape[0]
        return parts[i].at[pl.ds((z * 2 + x) * size, size)]

    def load(i, z):
        return pltpu.make_async_copy(rows(i, z, side), held[i].at[z], load_sem.at[i, z])

    def across(i, z):
        return pltpu.make_async_remote_copy(
            src_ref=rows(i, z, 1 - side),
            dst_ref=crossed[i].at[z],
            send_sem=x_send.at[i, z],
            recv_sem=x_recv.at[i, z],
            device_id=device(deep, 1 - side),
            device_id_type=MESH,
        )

    def upward(i, k, z, here):
        return pltpu.make_async_remote_copy(
            src_ref=held[i].at[z],
            dst_ref=from_below[i].at[k - 1],
            send_sem=up_send.at[i, k - 1],
            recv_sem=up_recv.at[i, k - 1],
            device_id=device(min(here + 1, DEEP - 1), side),
            device_id_type=MESH,
        )

    def downward(i, k, z, here):
        return pltpu.make_async_remote_copy(
            src_ref=held[i].at[z],
            dst_ref=from_above[i].at[k - 1],
            send_sem=down_send.at[i, k - 1],
            recv_sem=down_recv.at[i, k - 1],
            device_id=device(max(here - 1, 0), side),
            device_id_type=MESH,
        )

    def at_depth(here):
        order = X_ORDER[here]
        last = DEEP - 1
        started = []

        def send_across(number):
            for i in range(count):
                across(i, order[number]).start()

        def take(number):
            z = order[number]
            for i in range(count):
                across(i, z).wait_recv()
            if number + 2 < DEEP:
                send_across(number + 2)
            for i in range(count):
                load(i, z).wait()
                add_rows(held[i].at[z], held[i].at[z], crossed[i].at[z])

        def relay(k, up):
            z = DEEP - k + here if up else here + k - DEEP
            first = here == 0 if up else here == last
            for i in range(count):
                if not first:
                    make = upward if up else downward
                    back = from_below if up else from_above
                    make(i, k - 1, z, here).wait_recv()
                    add_rows(held[i].at[z], held[i].at[z], back[i].at[k - 2])
                copy = (upward if up else downward)(i, k, z, here)
                copy.start()
                started.append(copy)

        swap_small(0, small, small_buffer.at[3]).start()
        send_across(0)
        send_across(1)
        for number in range(DEEP):
            for i in range(count):
                load(i, order[number]).start()
        sum_small()
        if here in (0, last):
            up = here == 0
            for k in range(1, DEEP):
                take(k - 1)
                relay(k, up)
            take(DEEP - 1)
        else:
            up = here == 1
            take(0)
            take(1)
            relay(2, up)
            relay(3, not up)
            take(2)
            relay(3, up)
            take(3)
        for i in range(count):
            terms = [held[i].at[here]]
            if here > 0:
                upward(i, DEEP - 1, here, here).wait_recv()
                terms.append(from_below[i].at[DEEP - 2])
            if here < last:
                downward(i, DEEP - 1, here, here).wait_recv()
                terms.append(from_above[i].at[DEEP - 2])
            add_rows(results[i], *terms)
        for copy in started:
            copy.wait_send()
        for z in range(DEEP):
            for i in range(count):
                across(i, z).wait_send()

    for here in range(DEEP):

        @pl.when(deep == here)
        def _(here=here):
            at_depth(here)


def reduce_line(parts, small, name, collective_id):
    count = len(parts)
    shards = [(p.shape[0] // (2 * DEEP),) + p.shape[1:] for p in parts]
    pairs = pltpu.SemaphoreType.DMA((count, DEEP))
    sizes = sum(p.size for p in parts)
    blocks = lambda n: [pltpu.VMEM((n,) + shard, BF16) for shard in shards]
    shape = jax.ShapeDtypeStruct
    vmem = pl.BlockSpec(memory_space=pltpu.VMEM)
    return pl.pallas_call(
        functools.partial(reduce_kernel, count=count),
        out_shape=[shape(shard, F32) for shard in shards] + [shape(small.shape, F32)] * 3,
        in_specs=[pl.BlockSpec(memory_space=pl.ANY)] * count + [vmem],
        out_specs=[vmem] * (count + 3),
        scratch_shapes=blocks(DEEP)
        + blocks(DEEP)
        + blocks(DEEP - 1)
        + blocks(DEEP - 1)
        + [pairs] * 7
        + [
            pltpu.VMEM((9,) + small.shape, F32),
            pltpu.SemaphoreType.DMA((6,)),
            pltpu.SemaphoreType.DMA((6,)),
        ],
        compiler_params=pltpu.CompilerParams(
            collective_id=collective_id, has_side_effects=True, vmem_limit_bytes=VMEM_LIMIT
        ),
        cost_estimate=pl.CostEstimate(flops=1000, bytes_accessed=1000, transcendentals=0),
        name=name,
    )(*parts, small)


SWAP = [(0, 1), (1, 0)]


def swap_core(value):
    return lax.ppermute(value, "section", SWAP)


def swap_tp(value):
    return lax.ppermute(value, "tp", SWAP)


def by_index(index, own, other):
    first = index == 0
    return jnp.stack([jnp.where(first, own, other), jnp.where(first, other, own)])


def pick(pair, index):
    return lax.dynamic_index_in_dim(pair, index, 0, keepdims=False)


def gather_tokens(own, core, half, beside=()):
    both = by_index(half, own, after(swap_tp(own), *beside))
    whole = by_index(core, both, swap_core(both))
    whole = jnp.moveaxis(whole, 0, 1)
    return whole.reshape((4 * own.shape[0],) + own.shape[1:])


def after(value, *others):
    return lax.optimization_barrier((value,) + others)[0] if others else value


def over_cores(part, core):
    split_rows = part.reshape((2, 2, part.shape[0] // 4) + part.shape[1:])
    mine = lax.dynamic_index_in_dim(split_rows, core, 1, keepdims=False)
    theirs = lax.dynamic_index_in_dim(split_rows, 1 - core, 1, keepdims=False)
    return mine + swap_core(theirs)


class Sum:
    def __init__(self, part, core, half):
        self.half = half
        self.total = over_cores(part, core)
        sent = pick(self.total, 1 - half)
        self.sent = sent.astype(BF16) if part.ndim > 1 else sent

    def done(self, *beside):
        return pick(self.total, self.half) + after(swap_tp(self.sent), *beside).astype(F32)


def local(
    inputs,
    cotangent,
    norm_gain,
    w_zx,
    w_bc,
    w_dt,
    conv_x,
    conv_xb,
    conv_bc,
    conv_bcb,
    dt_bias,
    a_log,
    d_skip,
    gate_gain,
    w_out,
):
    cores = lax.axis_size("section")
    core = lax.axis_index("section")
    half = lax.axis_index("tp")
    micros = inputs.shape[1]
    rows = inputs.shape[2] // cores
    channels = w_zx.shape[3] // cores
    heads = w_dt.shape[2] // cores
    width = channels // heads
    shared = w_bc.shape[2]
    depth = w_zx.shape[1]
    in_width = 2 * channels + shared + LANES
    def cut(tensor, index, size):
        return lax.dynamic_slice_in_dim(tensor, index * size, size, tensor.ndim - 1)

    def weight_shard(index):
        zx = cut(w_zx[0], index, channels).reshape(depth, 2 * channels)
        steps = jnp.pad(cut(w_dt[0], index, heads), ((0, 0), (0, LANES - heads)))
        return jnp.concatenate([zx, w_bc[0], steps, cut(w_out[0], index, channels)], axis=1)

    def slab_of(index):
        pad = jnp.zeros((LANES - heads,), F32)
        steps = jnp.concatenate([cut(dt_bias[0], index, heads), pad])
        decay = jnp.concatenate([-jnp.exp(cut(a_log[0], index, heads)), pad])
        skip = jnp.repeat(cut(d_skip[0], index, heads), width)
        rest = jnp.zeros((shared - LANES,), F32)
        taps = jnp.concatenate([cut(conv_x[0], index, channels), conv_bc[0]], axis=1)
        bias = jnp.concatenate([cut(conv_xb[0], index, channels), conv_bcb[0]])
        return jnp.concatenate(
            [
                taps,
                bias[None],
                jnp.concatenate([cut(gate_gain[0], index, channels), steps, rest])[None],
                jnp.concatenate([skip, decay, rest])[None],
                jnp.zeros((1, channels + shared), F32),
            ]
        )

    own_shard = weight_shard(core)
    got_shard = swap_core(weight_shard(1 - core))
    own_slab = slab_of(core)
    got_slab = swap_core(slab_of(1 - core))
    in_line = lax.axis_size("fsdp") == 2 * DEEP and lax.axis_size("tp") == 2
    over_fsdp = functools.partial(lax.all_gather, axis_name="fsdp", tiled=True)
    slabs = [jnp.where(core == layer, own_slab, got_slab) for layer in range(2)]
    shards = []
    for layer in range(2):
        shard = jnp.where(core == layer, own_shard, got_shard)
        shards.append((shard[:, :in_width], shard[:, in_width:]))
    gain_pair = by_index(core, norm_gain[0], swap_core(norm_gain[0])).astype(F32)

    def own_rows(tensor):
        return [
            lax.dynamic_slice_in_dim(tensor[0, m], core * rows, rows, 0) for m in range(micros)
        ]

    first = own_rows(inputs)
    if in_line:
        packed = jnp.pad(gain_pair.reshape(-1, LANES), ((0, 8 - 2 * depth // LANES), (0, 0)))
        w_in, w_back, gains, first_normed = start_gather(
            shards[0], packed, jnp.concatenate(first), micros
        )
        projections = [(w_in, w_back)]
        shards[1] = lax.optimization_barrier(shards[1] + (gains,))[:2]
        gains = jnp.moveaxis(
            gains[:, : 2 * depth // LANES].reshape(2 * DEEP, 2, depth), 0, 1
        ).reshape(2, -1)
        first_normed = first_normed.reshape(micros, 4 * rows, -1)
    else:
        projections = [tuple(over_fsdp(v, axis=0) for v in shards[0])]
        gains = over_fsdp(gain_pair.astype(BF16), axis=1).astype(F32)
        first_normed = None
    projections.append(tuple(over_fsdp(v, axis=0) for v in shards[1]))

    lane = jnp.arange(LANES)
    head_of = jnp.arange(channels) // width
    spread = ((lane[:, None] % heads == head_of[None, :]) & (lane[:, None] < 2 * heads)).astype(BF16)
    gather = (head_of[:, None] == lane[None, :]).astype(BF16)

    size = channels + shared
    zero_state = jnp.zeros((shared // 2, channels), F32)
    zero_halo = jnp.zeros((HALO, size), F32)
    last = micros - 1

    def norm(h, layer):
        scale = lax.rsqrt(jnp.mean(h * h, axis=1, keepdims=True) + EPS)
        return scale, (h * scale * gains[layer][None]).astype(BF16)

    hidden = [v.astype(F32) for v in first]
    cotangents = own_rows(cotangent)
    normed = [None] * micros
    scales = [[None] * micros for _ in range(2)]
    for m in range(micros):
        scales[0][m], own = norm(hidden[m], 0)
        normed[m] = first_normed[m] if in_line else gather_tokens(own, core, half)

    hiddens, normeds, kept = [hidden, None], [normed, None], [[None] * micros for _ in range(2)]
    waiting = None

    def finish(pending, *beside):
        layer, m, part, squares = pending
        r = lax.rsqrt(squares.done(*beside) / DI + EPS)[:, None]
        branch = r * part.done(*beside)
        kept[layer][m].update(r=r, branch=branch)
        h = hiddens[layer][m] + branch
        if layer == 0:
            hiddens[1][m] = h
            scales[1][m], own = norm(h, 1)
            return own
        results[m] = h
        g = cotangents[m].astype(F32)
        return jnp.concatenate([r, r * r * jnp.sum(g * branch, axis=1, keepdims=True) / DI], axis=1)

    def spread_out(pending, own, *beside):
        layer, m = pending[:2]
        if layer == 0:
            normeds[1][m] = gather_tokens(own, core, half, beside)
        else:
            factors[m] = gather_tokens(own, core, half, beside)

    results, factors = [None] * micros, [None] * micros
    hiddens[1], normeds[1] = [None] * micros, [None] * micros
    everyones = [gather_tokens(v, core, half) for v in cotangents]
    for layer in range(2):
        w_in, w_back = projections[layer]
        state, tail = zero_state, zero_halo
        for m in range(micros):
            tokens = normeds[layer][m]
            if layer == 1 and m == 0:
                tokens = after(tokens, *everyones)
            if waiting is not None:
                tokens = after(tokens, waiting[2].sent, waiting[3].sent)
            pre = dot_nn(tokens, w_in)
            mixed_pre = pre
            if waiting is not None:
                own = finish(waiting, pre)
                mixed_pre = after(pre, own)
            u, squares, y, entering, state_out = mixer_forward(
                mixed_pre, tail, state, slabs[layer], spread, heads
            )
            if waiting is not None:
                spread_out(waiting, own, u)
            kept[layer][m] = dict(pre=pre, tail=tail, u=u, y=y, entering=entering)
            state, tail = state_out, pre[-HALO:, channels : channels + size]
            part = Sum(dot_nt(u, w_back), core, half)
            waiting = (layer, m, part, Sum(squares[:, 0], core, half))
    spread_out(waiting, finish(waiting))

    over_tokens = (((0,), (0,)), ((), ()))

    def weight_grad(left, right):
        return lax.dot_general(
            jnp.concatenate(left), jnp.concatenate(right), over_tokens, preferred_element_type=F32
        ).astype(BF16)

    reduced, small = [None, None], [None, None]
    grads = [v.astype(F32) for v in cotangents]
    backs = [
        (everyone.astype(F32) * factor[:, :1]).astype(BF16)
        for everyone, factor in zip(everyones, factors)
    ]
    kappas = [factor[:, 1:] for factor in factors]
    gain_parts = [[], []]
    next_backs, next_kappas = [None] * micros, [None] * micros
    waiting = None

    def finish_back(pending, *beside):
        layer, m, part = pending
        h, scale = hiddens[layer][m], scales[layer][m]
        g_norm = part.done(*beside)
        gain_parts[layer].append(jnp.sum(g_norm * (h * scale), axis=0))
        g_norm = g_norm * gains[layer][None]
        mean = jnp.mean(g_norm * h, axis=1, keepdims=True)
        g = grads[m] + scale * g_norm - h * (scale * scale * scale) * mean
        grads[m] = g
        if layer == 0:
            return g, g
        r, branch = kept[0][m]["r"], kept[0][m]["branch"]
        return (g * r).astype(BF16), r * r * jnp.sum(g * branch, axis=1)[:, None] / DI

    def spread_back(pending, own, *beside):
        layer, m = pending[:2]
        if layer == 1:
            next_backs[m] = gather_tokens(own[0], core, half, beside)
            next_kappas[m] = gather_tokens(own[1], core, half, beside)

    def reduce_rows(part):
        return lax.psum_scatter(part, "fsdp", scatter_dimension=0, tiled=True).astype(F32)

    previous = ()
    for layer in (1, 0):
        w_in, w_back = projections[layer]
        state, e_rows = zero_state, zero_halo
        totals = jnp.zeros(slabs[0].shape, F32)
        gpres = [None] * micros
        for m in reversed(range(micros)):
            k = kept[layer][m]
            back = backs[m]
            if waiting is not None and waiting[0] == layer:
                back = after(back, waiting[2].sent)
            q = dot_nn(back, w_back)
            if m == last:
                if layer == 1:
                    grad_back = weight_grad(backs, [kept[layer][j]["u"] for j in range(micros)])
                    q = after(q, grad_back)
                    reduced_back = reduce_rows(grad_back)
                    previous = (reduced_back,)
            gpre, state, e_rows, sums = mixer_backward(
                q,
                kappas[m],
                k["pre"],
                k["tail"],
                k["y"],
                k["entering"],
                state,
                e_rows,
                slabs[layer],
                spread,
                gather,
                heads,
            )
            totals = totals + sums
            gpres[m] = gpre
            if waiting is not None and waiting[0] != layer:
                spread_back(waiting, own, gpre)
                backs[waiting[1]], kappas[waiting[1]] = next_backs[waiting[1]], next_kappas[waiting[1]]
                waiting = None
            ready = gpre
            if waiting is not None:
                own = finish_back(waiting, gpre)
                ready = after(gpre, *own)
            part = Sum(dot_nt(ready, w_in), core, half)
            if waiting is not None:
                spread_back(waiting, own, part.total)
            waiting = (layer, m, part)
        grad_in = weight_grad(normeds[layer], [after(v, waiting[2].sent) for v in gpres])
        if layer == 0:
            grad_back = weight_grad(backs, [kept[layer][j]["u"] for j in range(micros)])
        own = finish_back(waiting, grad_in)
        small[layer] = jnp.concatenate([totals.reshape(-1), sum(gain_parts[layer])])
        if layer == 1 or not in_line:
            if layer == 0:
                reduced_back = reduce_rows(grad_back)
            reduced[layer] = (reduce_rows(after(grad_in, *previous)), reduced_back)
        backs = [after(v, *own) if v is not None else None for v in next_backs]
        kappas = list(next_kappas)

    def placed_rows(parts):
        own = jnp.where(core == 0, parts[0], parts[1])
        other = jnp.where(core == 0, parts[1], parts[0])
        return by_index(core, own, swap_core(other)).reshape(1, 1, 2 * rows, -1)

    outputs, input_grads = placed_rows(results), placed_rows(grads)

    small_sums = jnp.stack(small)
    if in_line:
        flat = small_sums.reshape(-1, LANES)
        *reduced[0], own_small, next_small, both_small = reduce_line(
            [grad_in, grad_back], flat, "grads_reduce", 2
        )
        own_small, next_small, both_small = (
            pick(v.reshape(small_sums.shape), core) for v in (own_small, next_small, both_small)
        )
    else:
        small_sums = lax.psum(small_sums, "fsdp")
        own_small = pick(small_sums, core)
        next_small = swap_core(pick(small_sums, 1 - core))
        both_small = own_small + next_small
        both_small = both_small + swap_tp(both_small)
    count = slabs[0].size
    halves = by_index(core, own_small[:count], next_small[:count]).reshape((2,) + slabs[0].shape)
    conv_sum = both_small[:count].reshape(slabs[0].shape)[:5, channels:]
    gain_sum = lax.dynamic_slice_in_dim(
        both_small[count:], lax.axis_index("fsdp") * depth, depth, 0
    )
    wide = jnp.concatenate([halves[0, :7, :channels], halves[1, :7, :channels]], axis=1)
    narrow = jnp.concatenate(
        [halves[j, 5:7, channels : channels + heads] for j in range(2)], axis=1
    )
    skip_sum = wide[6].reshape(2 * heads, width).sum(axis=1)

    mine = [jnp.where(core == 0, reduced[0][i], reduced[1][i]) for i in range(2)]
    theirs = [jnp.where(core == 0, reduced[1][i], reduced[0][i]) for i in range(2)]
    got = [swap_core(v) for v in theirs]
    first_half = [jnp.where(core == 0, own, other) for own, other in zip(mine, got)]
    second_half = [jnp.where(core == 0, other, own) for own, other in zip(mine, got)]

    def joined(begin, end, i=0):
        return jnp.concatenate([first_half[i][:, begin:end], second_half[i][:, begin:end]], axis=1)

    g_zx = jnp.stack([joined(0, channels), joined(channels, 2 * channels)], axis=1)
    at = 2 * channels
    g_bc = mine[0][:, at : at + shared] + got[0][:, at : at + shared]
    g_bc = g_bc + swap_tp(g_bc)
    g_dt = joined(at + shared, at + shared + heads)
    g_back = joined(0, channels, 1)

    return (
        outputs,
        input_grads,
        gain_sum[None],
        g_zx[None],
        g_bc[None],
        g_dt[None],
        wide[:4][None],
        wide[4][None],
        conv_sum[:4][None],
        conv_sum[4][None],
        narrow[0][None],
        narrow[1][None],
        skip_sum[None],
        wide[5][None],
        g_back[None],
    )


def solution(mesh):
    placed = (
        P("fsdp", None, "tp", None),
        P("fsdp", None, "tp", None),
        P("section", "fsdp"),
        P("section", "fsdp", None, "tp"),
        P("section", "fsdp", None),
        P("section", "fsdp", "tp"),
        P("section", None, "tp"),
        P("section", "tp"),
        P("section", None, None),
        P("section", None),
        P("section", "tp"),
        P("section", "tp"),
        P("section", "tp"),
        P("section", "tp"),
        P("section", "fsdp", "tp"),
    )
    return jax.shard_map(
        local,
        mesh=mesh,
        in_specs=placed,
        out_specs=(
            P("fsdp", "section", "tp", None),
            P("fsdp", "section", "tp", None),
        )
        + placed[2:],
        check_vma=False,
    )
```

```python
import functools

import jax
import jax.numpy as jnp
import numpy as np
from jax import lax
from jax.experimental import pallas as pl
from jax.experimental.pallas import tpu as pltpu
from jax.sharding import PartitionSpec as P

CONV = 4
DI = 4096
EPS = 1e-05
CHUNK = 128
LANES = 128
HALO = 8
NEG = -10000.0
HIGHEST = lax.Precision.HIGHEST
F32 = jnp.float32
BF16 = jnp.bfloat16
VMEM_LIMIT = 56 * 1024 * 1024
MIXER_VMEM = 24 * 1024 * 1024
BACK_VMEM = 40 * 1024 * 1024


def sigmoid(v):
    return 0.5 * jnp.tanh(0.5 * v) + 0.5


def dot_nn(a, b):
    return lax.dot_general(a, b, (((1,), (0,)), ((), ())), preferred_element_type=F32)


def dot_nt(a, b):
    return lax.dot_general(a, b, (((1,), (1,)), ((), ())), preferred_element_type=F32)


def dot_exact(a, b):
    return lax.dot_general(
        a, b, (((1,), (0,)), ((), ())), preferred_element_type=F32, precision=HIGHEST
    )


def split(a):
    high = a.astype(BF16)
    return high, (a - high.astype(F32)).astype(BF16)


def dot3(a, b, dot=dot_nn):
    return dot(a[0], b[0]) + (dot(a[1], b[0]) + dot(a[0], b[1]))


def tri(shape, keep):
    rows = lax.broadcasted_iota(jnp.int32, shape, 0)
    cols = lax.broadcasted_iota(jnp.int32, shape, 1)
    return keep(rows, cols)


def expand(columns, spread, heads):
    high = columns.astype(BF16).astype(F32)
    rest = columns - high
    packed = high + pltpu.roll(rest, heads, 1)
    return dot_nn(packed.astype(BF16), spread)


def step_terms(pre_dt, slab, channels, heads, spread):
    lane = lax.broadcasted_iota(jnp.int32, pre_dt.shape, 1)
    live = lane < heads
    arg = pre_dt + slab[5:6, channels : channels + LANES]
    dt = jnp.where(live, jnp.maximum(arg, 0.0) + jnp.log1p(jnp.exp(-jnp.abs(arg))), 0.0)
    decay = slab[6:7, channels : channels + LANES]
    lower = tri((CHUNK, CHUNK), lambda r, c: r >= c).astype(F32)
    cum = dot_exact(lower, dt * decay)
    last = cum[CHUNK - 1 : CHUNK, :]
    grown = jnp.where(live, jnp.exp(cum), 0.0)
    left = jnp.where(live, jnp.exp(last - cum), 0.0)
    wide = expand(jnp.concatenate([dt, grown, left], axis=0), spread, heads)
    return arg, dt, decay, cum, wide[:CHUNK], wide[CHUNK : 2 * CHUNK], wide[2 * CHUNK :]


def conv_rows(buffer, slab):
    out = slab[4:5, :] + slab[CONV - 1 : CONV, :] * buffer[HALO : HALO + CHUNK, :]
    for k in range(CONV - 1):
        first = HALO - (CONV - 1) + k
        out = out + slab[k : k + 1, :] * buffer[first : first + CHUNK, :]
    return out


def forward_kernel(
    gate, rest, tail, start, slab, spread, u, sq, y, entering, leaving, state, buffer, *, channels, heads
):
    step = pl.program_id(0)
    size = channels + 2 * LANES

    @pl.when(step == 0)
    def _():
        state[...] = start[...]
        buffer[0:HALO, :] = tail[...]

    @pl.when(step > 0)
    def _():
        buffer[0:HALO, :] = buffer[CHUNK : CHUNK + HALO, :]

    buffer[HALO:, :] = rest[:, :size]
    entering[0] = state[...]
    conv = conv_rows(buffer, slab)
    act = conv * sigmoid(conv)
    xs = act[:, :channels]
    in_map = act[:, channels : channels + LANES]
    out_map = act[:, channels + LANES :]
    arg, dt, decay, cum, dt_w, grown_w, left_w = step_terms(
        rest[:, size:], slab, channels, heads, spread[...]
    )
    cum_t = cum.T
    xt = xs * dt_w
    xt_s = split(xt)
    out_s = split(out_map)
    scores = dot3(out_s, split(in_map), dot_nt)
    held = state[...]
    base = grown_w * dot3(out_s, split(held)) + slab[6:7, :channels] * xs
    state[...] = held * grown_w[CHUNK - 1 : CHUNK, :] + dot3(
        split(in_map.T), split(xt * left_w)
    )
    causal = tri((CHUNK, CHUNK), lambda r, c: r >= c)
    first_half = lax.broadcasted_iota(jnp.int32, (CHUNK, LANES), 1) < LANES // 2
    zero = jnp.zeros((CHUNK, LANES), BF16)
    for pair in range(channels // LANES):
        cols = slice(pair * LANES, (pair + 1) * LANES)
        mats = []
        for h in (2 * pair, 2 * pair + 1):
            gap = cum[:, h : h + 1] - cum_t[h : h + 1, :]
            mats.append(scores * jnp.exp(jnp.where(causal, gap, NEG)))
        stacked = tuple(
            jnp.concatenate(
                [jnp.where(first_half, xp[:, cols], zero), jnp.where(first_half, zero, xp[:, cols])],
                axis=0,
            )
            for xp in xt_s
        )
        y[:, cols] = base[:, cols] + dot3(split(jnp.concatenate(mats, axis=1)), stacked)
    z = gate[...]
    gated = y[...] * (z * sigmoid(z))
    sq[...] = jnp.sum(gated * gated, axis=1, keepdims=True)
    u[...] = (gated * slab[5:6, :channels]).astype(BF16)

    @pl.when(step == pl.num_programs(0) - 1)
    def _():
        leaving[...] = state[...]


def backward_kernel(
    q,
    factor,
    gate,
    rest,
    before,
    tail,
    y,
    entering,
    grad_start,
    e_start,
    slab,
    spread,
    gather,
    gpre,
    grad_leaving,
    e_leaving,
    sums,
    grad,
    buffer,
    e_buffer,
    *,
    channels,
    heads,
):
    step = pl.program_id(0)
    steps = pl.num_programs(0)
    size = channels + 2 * LANES

    @pl.when(step == 0)
    def _():
        grad[...] = grad_start[...]
        e_buffer[CHUNK:, :] = e_start[...]
        sums[...] = jnp.zeros_like(sums)

    @pl.when(step > 0)
    def _():
        e_buffer[CHUNK:, :] = e_buffer[0:HALO, :]

    @pl.when(step == steps - 1)
    def _():
        buffer[0:HALO, :] = tail[...]

    @pl.when(step < steps - 1)
    def _():
        buffer[0:HALO, :] = before[:, :size]

    buffer[HALO:, :] = rest[:, :size]
    conv = conv_rows(buffer, slab)
    sig = sigmoid(conv)
    act = conv * sig
    d_act = sig * (1.0 + conv * (1.0 - sig))
    xs = act[:, :channels]
    in_map = act[:, channels : channels + LANES]
    out_map = act[:, channels + LANES :]
    arg, dt, decay, cum, dt_w, grown_w, left_w = step_terms(
        rest[:, size:], slab, channels, heads, spread[...]
    )
    cum_t = cum.T

    z = gate[...]
    sig_z = sigmoid(z)
    silu_z = z * sig_z
    yv = y[...]
    gated = yv * silu_z
    qv = q[...] * factor[:, 0:1]
    sums[5:6, :channels] += jnp.sum(qv * gated, axis=0, keepdims=True)
    g_gated = qv * slab[5:6, :channels] - gated * factor[:, 1:2]
    gpre[:, :channels] = (g_gated * yv * (sig_z * (1.0 + z * (1.0 - sig_z)))).astype(BF16)
    gy = g_gated * silu_z
    gy_b = gy.astype(BF16)
    skip_row = jnp.sum(gy * xs, axis=0, keepdims=True)

    xt = xs * dt_w
    xt_b = xt.astype(BF16)
    in_b = in_map.astype(BF16)
    out_b = out_map.astype(BF16)
    held = entering[0]
    held_b = held.astype(BF16)
    g_state = grad[...]
    g_state_b = g_state.astype(BF16)
    grown_last = grown_w[CHUNK - 1 : CHUNK, :]

    from_state = grown_w * dot_nn(out_b, held_b)
    ge_b = (grown_w * gy).astype(BF16)
    g_out_map = dot_nt(ge_b, held_b)
    g_xt = left_w * dot_nn(in_b, g_state_b)
    g_in_map = dot_nt((xt * left_w).astype(BF16), g_state_b)
    through = jnp.sum(g_state * held, axis=0, keepdims=True) * grown_last
    grad[...] = g_state * grown_last + dot_nn(out_map.T.astype(BF16), ge_b)
    row_terms = gy * from_state
    col_terms = xt * g_xt

    scores_t = dot3(split(in_map), split(out_map), dot_nt)
    later = tri((CHUNK, CHUNK), lambda r, c: c >= r)
    first_half = lax.broadcasted_iota(jnp.int32, (CHUNK, LANES), 1) < LANES // 2
    lane = lax.broadcasted_iota(jnp.int32, (CHUNK, LANES), 1)
    zero = jnp.zeros((CHUNK, LANES), BF16)
    g_scores_t = jnp.zeros((CHUNK, CHUNK), F32)
    gap_rows = []
    gap_cols = jnp.zeros((CHUNK, LANES), F32)
    g_xt_parts = []
    for pair in range(channels // LANES):
        cols = slice(pair * LANES, (pair + 1) * LANES)
        gp = gy_b[:, cols]
        stacked = jnp.concatenate(
            [jnp.where(first_half, gp, zero), jnp.where(first_half, zero, gp)], axis=0
        )
        g_mats = dot_nt(xt_b[:, cols], stacked)
        mats = []
        for number in range(2):
            h = 2 * pair + number
            gap = cum_t[h : h + 1, :] - cum[:, h : h + 1]
            weight = jnp.exp(jnp.where(later, gap, NEG))
            mats.append((scores_t * weight).astype(BF16))
            g_score = g_mats[:, number * CHUNK : (number + 1) * CHUNK] * weight
            g_scores_t = g_scores_t + g_score
            g_gap = g_score * scores_t
            gap_rows.append(jnp.sum(g_gap, axis=0, keepdims=True))
            gap_cols = jnp.where(lane == h, jnp.sum(g_gap, axis=1, keepdims=True), gap_cols)
        g_xt_parts.append(g_xt[:, cols] + dot_nn(jnp.concatenate(mats, axis=1), stacked))
    g_xt = jnp.concatenate(g_xt_parts, axis=1)
    g_scores_b = g_scores_t.astype(BF16)
    g_in_map = g_in_map + dot_nn(g_scores_b, out_b)
    g_out_map = g_out_map + dot_nn(g_scores_t.T.astype(BF16), in_b)
    g_xs = slab[6:7, :channels] * gy + dt_w * g_xt

    pad = jnp.zeros((CHUNK - heads, CHUNK), F32)
    gap_rows_t = jnp.concatenate(gap_rows + [pad], axis=0).T
    packed = jnp.concatenate(
        [
            xs * g_xt,
            row_terms,
            col_terms,
            jnp.broadcast_to(through, (HALO, channels)),
            jnp.broadcast_to(skip_row, (HALO, channels)),
        ],
        axis=0,
    )
    high, rest = split(packed)
    grouped = dot_nn(high, gather[...]) + dot_nn(rest, gather[...])
    direct = grouped[:CHUNK]
    row_sum = grouped[CHUNK : 2 * CHUNK]
    col_sum = grouped[2 * CHUNK : 3 * CHUNK]
    through_sum = grouped[3 * CHUNK : 3 * CHUNK + 1]
    sums[7:8, channels : channels + LANES] += grouped[3 * CHUNK + HALO : 3 * CHUNK + HALO + 1]
    upper = tri((CHUNK, CHUNK), lambda r, c: c >= r).astype(F32)
    below = tri((CHUNK, CHUNK), lambda r, c: r > c).astype(F32)
    g_log = (
        dot_exact(upper, gap_rows_t - gap_cols + row_sum) + dot_exact(below, col_sum) + through_sum
    )
    g_dt = direct + g_log * decay
    g_dtin = jnp.where(lane < heads, g_dt * sigmoid(arg), 0.0)
    sums[5:6, channels : channels + LANES] += jnp.sum(g_dtin, axis=0, keepdims=True)
    sums[6:7, channels : channels + LANES] += decay * jnp.sum(dt * g_log, axis=0, keepdims=True)

    e = jnp.concatenate([g_xs, g_in_map, g_out_map], axis=1) * d_act
    e_buffer[0:CHUNK, :] = e
    sums[4:5, :] += jnp.sum(e, axis=0, keepdims=True)
    for k in range(CONV):
        first = HALO - (CONV - 1) + k
        sums[k : k + 1, :] += jnp.sum(e * buffer[first : first + CHUNK, :], axis=0, keepdims=True)
    g_pre = slab[CONV - 1 : CONV, :] * e
    for k in range(CONV - 1):
        first = CONV - 1 - k
        g_pre = g_pre + slab[k : k + 1, :] * e_buffer[first : first + CHUNK, :]
    gpre[:, channels : channels + size] = g_pre.astype(BF16)
    gpre[:, channels + size :] = g_dtin.astype(BF16)

    @pl.when(step == steps - 1)
    def _():
        grad_leaving[...] = grad[...]
        e_leaving[...] = e_buffer[0:HALO, :]


def fixed(shape):
    return pl.BlockSpec(shape, lambda i: (0,) * len(shape))


def mixer_forward(gate, rest, tail, start, slab, spread, heads):
    rows, width = rest.shape
    state_size, channels = start.shape
    size = channels + 2 * LANES
    steps = rows // CHUNK
    by_row = lambda cols: pl.BlockSpec((CHUNK, cols), lambda i: (i, 0))
    shape = jax.ShapeDtypeStruct

    def body(*refs):
        forward_kernel(*refs, channels=channels, heads=heads)

    return pl.pallas_call(
        body,
        grid=(steps,),
        in_specs=[
            by_row(channels),
            by_row(width),
            fixed((HALO, size)),
            fixed(start.shape),
            fixed(slab.shape),
            fixed(spread.shape),
        ],
        out_specs=[
            by_row(channels),
            by_row(1),
            by_row(channels),
            pl.BlockSpec((1, state_size, channels), lambda i: (i, 0, 0)),
            fixed(start.shape),
        ],
        out_shape=[
            shape((rows, channels), BF16),
            shape((rows, 1), F32),
            shape((rows, channels), F32),
            shape((steps, state_size, channels), F32),
            shape(start.shape, F32),
        ],
        scratch_shapes=[
            pltpu.VMEM((state_size, channels), F32),
            pltpu.VMEM((CHUNK + HALO, size), F32),
        ],
        compiler_params=pltpu.CompilerParams(
            dimension_semantics=("arbitrary",), vmem_limit_bytes=MIXER_VMEM
        ),
        cost_estimate=pl.CostEstimate(flops=1000, bytes_accessed=1000, transcendentals=0),
        name="mixer_forward",
    )(gate, rest, tail, start, slab, spread)


def mixer_backward(
    q, factor, gate, rest, tail, y, entering, grad, e_rows, slab, spread, gather, heads
):
    rows, width = rest.shape
    state_size, channels = grad.shape
    size = channels + 2 * LANES
    steps = rows // CHUNK
    by_row = lambda cols: pl.BlockSpec((CHUNK, cols), lambda i: (steps - 1 - i, 0))
    shape = jax.ShapeDtypeStruct
    groups = CHUNK // HALO

    def body(*refs):
        backward_kernel(*refs, channels=channels, heads=heads)

    return pl.pallas_call(
        body,
        grid=(steps,),
        in_specs=[
            by_row(channels),
            by_row(2),
            by_row(channels),
            by_row(width),
            pl.BlockSpec(
                (HALO, width), lambda i: (jnp.maximum((steps - 1 - i) * groups - 1, 0), 0)
            ),
            fixed((HALO, size)),
            by_row(channels),
            pl.BlockSpec((1, state_size, channels), lambda i: (steps - 1 - i, 0, 0)),
            fixed(grad.shape),
            fixed(e_rows.shape),
            fixed(slab.shape),
            fixed(spread.shape),
            fixed(gather.shape),
        ],
        out_specs=[
            by_row(channels + width),
            fixed(grad.shape),
            fixed(e_rows.shape),
            fixed(slab.shape),
        ],
        out_shape=[
            shape((rows, channels + width), BF16),
            shape(grad.shape, F32),
            shape(e_rows.shape, F32),
            shape(slab.shape, F32),
        ],
        scratch_shapes=[
            pltpu.VMEM((state_size, channels), F32),
            pltpu.VMEM((CHUNK + HALO, size), F32),
            pltpu.VMEM((CHUNK + HALO, size), F32),
        ],
        compiler_params=pltpu.CompilerParams(
            dimension_semantics=("arbitrary",), vmem_limit_bytes=BACK_VMEM
        ),
        cost_estimate=pl.CostEstimate(flops=1000, bytes_accessed=1000, transcendentals=0),
        name="mixer_backward",
    )(q, factor, gate, rest, rest, tail, y, entering, grad, e_rows, slab, spread, gather)


MESH = pl.DeviceIdType.MESH
DEEP = 4


def place_in_line():
    core, line, half = lax.axis_index("section"), lax.axis_index("fsdp"), lax.axis_index("tp")
    deep, side = line // 2, line % 2

    def device(z, x):
        return (core, z * 2 + x, half)

    return deep, side, device


def greet_all():
    core, line, half = lax.axis_index("section"), lax.axis_index("fsdp"), lax.axis_index("tp")
    barrier = pltpu.get_barrier_semaphore()

    def greet(target):
        pl.semaphore_signal(barrier, inc=1, device_id=target, device_id_type=MESH)

    greet((core, line, 1 - half))
    greet((1 - core, line, half))
    for step in range(1, 2 * DEEP):
        greet((core, (line + step) % (2 * DEEP), half))
    pl.semaphore_wait(barrier, 2 * DEEP + 1)


def gather_steps(shards, wholes, sems, beside=None):
    count = len(shards)
    local_sem, x_send, x_recv, up_send, up_recv, down_send, down_recv = sems
    deep, side, device = place_in_line()

    def rows(i, z, x):
        size = shards[i].shape[0]
        return wholes[i].at[pl.ds((z * 2 + x) * size, size)]

    def move(i, z, source, send, recv, target):
        return pltpu.make_async_remote_copy(
            src_ref=rows(i, z, side) if source is None else source,
            dst_ref=rows(i, z, side),
            send_sem=send,
            recv_sem=recv,
            device_id=target,
            device_id_type=MESH,
        )

    def across(i, z, source=None):
        return move(i, z, source, x_send.at[i, z], x_recv.at[i, z], device(deep, 1 - side))

    def upward(i, k, source=None):
        above = jnp.minimum(deep + 1, DEEP - 1)
        return move(i, deep - k, source, up_send.at[i, k], up_recv.at[i, k], device(above, side))

    def downward(i, k, source=None):
        below = jnp.maximum(deep - 1, 0)
        return move(i, deep + k, source, down_send.at[i, k], down_recv.at[i, k], device(below, side))

    has_above, has_below = deep < DEEP - 1, deep > 0
    for i in range(count):
        pltpu.make_async_copy(shards[i], rows(i, deep, side), local_sem.at[i]).start()

        @pl.when(has_above)
        def _(i=i):
            upward(i, 0, shards[i]).start()

        @pl.when(has_below)
        def _(i=i):
            downward(i, 0, shards[i]).start()

        across(i, deep, shards[i]).start()

    if beside is not None:
        beside()
    for k in range(1, DEEP):
        for i in range(count):

            @pl.when(deep >= k)
            def _(i=i, k=k):
                arrived = move(
                    i, deep - k, None, up_send.at[i, k - 1], up_recv.at[i, k - 1], device(deep, side)
                )
                arrived.wait_recv()

                @pl.when(has_above)
                def _():
                    upward(i, k).start()

                across(i, deep - k).start()

            @pl.when(deep + k <= DEEP - 1)
            def _(i=i, k=k):
                arrived = move(
                    i, deep + k, None, down_send.at[i, k - 1], down_recv.at[i, k - 1], device(deep, side)
                )
                arrived.wait_recv()

                @pl.when(has_below)
                def _():
                    downward(i, k).start()

                across(i, deep + k).start()

    for i in range(count):
        pltpu.make_async_copy(shards[i], rows(i, deep, side), local_sem.at[i]).wait()
        for z in range(DEEP):
            other = pltpu.make_async_remote_copy(
                src_ref=rows(i, z, side),
                dst_ref=rows(i, z, 1 - side),
                send_sem=x_send.at[i, z],
                recv_sem=x_recv.at[i, z],
                device_id=device(deep, 1 - side),
                device_id_type=MESH,
            )
            other.wait_send()
            other.wait_recv()
        for k in range(DEEP - 1):

            @pl.when(has_above & (deep >= k))
            def _(i=i, k=k):
                upward(i, k).wait_send()

            @pl.when(has_below & (deep + k <= DEEP - 1))
            def _(i=i, k=k):
                downward(i, k).wait_send()


def start_kernel(*refs, count, micros, heads, gain_rows):
    shards, (gain, own, cotangent) = refs[:count], refs[count : count + 3]
    params, spread = refs[count + 3 : count + 9], refs[count + 9]
    outs = refs[count + 10 :]
    wholes, (gains, slabs), targets = outs[:count], outs[count : count + 2], outs[count + 2 :]
    targets, scratch = targets[: 2 * micros], targets[2 * micros :]
    gain_send, gain_recv, own_sem, y_send, y_recv, core_send, core_recv, rows_out = scratch[7:15]
    other_slab, slab_send, slab_recv, line_send, line_recv = scratch[15:]
    core, line, half = lax.axis_index("section"), lax.axis_index("fsdp"), lax.axis_index("tp")
    lines = 2 * DEEP

    greet_all()
    across_tp, across_core = (core, line, 1 - half), (1 - core, line, half)

    def send_gain(step):
        return pltpu.make_async_remote_copy(
            src_ref=gain,
            dst_ref=gains.at[core, line],
            send_sem=gain_send.at[step],
            recv_sem=gain_recv.at[step],
            device_id=(core, (line + step) % lines, half),
            device_id_type=MESH,
        )

    for step in range(1, lines):
        send_gain(step).start()

    tokens = own.shape[0] // micros

    def token_copies(n):
        m, held = n % micros, (rows_out, cotangent)[n // micros]
        source = held.at[pl.ds(m * tokens, tokens)]
        place = targets[n].at[half, core]
        later = targets[n].at[1 - half, core]
        more = 2 * micros + n
        remote = functools.partial(pltpu.make_async_remote_copy, device_id_type=MESH)
        return (
            pltpu.make_async_copy(source, place, own_sem.at[n]),
            remote(source, place, y_send.at[n], y_recv.at[n], device_id=across_tp),
            remote(source, place, core_send.at[n], core_recv.at[n], device_id=across_core),
            remote(later, later, core_send.at[more], core_recv.at[more], device_id=across_core),
        )

    send_slab = pltpu.make_async_remote_copy(
        src_ref=other_slab,
        dst_ref=slabs.at[core],
        send_sem=slab_send.at[0],
        recv_sem=slab_recv.at[0],
        device_id=across_core,
        device_id_type=MESH,
    )
    send_line = pltpu.make_async_remote_copy(
        src_ref=gains.at[core],
        dst_ref=gains.at[core],
        send_sem=line_send.at[0],
        recv_sem=line_recv.at[0],
        device_id=across_core,
        device_id_type=MESH,
    )

    def write_slab(place, index):
        taps, bias, shared_taps, shared_bias, gate, per_head = (v[...] for v in params)
        channels = spread.shape[1]
        first = index == 0
        cut = lambda v: jnp.where(first, v[:, :channels], v[:, channels:])
        lane = lax.broadcasted_iota(jnp.int32, per_head.shape, 1)
        here = jnp.where(first, per_head, pltpu.roll(per_head, LANES - heads, 1))
        here = jnp.where(lane < heads, here, 0.0)
        skip = expand(here, spread[...], heads)
        decay = jnp.where(lane < heads, -jnp.exp(here), 0.0)
        place[...] = jnp.zeros(place.shape, F32)
        place[0:CONV, :channels] = cut(taps)
        place[0:CONV, channels:] = shared_taps
        place[CONV : CONV + 1, :channels] = cut(bias)
        place[CONV : CONV + 1, channels:] = shared_bias
        place[5:6, :channels] = cut(gate)
        place[5:6, channels : channels + LANES] = here[0:1]
        place[6:7, :channels] = skip[2:3]
        place[6:7, channels : channels + LANES] = decay[1:2]

    def send_tokens():
        write_slab(other_slab, 1 - core)
        send_slab.start()
        write_slab(slabs.at[core], core)
        gains[core, line] = gain[...]
        for step in range(1, lines):
            send_gain(step).wait()
        send_line.start()
        send_line.wait()
        gain_row = jnp.concatenate(
            [gains[0, f, j : j + 1, :] for f in range(lines) for j in range(gain_rows)], axis=1
        )
        h = own[...].astype(F32)
        scale = lax.rsqrt(jnp.mean(h * h, axis=1, keepdims=True) + EPS)
        rows_out[...] = (h * scale * gain_row).astype(BF16)

        for n in range(2 * micros):
            for copy in token_copies(n)[:3]:
                copy.start()
        for n in range(micros):
            token_copies(n)[1].wait_recv()
            token_copies(n)[3].start()

    gather_steps(shards, wholes, scratch[:7], send_tokens)
    for n in range(micros, 2 * micros):
        token_copies(n)[1].wait_recv()
        token_copies(n)[3].start()
    send_slab.wait()
    for n in range(2 * micros):
        own_copy, y_copy, core_copy, core_later = token_copies(n)
        own_copy.wait()
        y_copy.wait_send()
        core_copy.wait()
        core_later.wait()


def start_gather(shards, gain, own, cotangent, params, spread, micros, heads, gain_rows):
    count = len(shards)
    lines = 2 * DEEP
    pairs = pltpu.SemaphoreType.DMA((count, DEEP))
    dma = lambda n: pltpu.SemaphoreType.DMA((n,))
    shape = jax.ShapeDtypeStruct
    anywhere = pl.BlockSpec(memory_space=pl.ANY)
    vmem = pl.BlockSpec(memory_space=pltpu.VMEM)
    rows, width = own.shape
    slab = (8, spread.shape[1] + params[2].shape[1])
    return pl.pallas_call(
        functools.partial(
            start_kernel, count=count, micros=micros, heads=heads, gain_rows=gain_rows
        ),
        out_shape=[shape((v.shape[0] * lines, v.shape[1]), v.dtype) for v in shards]
        + [
            shape((2, lines) + gain.shape, F32),
            shape((2,) + slab, F32),
        ]
        + [shape((2, 2, rows // micros, width), BF16)] * (2 * micros),
        in_specs=[anywhere] * count + [vmem, vmem, anywhere] + [vmem] * 7,
        out_specs=[anywhere] * count + [vmem, vmem] + [anywhere] * (2 * micros),
        scratch_shapes=[dma(count)]
        + [pairs] * 6
        + [dma(lines)] * 2
        + [dma(2 * micros)] * 3
        + [dma(4 * micros)] * 2
        + [pltpu.VMEM(own.shape, BF16), pltpu.VMEM(slab, F32)]
        + [dma(1)] * 4,
        compiler_params=pltpu.CompilerParams(
            collective_id=1, has_side_effects=True, vmem_limit_bytes=VMEM_LIMIT
        ),
        cost_estimate=pl.CostEstimate(flops=170_000_000_000, bytes_accessed=1000, transcendentals=0),
        name="start_gather",
    )(*shards, gain, own, cotangent, *params, spread)


def add_rows(out, *parts):
    rows = out.shape[0]
    step = 32

    def body(n, _):
        at = pl.ds(pl.multiple_of(n * step, step), step)
        total = parts[0][at].astype(F32)
        for part in parts[1:]:
            total = total + part[at].astype(F32)
        out[at] = total.astype(out.dtype)
        return 0

    lax.fori_loop(0, rows // step, body, 0)


X_ORDER = ((3, 2, 1, 0), (3, 0, 2, 1), (0, 3, 1, 2), (0, 1, 2, 3))


def reduce_kernel(*refs, count):
    parts, small, results = refs[:count], refs[count], refs[count + 1 : 2 * count + 1]
    others = refs[2 * count + 1 : 3 * count + 1]
    own_small, next_small, both_small = refs[3 * count + 1 : 3 * count + 4]
    scratch = refs[3 * count + 4 :]
    held, crossed, from_below, from_above = (
        scratch[n * count : (n + 1) * count] for n in range(4)
    )
    load_sem, x_send, x_recv, up_send, up_recv, down_send, down_recv = scratch[4 * count : -5]
    small_buffer, small_send, small_recv, other_send, other_recv = scratch[-5:]
    deep, side, device = place_in_line()
    core, line, half = lax.axis_index("section"), lax.axis_index("fsdp"), lax.axis_index("tp")
    greet_all()
    across_core = (1 - core, line, half)
    partners = [
        device(deep, 1 - side),
        device(deep + 1 - 2 * (deep % 2), side),
        device((deep + 2) % DEEP, side),
        (core, line, 1 - half),
        across_core,
        across_core,
    ]

    def swap_small(n, source, target):
        return pltpu.make_async_remote_copy(
            src_ref=source,
            dst_ref=target,
            send_sem=small_send.at[n],
            recv_sem=small_recv.at[n],
            device_id=partners[n],
            device_id_type=MESH,
        )

    def sum_small():
        for n in range(3):
            copy = swap_small(n, small if n == 0 else small_buffer.at[n - 1], small_buffer.at[3 + n])
            if n > 0:
                copy.start()
            copy.wait()
            value = small[...] if n == 0 else small_buffer[n - 1]
            small_buffer[n] = value + small_buffer[3 + n]
        over_tp = swap_small(3, small_buffer.at[2], small_buffer.at[6])
        over_core = swap_small(4, small_buffer.at[2, 1 - core], next_small)
        over_tp.start()
        over_core.start()
        own_small[...] = small_buffer[2, core]
        over_tp.wait()
        small_buffer[7] = small_buffer[2] + small_buffer[6]
        last = swap_small(5, small_buffer.at[7, 1 - core], small_buffer.at[8, 0])
        last.start()
        last.wait()
        both_small[...] = small_buffer[7, core] + small_buffer[8, 0]
        over_core.wait()

    def rows(i, z, x):
        size = results[i].shape[0]
        return parts[i].at[pl.ds((z * 2 + x) * size, size)]

    def load(i, z):
        return pltpu.make_async_copy(rows(i, z, side), held[i].at[z], load_sem.at[i, z])

    def across(i, z):
        return pltpu.make_async_remote_copy(
            src_ref=rows(i, z, 1 - side),
            dst_ref=crossed[i].at[z],
            send_sem=x_send.at[i, z],
            recv_sem=x_recv.at[i, z],
            device_id=device(deep, 1 - side),
            device_id_type=MESH,
        )

    def upward(i, k, z, here):
        return pltpu.make_async_remote_copy(
            src_ref=held[i].at[z],
            dst_ref=from_below[i].at[k - 1],
            send_sem=up_send.at[i, k - 1],
            recv_sem=up_recv.at[i, k - 1],
            device_id=device(min(here + 1, DEEP - 1), side),
            device_id_type=MESH,
        )

    def downward(i, k, z, here):
        return pltpu.make_async_remote_copy(
            src_ref=held[i].at[z],
            dst_ref=from_above[i].at[k - 1],
            send_sem=down_send.at[i, k - 1],
            recv_sem=down_recv.at[i, k - 1],
            device_id=device(max(here - 1, 0), side),
            device_id_type=MESH,
        )

    def to_other(i):
        return pltpu.make_async_remote_copy(
            src_ref=results[i],
            dst_ref=others[i],
            send_sem=other_send.at[i],
            recv_sem=other_recv.at[i],
            device_id=across_core,
            device_id_type=MESH,
        )

    def at_depth(here):
        order = X_ORDER[here]
        last = DEEP - 1
        started = []

        def send_across(number):
            for i in range(count):
                across(i, order[number]).start()

        def take(number):
            z = order[number]
            for i in range(count):
                across(i, z).wait_recv()
            if number + 2 < DEEP:
                send_across(number + 2)
            for i in range(count):
                load(i, z).wait()
                add_rows(held[i].at[z], held[i].at[z], crossed[i].at[z])

        def relay(k, up):
            z = DEEP - k + here if up else here + k - DEEP
            first = here == 0 if up else here == last
            for i in range(count):
                if not first:
                    make = upward if up else downward
                    back = from_below if up else from_above
                    make(i, k - 1, z, here).wait_recv()
                    add_rows(held[i].at[z], held[i].at[z], back[i].at[k - 2])
                copy = (upward if up else downward)(i, k, z, here)
                copy.start()
                started.append(copy)

        swap_small(0, small, small_buffer.at[3]).start()
        send_across(0)
        send_across(1)
        for number in range(DEEP):
            for i in range(count):
                load(i, order[number]).start()
        sum_small()
        if here in (0, last):
            up = here == 0
            for k in range(1, DEEP):
                take(k - 1)
                relay(k, up)
            take(DEEP - 1)
        else:
            up = here == 1
            take(0)
            take(1)
            relay(2, up)
            relay(3, not up)
            take(2)
            relay(3, up)
            take(3)
        for i in range(count):
            terms = [held[i].at[here]]
            if here > 0:
                upward(i, DEEP - 1, here, here).wait_recv()
                terms.append(from_below[i].at[DEEP - 2])
            if here < last:
                downward(i, DEEP - 1, here, here).wait_recv()
                terms.append(from_above[i].at[DEEP - 2])
            add_rows(results[i], *terms)
            to_other(i).start()
        for i in range(count):
            to_other(i).wait()
        for copy in started:
            copy.wait_send()
        for z in range(DEEP):
            for i in range(count):
                across(i, z).wait_send()

    for here in range(DEEP):

        @pl.when(deep == here)
        def _(here=here):
            at_depth(here)


def reduce_line(parts, small, name, collective_id):
    count = len(parts)
    shards = [(p.shape[0] // (2 * DEEP),) + p.shape[1:] for p in parts]
    pairs = pltpu.SemaphoreType.DMA((count, DEEP))
    sizes = sum(p.size for p in parts)
    blocks = lambda n: [pltpu.VMEM((n,) + shard, BF16) for shard in shards]
    shape = jax.ShapeDtypeStruct
    vmem = pl.BlockSpec(memory_space=pltpu.VMEM)
    return pl.pallas_call(
        functools.partial(reduce_kernel, count=count),
        out_shape=[shape(shard, F32) for shard in shards] * 2 + [shape(small.shape[1:], F32)] * 3,
        in_specs=[pl.BlockSpec(memory_space=pl.ANY)] * count + [vmem],
        out_specs=[vmem] * (2 * count + 3),
        scratch_shapes=blocks(DEEP)
        + blocks(DEEP)
        + blocks(DEEP - 1)
        + blocks(DEEP - 1)
        + [pairs] * 7
        + [
            pltpu.VMEM((9,) + small.shape, F32),
            pltpu.SemaphoreType.DMA((6,)),
            pltpu.SemaphoreType.DMA((6,)),
            pltpu.SemaphoreType.DMA((count,)),
            pltpu.SemaphoreType.DMA((count,)),
        ],
        compiler_params=pltpu.CompilerParams(
            collective_id=collective_id, has_side_effects=True, vmem_limit_bytes=VMEM_LIMIT
        ),
        cost_estimate=pl.CostEstimate(flops=1000, bytes_accessed=1000, transcendentals=0),
        name=name,
    )(*parts, small)


SWAP = [(0, 1), (1, 0)]


def swap_core(value):
    return lax.ppermute(value, "section", SWAP)


def swap_tp(value):
    return lax.ppermute(value, "tp", SWAP)


def by_index(index, own, other):
    first = index == 0
    return jnp.stack([jnp.where(first, own, other), jnp.where(first, other, own)])


def pick(pair, index):
    return lax.dynamic_index_in_dim(pair, index, 0, keepdims=False)


def gather_tokens(own, core, half, beside=()):
    both = by_index(half, own, after(swap_tp(own), *beside))
    whole = by_index(core, both, swap_core(both))
    whole = jnp.moveaxis(whole, 0, 1)
    return whole.reshape((4 * own.shape[0],) + own.shape[1:])


def after(value, *others):
    return lax.optimization_barrier((value,) + others)[0] if others else value


def over_cores(part, core, *beside):
    split_rows = part.reshape((2, 2, part.shape[0] // 4) + part.shape[1:])
    mine = lax.dynamic_index_in_dim(split_rows, core, 1, keepdims=False)
    theirs = lax.dynamic_index_in_dim(split_rows, 1 - core, 1, keepdims=False)
    return mine.astype(F32) + after(swap_core(theirs), *beside).astype(F32)


class Sum:
    def __init__(self, part, core, half, needed=(), beside=()):
        self.half = half
        self.total = over_cores(part, core, *beside)
        sent = after(pick(self.total, 1 - half), *needed)
        self.sent = sent.astype(BF16) if part.ndim > 1 else sent

    def done(self, *beside):
        return pick(self.total, self.half) + after(swap_tp(self.sent), *beside).astype(F32)


def local(
    inputs,
    cotangent,
    norm_gain,
    w_zx,
    w_bc,
    w_dt,
    conv_x,
    conv_xb,
    conv_bc,
    conv_bcb,
    dt_bias,
    a_log,
    d_skip,
    gate_gain,
    w_out,
):
    cores = lax.axis_size("section")
    core = lax.axis_index("section")
    half = lax.axis_index("tp")
    micros = inputs.shape[1]
    rows = inputs.shape[2] // cores
    channels = w_zx.shape[3] // cores
    heads = w_dt.shape[2] // cores
    width = channels // heads
    shared = w_bc.shape[2]
    depth = w_zx.shape[1]
    in_width = 2 * channels + shared + LANES
    def cut(tensor, index, size):
        return lax.dynamic_slice_in_dim(tensor, index * size, size, tensor.ndim - 1)

    def weight_shard(index):
        zx = cut(w_zx[0], index, channels).reshape(depth, 2 * channels)
        steps = jnp.pad(cut(w_dt[0], index, heads), ((0, 0), (0, LANES - heads)))
        return jnp.concatenate([zx, w_bc[0], steps, cut(w_out[0], index, channels)], axis=1)

    def slab_of(index):
        pad = jnp.zeros((LANES - heads,), F32)
        steps = jnp.concatenate([cut(dt_bias[0], index, heads), pad])
        decay = jnp.concatenate([-jnp.exp(cut(a_log[0], index, heads)), pad])
        skip = jnp.repeat(cut(d_skip[0], index, heads), width)
        rest = jnp.zeros((shared - LANES,), F32)
        taps = jnp.concatenate([cut(conv_x[0], index, channels), conv_bc[0]], axis=1)
        bias = jnp.concatenate([cut(conv_xb[0], index, channels), conv_bcb[0]])
        return jnp.concatenate(
            [
                taps,
                bias[None],
                jnp.concatenate([cut(gate_gain[0], index, channels), steps, rest])[None],
                jnp.concatenate([skip, decay, rest])[None],
                jnp.zeros((1, channels + shared), F32),
            ]
        )

    lane = np.arange(LANES)
    head_of = np.arange(channels) // width
    spread = (lane[:, None] % heads == head_of[None, :]) & (lane[:, None] < 2 * heads)
    spread = jnp.asarray(spread.astype(np.float32), BF16)
    gather = jnp.asarray((head_of[:, None] == lane[None, :]).astype(np.float32), BF16)

    own_shard = weight_shard(core)
    got_shard = swap_core(weight_shard(1 - core))
    in_line = lax.axis_size("fsdp") == 2 * DEEP and lax.axis_size("tp") == 2
    over_fsdp = functools.partial(lax.all_gather, axis_name="fsdp", tiled=True)
    shards = []
    for layer in range(2):
        shard = jnp.where(core == layer, own_shard, got_shard)
        shards.append((shard[:, :in_width], shard[:, in_width:]))

    def own_rows(tensor):
        return [
            lax.dynamic_slice_in_dim(tensor[0, m], core * rows, rows, 0) for m in range(micros)
        ]

    first, cotangents = own_rows(inputs), own_rows(cotangent)
    if in_line:
        gain_rows = depth // LANES
        packed = jnp.pad(norm_gain.astype(F32).reshape(-1, LANES), ((0, 8 - gain_rows), (0, 0)))
        per_head = jnp.concatenate([dt_bias, a_log, d_skip])
        per_head = jnp.pad(per_head, ((0, 5), (0, LANES - per_head.shape[1])))
        params = (conv_x[0], conv_xb, conv_bc[0], conv_bcb, gate_gain, per_head)
        w_in, w_back, gains, slabs, *tokens = start_gather(
            shards[0],
            packed,
            jnp.concatenate(first),
            jnp.concatenate(cotangents),
            params,
            spread,
            micros,
            heads,
            gain_rows,
        )
        slabs = [slabs[0], slabs[1]]
        projections = [(w_in, w_back)]
        early = 8 * LANES
        parts = [over_fsdp(shards[1][0][:, :early], axis=0)]
        parts.append(over_fsdp(after(shards[1][0][:, early:], gains), axis=0))
        projections.append((parts, over_fsdp(after(shards[1][1], gains), axis=0)))
        gains = gains[:, :, :gain_rows].reshape(2, -1)
        tokens = [v.reshape(4 * rows, -1) for v in tokens]
        first_normed, everyones = tokens[:micros], tokens[micros:]
        first_normed[0] = after(first_normed[0], parts[0])
    else:
        own_slab, got_slab = slab_of(core), swap_core(slab_of(1 - core))
        slabs = [jnp.where(core == layer, own_slab, got_slab) for layer in range(2)]
        gain_pair = by_index(core, norm_gain[0], swap_core(norm_gain[0])).astype(F32)
        projections = [tuple(over_fsdp(v, axis=0) for v in shards[0])]
        gains = over_fsdp(gain_pair.astype(BF16), axis=1).astype(F32)
        first_normed = None
        everyones = [gather_tokens(v, core, half) for v in cotangents]
    if not in_line:
        projections.append(tuple(over_fsdp(v, axis=0) for v in shards[1]))

    size = channels + shared
    zero_state = jnp.zeros((shared // 2, channels), F32)
    zero_halo = jnp.zeros((HALO, size), F32)
    last = micros - 1

    def scale_of(h):
        return lax.rsqrt(jnp.mean(h * h, axis=1, keepdims=True) + EPS)

    def norm(h, layer):
        return (h * scale_of(h) * gains[layer][None]).astype(BF16)

    hidden = [v.astype(F32) for v in first]
    normed = [None] * micros
    for m in range(micros):
        normed[m] = (
            first_normed[m] if in_line else gather_tokens(norm(hidden[m], 0), core, half)
        )

    hiddens, normeds, kept = [hidden, None], [normed, None], [[None] * micros for _ in range(2)]
    waiting = None

    def finish(pending, *beside):
        m, part, squares = pending
        r = lax.rsqrt(squares.done(*beside) / DI + EPS)[:, None]
        branch = r * part.done(*beside)
        kept[0][m].update(r=r, branch=branch)
        h = hiddens[0][m] + branch
        hiddens[1][m] = h
        return norm(h, 1)

    def spread_out(pending, own, *beside):
        normeds[1][pending[0]] = gather_tokens(own, core, half, beside)

    hiddens[1], normeds[1] = [None] * micros, [None] * micros
    for layer in range(2):
        w_in, w_back = projections[layer]
        state, tail = zero_state, zero_halo
        for m in range(micros):
            tokens = normeds[layer][m]
            if layer == 0 or not in_line:
                w_pair = (w_in[:, :channels], w_in[:, channels:])
            else:
                w_pair = w_in
            gate = dot_nn(tokens, w_pair[0])
            if waiting is not None and layer == 1:
                tokens = after(tokens, waiting[1].sent, waiting[2].sent)
            rest = dot_nn(tokens, w_pair[1])
            mixed_rest = rest
            if waiting is not None and layer == 1:
                own = finish(waiting, rest)
                mixed_rest = after(rest, own)
            elif waiting is not None:
                mixed_rest = after(rest, waiting[1].sent, waiting[2].sent)
            u, squares, y, entering, state_out = mixer_forward(
                gate, mixed_rest, tail, state, slabs[layer], spread, heads
            )
            if waiting is not None:
                spread_out(waiting, own if layer == 1 else finish(waiting, u), u)
            kept[layer][m] = dict(
                gate=gate, rest=rest, tail=tail, u=u, y=y, entering=entering, squares=squares
            )
            state, tail = state_out, rest[-HALO:, :size]
            waiting = None
            if layer == 0:
                part = Sum(dot_nt(u, w_back).astype(BF16), core, half)
                waiting = (m, part, Sum(squares[:, 0], core, half))

    over_tokens = (((0,), (0,)), ((), ()))

    def weight_grad(left, right):
        return lax.dot_general(
            jnp.concatenate(left), jnp.concatenate(right), over_tokens, preferred_element_type=F32
        ).astype(BF16)

    reduced, small = [None, None], [None, None]
    grads = [v.astype(F32) for v in cotangents]
    w_back = after(projections[1][1], *[kept[1][m]["u"] for m in range(micros)])
    w_in = projections[1][0]
    if in_line:
        w_in = jnp.concatenate([after(v, *[kept[1][m]["u"] for m in range(micros)]) for v in w_in], axis=1)
    projections[1] = (w_in, w_back)
    backs, products, factors = list(everyones), [None] * micros, [None] * micros
    pairs = [None] * micros
    for m in reversed(range(micros)):
        k = kept[1][m]
        products[m] = dot_nn(backs[m], w_back)
        dots = jnp.sum(products[m] * k["u"].astype(F32), axis=1)
        pairs[m] = jnp.stack([k["squares"][:, 0], dots])
    pair = jnp.stack(pairs)
    pair = pair + swap_core(pair)
    pair = pair + swap_tp(pair)
    r = lax.rsqrt(pair[:, 0] / DI + EPS)
    factors = [jnp.stack([r[m], r[m] * r[m] * r[m] * pair[m, 1] / DI], axis=1) for m in range(micros)]
    gain_parts = [[], []]

    def finish_back(pending, *beside):
        layer, m, part = pending
        h = hiddens[layer][m]
        scale = scale_of(h)
        g_norm = part.done(*beside)
        gain_parts[layer].append(jnp.sum(g_norm * (h * scale), axis=0))
        g_norm = g_norm * gains[layer][None]
        mean = jnp.mean(g_norm * h, axis=1, keepdims=True)
        g = grads[m] + scale * g_norm - h * (scale * scale * scale) * mean
        grads[m] = g
        if layer == 0:
            return (g,)
        r, branch = kept[0][m]["r"], kept[0][m]["branch"]
        kappa = r * r * jnp.sum(g * branch, axis=1)[:, None] / DI
        return g.astype(BF16), jnp.concatenate([r, kappa], axis=1)

    def spread_back(pending, own, *beside):
        layer, m = pending[:2]
        if layer == 1:
            next_backs[m] = gather_tokens(own[0], core, half, beside)
            next_factors[m] = gather_tokens(own[1], core, half, beside)

    def reduce_rows(part):
        return lax.psum_scatter(part, "fsdp", scatter_dimension=0, tiled=True)

    waiting, spreading, outs = None, None, [None] * micros
    next_backs, next_factors = [None] * micros, [None] * micros
    for layer in (1, 0):
        w_in, w_back = projections[layer]
        state, e_rows = zero_state, zero_halo
        totals = jnp.zeros(slabs[0].shape, F32)
        gpres = [None] * micros
        for m in reversed(range(micros)):
            k = kept[layer][m]
            q = products[m] if layer == 1 else dot_nn(backs[m], w_back)
            if m == last and layer == 1:
                mixed = [
                    (kept[1][j]["u"].astype(F32) * factors[j][:, :1]).astype(BF16)
                    for j in range(micros)
                ]
                reduced_back = weight_grad(backs, mixed)
                q = after(q, reduced_back)
                reduced_back = reduce_rows(reduced_back)
            if waiting is not None:
                q = after(q, waiting[2].sent)
            gpre, state, e_rows, sums = mixer_backward(
                q,
                factors[m],
                k["gate"],
                k["rest"],
                k["tail"],
                k["y"],
                k["entering"],
                state,
                e_rows,
                slabs[layer],
                spread,
                gather,
                heads,
            )
            totals = totals + sums
            gpres[m] = gpre
            if spreading is not None:
                spread_back(*spreading, gpre)
                j = spreading[0][1]
                backs[j], factors[j] = next_backs[j], next_factors[j]
                spreading = None
            ready = gpre
            earlier = None
            if waiting is not None:
                own = finish_back(waiting, gpre)
                ready = after(gpre, *own)
                earlier = (waiting, own)
            part = dot_nt(ready, w_in).astype(BF16)
            beside = ()
            if layer == 1:
                outs[m] = dot_nt(after(k["u"], part), w_back).astype(BF16)
                beside = (outs[m],)
            waiting = (layer, m, Sum(part, core, half, (), beside))
        grad_in = weight_grad(normeds[layer], [after(v, waiting[2].sent) for v in gpres])
        if layer == 1 or not in_line:
            reduced[layer] = (reduce_rows(grad_in), reduced_back)
        if layer == 0:
            mixed = [
                (kept[0][j]["u"].astype(F32) * factors[j][:, :1]).astype(BF16) for j in range(micros)
            ]
            grad_back = weight_grad(backs, mixed)
            if not in_line:
                reduced[0] = (reduced[0][0], reduce_rows(grad_back))
            outs = [Sum(out, core, half, (gpres[0],)) for out in outs]
        if earlier is not None:
            spread_back(*earlier, grad_in)
        own = finish_back(waiting, grad_in)
        if layer == 1:
            spreading = (waiting, own)
            second_factors = factors
            backs = [None if v is None else after(v, *own) for v in next_backs]
            factors = list(next_factors)
        waiting = None
        small[layer] = jnp.concatenate(
            [
                totals[:6],
                jnp.concatenate(
                    [sum(gain_parts[layer]).reshape(2, -1), totals[6:, channels:]], axis=1
                ),
            ]
        )

    outputs_rows = []
    for m in range(micros):
        r = lax.dynamic_slice_in_dim(second_factors[m], (2 * half + core) * rows, rows, 0)[:, :1]
        outputs_rows.append(hiddens[1][m] + r * outs[m].done(grad_in))

    def placed_rows(parts):
        own = jnp.where(core == 0, parts[0], parts[1])
        other = jnp.where(core == 0, parts[1], parts[0])
        return by_index(core, own, swap_core(other)).reshape(1, 1, 2 * rows, -1)

    outputs, input_grads = placed_rows(outputs_rows), placed_rows(grads)

    small_sums = after(jnp.stack(small), outputs, input_grads)
    if in_line:
        *both_parts, own_small, next_small, both_small = reduce_line(
            [grad_in, grad_back], small_sums, "grads_reduce", 2
        )
        first_own, first_other = both_parts[:2], both_parts[2:]
    else:
        small_sums = lax.psum(small_sums, "fsdp")
        own_small = pick(small_sums, core)
        next_small = swap_core(pick(small_sums, 1 - core))
        both_small = own_small + next_small
        both_small = both_small + swap_tp(both_small)
        first_own, first_other = reduced[0], [swap_core(v) for v in reduced[0]]
    low_small = jnp.where(core == 0, own_small, next_small)
    high_small = jnp.where(core == 0, next_small, own_small)
    wide = jnp.concatenate([low_small[:6, :channels], high_small[:6, :channels]], axis=1)
    narrow = jnp.concatenate(
        [v[5:, channels : channels + heads] for v in (low_small, high_small)], axis=1
    )
    conv_sum = both_small[:5, channels:]
    gain_sum = lax.dynamic_slice_in_dim(
        both_small[6:8, :channels].reshape(-1), lax.axis_index("fsdp") * depth, depth, 0
    )

    second_own = [after(v, own_small) for v in reduced[1]]
    second_other = [swap_core(v) for v in second_own]
    either = lambda one, two: jnp.where(core == 0, one.astype(F32), two.astype(F32))
    low_half = [either(first_own[i], second_other[i]) for i in range(2)]
    high_half = [either(first_other[i], second_own[i]) for i in range(2)]

    def joined(begin, end, i=0):
        return jnp.concatenate([low_half[i][:, begin:end], high_half[i][:, begin:end]], axis=1)

    g_zx = jnp.stack([joined(0, channels), joined(channels, 2 * channels)], axis=1)
    at = 2 * channels
    g_bc = low_half[0][:, at : at + shared] + high_half[0][:, at : at + shared]
    g_bc = g_bc + swap_tp(g_bc)
    g_dt = joined(at + shared, at + shared + heads)
    g_back = joined(0, channels, 1)

    return (
        outputs,
        input_grads,
        gain_sum[None],
        g_zx[None],
        g_bc[None],
        g_dt[None],
        wide[:4][None],
        wide[4][None],
        conv_sum[:4][None],
        conv_sum[4][None],
        narrow[0][None],
        narrow[1][None],
        narrow[2][None],
        wide[5][None],
        g_back[None],
    )


def solution(mesh):
    placed = (
        P("fsdp", None, "tp", None),
        P("fsdp", None, "tp", None),
        P("section", "fsdp"),
        P("section", "fsdp", None, "tp"),
        P("section", "fsdp", None),
        P("section", "fsdp", "tp"),
        P("section", None, "tp"),
        P("section", "tp"),
        P("section", None, None),
        P("section", None),
        P("section", "tp"),
        P("section", "tp"),
        P("section", "tp"),
        P("section", "tp"),
        P("section", "fsdp", "tp"),
    )
    return jax.shard_map(
        local,
        mesh=mesh,
        in_specs=placed,
        out_specs=(
            P("fsdp", "section", "tp", None),
            P("fsdp", "section", "tp", None),
        )
        + placed[2:],
        check_vma=False,
    )
```

```python
import functools

import jax
import jax.numpy as jnp
import numpy as np
from jax import lax
from jax.experimental import pallas as pl
from jax.experimental.pallas import tpu as pltpu
from jax.sharding import PartitionSpec as P

CONV = 4
DI = 4096
EPS = 1e-05
CHUNK = 128
LANES = 128
HALO = 8
NEG = -10000.0
F32 = jnp.float32
BF16 = jnp.bfloat16
VMEM_LIMIT = 56 * 1024 * 1024
MIXER_VMEM = 24 * 1024 * 1024
BACK_VMEM = 40 * 1024 * 1024


def sigmoid(v):
    return 0.5 * jnp.tanh(0.5 * v) + 0.5


def dot_nn(a, b):
    return lax.dot_general(a, b, (((1,), (0,)), ((), ())), preferred_element_type=F32)


def dot_nt(a, b):
    return lax.dot_general(a, b, (((1,), (1,)), ((), ())), preferred_element_type=F32)


def dot_sums(ones, columns, heads):
    high = columns.astype(BF16).astype(F32)
    middle = (columns - high).astype(BF16).astype(F32)
    low = columns - high - middle
    packed = high + pltpu.roll(middle, heads, 1) + pltpu.roll(low, 2 * heads, 1)
    sums = dot_nn(ones.astype(BF16), packed.astype(BF16))
    return sums + pltpu.roll(sums, LANES - heads, 1) + pltpu.roll(sums, LANES - 2 * heads, 1)


def split(a):
    high = a.astype(BF16)
    return high, (a - high.astype(F32)).astype(BF16)


def dot3(a, b, dot=dot_nn):
    return dot(a[0], b[0]) + (dot(a[1], b[0]) + dot(a[0], b[1]))


def tri(shape, keep):
    rows = lax.broadcasted_iota(jnp.int32, shape, 0)
    cols = lax.broadcasted_iota(jnp.int32, shape, 1)
    return keep(rows, cols)


def expand(columns, spread, heads):
    high = columns.astype(BF16).astype(F32)
    rest = columns - high
    packed = high + pltpu.roll(rest, heads, 1)
    return dot_nn(packed.astype(BF16), spread)


def step_terms(pre_dt, slab, channels, heads, spread):
    lane = lax.broadcasted_iota(jnp.int32, pre_dt.shape, 1)
    live = lane < heads
    arg = pre_dt + slab[5:6, channels : channels + LANES]
    dt = jnp.where(live, jnp.maximum(arg, 0.0) + jnp.log1p(jnp.exp(-jnp.abs(arg))), 0.0)
    decay = slab[6:7, channels : channels + LANES]
    lower = tri((CHUNK, CHUNK), lambda r, c: r >= c).astype(F32)
    cum = dot_sums(lower, dt * decay, heads)
    last = cum[CHUNK - 1 : CHUNK, :]
    grown = jnp.where(live, jnp.exp(cum), 0.0)
    left = jnp.where(live, jnp.exp(last - cum), 0.0)
    wide = expand(jnp.concatenate([dt, grown, left], axis=0), spread, heads)
    return arg, dt, decay, cum, wide[:CHUNK], wide[CHUNK : 2 * CHUNK], wide[2 * CHUNK :]


def conv_rows(buffer, slab):
    out = slab[4:5, :] + slab[CONV - 1 : CONV, :] * buffer[HALO : HALO + CHUNK, :]
    for k in range(CONV - 1):
        first = HALO - (CONV - 1) + k
        out = out + slab[k : k + 1, :] * buffer[first : first + CHUNK, :]
    return out


def forward_kernel(
    gate, rest, tail, start, slab, spread, u, sq, y, entering, leaving, state, buffer, *, channels, heads
):
    step = pl.program_id(0)
    size = channels + 2 * LANES

    @pl.when(step == 0)
    def _():
        state[...] = start[...]
        buffer[0:HALO, :] = tail[...]

    @pl.when(step > 0)
    def _():
        buffer[0:HALO, :] = buffer[CHUNK : CHUNK + HALO, :]

    buffer[HALO:, :] = rest[:, :size]
    entering[0] = state[...]
    conv = conv_rows(buffer, slab)
    act = conv * sigmoid(conv)
    xs = act[:, :channels]
    in_map = act[:, channels : channels + LANES]
    out_map = act[:, channels + LANES :]
    arg, dt, decay, cum, dt_w, grown_w, left_w = step_terms(
        rest[:, size:], slab, channels, heads, spread[...]
    )
    cum_t = cum.T
    xt = xs * dt_w
    xt_s = split(xt)
    out_s = split(out_map)
    scores = dot3(out_s, split(in_map), dot_nt)
    held = state[...]
    base = grown_w * dot3(out_s, split(held)) + slab[6:7, :channels] * xs
    state[...] = held * grown_w[CHUNK - 1 : CHUNK, :] + dot3(
        split(in_map.T), split(xt * left_w)
    )
    causal = tri((CHUNK, CHUNK), lambda r, c: r >= c)
    first_half = lax.broadcasted_iota(jnp.int32, (CHUNK, LANES), 1) < LANES // 2
    zero = jnp.zeros((CHUNK, LANES), BF16)
    for pair in range(channels // LANES):
        cols = slice(pair * LANES, (pair + 1) * LANES)
        mats = []
        for h in (2 * pair, 2 * pair + 1):
            gap = cum[:, h : h + 1] - cum_t[h : h + 1, :]
            mats.append(scores * jnp.exp(jnp.where(causal, gap, NEG)))
        stacked = tuple(
            jnp.concatenate(
                [jnp.where(first_half, xp[:, cols], zero), jnp.where(first_half, zero, xp[:, cols])],
                axis=0,
            )
            for xp in xt_s
        )
        y[:, cols] = base[:, cols] + dot3(split(jnp.concatenate(mats, axis=1)), stacked)
    z = gate[...]
    gated = y[...] * (z * sigmoid(z))
    sq[...] = jnp.sum(gated * gated, axis=1, keepdims=True)
    u[...] = (gated * slab[5:6, :channels]).astype(BF16)

    @pl.when(step == pl.num_programs(0) - 1)
    def _():
        leaving[...] = state[...]


def backward_kernel(
    q,
    factor,
    gate,
    rest,
    before,
    tail,
    y,
    entering,
    grad_start,
    e_start,
    slab,
    spread,
    gather,
    gpre,
    grad_leaving,
    e_leaving,
    sums,
    grad,
    buffer,
    e_buffer,
    *,
    channels,
    heads,
):
    step = pl.program_id(0)
    steps = pl.num_programs(0)
    size = channels + 2 * LANES

    @pl.when(step == 0)
    def _():
        grad[...] = grad_start[...]
        e_buffer[CHUNK:, :] = e_start[...]
        sums[...] = jnp.zeros_like(sums)

    @pl.when(step > 0)
    def _():
        e_buffer[CHUNK:, :] = e_buffer[0:HALO, :]

    @pl.when(step == steps - 1)
    def _():
        buffer[0:HALO, :] = tail[...]

    @pl.when(step < steps - 1)
    def _():
        buffer[0:HALO, :] = before[:, :size]

    buffer[HALO:, :] = rest[:, :size]
    conv = conv_rows(buffer, slab)
    sig = sigmoid(conv)
    act = conv * sig
    d_act = sig * (1.0 + conv * (1.0 - sig))
    xs = act[:, :channels]
    in_map = act[:, channels : channels + LANES]
    out_map = act[:, channels + LANES :]
    arg, dt, decay, cum, dt_w, grown_w, left_w = step_terms(
        rest[:, size:], slab, channels, heads, spread[...]
    )
    cum_t = cum.T

    z = gate[...]
    sig_z = sigmoid(z)
    silu_z = z * sig_z
    yv = y[...]
    gated = yv * silu_z
    qv = q[...] * factor[:, 0:1]
    sums[5:6, :channels] += jnp.sum(qv * gated, axis=0, keepdims=True)
    g_gated = qv * slab[5:6, :channels] - gated * factor[:, 1:2]
    gpre[:, :channels] = (g_gated * yv * (sig_z * (1.0 + z * (1.0 - sig_z)))).astype(BF16)
    gy = g_gated * silu_z
    gy_b = gy.astype(BF16)
    skip_row = jnp.sum(gy * xs, axis=0, keepdims=True)

    xt = xs * dt_w
    xt_b = xt.astype(BF16)
    in_b = in_map.astype(BF16)
    out_b = out_map.astype(BF16)
    held = entering[0]
    held_b = held.astype(BF16)
    g_state = grad[...]
    g_state_b = g_state.astype(BF16)
    grown_last = grown_w[CHUNK - 1 : CHUNK, :]

    from_state = grown_w * dot_nn(out_b, held_b)
    ge_b = (grown_w * gy).astype(BF16)
    g_out_map = dot_nt(ge_b, held_b)
    g_xt = left_w * dot_nn(in_b, g_state_b)
    g_in_map = dot_nt((xt * left_w).astype(BF16), g_state_b)
    through = jnp.sum(g_state * held, axis=0, keepdims=True) * grown_last
    grad[...] = g_state * grown_last + dot_nn(out_map.T.astype(BF16), ge_b)
    row_terms = gy * from_state
    col_terms = xt * g_xt

    scores_t = dot3(split(in_map), split(out_map), dot_nt)
    later = tri((CHUNK, CHUNK), lambda r, c: c >= r)
    first_half = lax.broadcasted_iota(jnp.int32, (CHUNK, LANES), 1) < LANES // 2
    lane = lax.broadcasted_iota(jnp.int32, (CHUNK, LANES), 1)
    zero = jnp.zeros((CHUNK, LANES), BF16)
    g_scores_t = jnp.zeros((CHUNK, CHUNK), F32)
    gap_rows = []
    gap_cols = jnp.zeros((CHUNK, LANES), F32)
    g_xt_parts = []
    for pair in range(channels // LANES):
        cols = slice(pair * LANES, (pair + 1) * LANES)
        gp = gy_b[:, cols]
        stacked = jnp.concatenate(
            [jnp.where(first_half, gp, zero), jnp.where(first_half, zero, gp)], axis=0
        )
        g_mats = dot_nt(xt_b[:, cols], stacked)
        mats = []
        for number in range(2):
            h = 2 * pair + number
            gap = cum_t[h : h + 1, :] - cum[:, h : h + 1]
            weight = jnp.exp(jnp.where(later, gap, NEG))
            mats.append((scores_t * weight).astype(BF16))
            g_score = g_mats[:, number * CHUNK : (number + 1) * CHUNK] * weight
            g_scores_t = g_scores_t + g_score
            g_gap = g_score * scores_t
            gap_rows.append(jnp.sum(g_gap, axis=0, keepdims=True))
            gap_cols = jnp.where(lane == h, jnp.sum(g_gap, axis=1, keepdims=True), gap_cols)
        g_xt_parts.append(g_xt[:, cols] + dot_nn(jnp.concatenate(mats, axis=1), stacked))
    g_xt = jnp.concatenate(g_xt_parts, axis=1)
    g_scores_b = g_scores_t.astype(BF16)
    g_in_map = g_in_map + dot_nn(g_scores_b, out_b)
    g_out_map = g_out_map + dot_nn(g_scores_t.T.astype(BF16), in_b)
    g_xs = slab[6:7, :channels] * gy + dt_w * g_xt

    pad = jnp.zeros((CHUNK - heads, CHUNK), F32)
    gap_rows_t = jnp.concatenate(gap_rows + [pad], axis=0).T
    packed = jnp.concatenate(
        [
            xs * g_xt,
            row_terms,
            col_terms,
            jnp.broadcast_to(through, (HALO, channels)),
            jnp.broadcast_to(skip_row, (HALO, channels)),
        ],
        axis=0,
    )
    high, rest = split(packed)
    grouped = dot_nn(high, gather[...]) + dot_nn(rest, gather[...])
    direct = grouped[:CHUNK]
    row_sum = grouped[CHUNK : 2 * CHUNK]
    col_sum = grouped[2 * CHUNK : 3 * CHUNK]
    through_sum = grouped[3 * CHUNK : 3 * CHUNK + 1]
    sums[7:8, channels : channels + LANES] += grouped[3 * CHUNK + HALO : 3 * CHUNK + HALO + 1]
    upper = tri((CHUNK, CHUNK), lambda r, c: c >= r).astype(F32)
    below = tri((CHUNK, CHUNK), lambda r, c: r > c).astype(F32)
    g_log = (
        dot_sums(upper, gap_rows_t - gap_cols + row_sum, heads)
        + dot_sums(below, col_sum, heads)
        + through_sum
    )
    g_dt = direct + g_log * decay
    g_dtin = jnp.where(lane < heads, g_dt * sigmoid(arg), 0.0)
    sums[5:6, channels : channels + LANES] += jnp.sum(g_dtin, axis=0, keepdims=True)
    sums[6:7, channels : channels + LANES] += decay * jnp.sum(dt * g_log, axis=0, keepdims=True)

    e = jnp.concatenate([g_xs, g_in_map, g_out_map], axis=1) * d_act
    e_buffer[0:CHUNK, :] = e
    sums[4:5, :] += jnp.sum(e, axis=0, keepdims=True)
    for k in range(CONV):
        first = HALO - (CONV - 1) + k
        sums[k : k + 1, :] += jnp.sum(e * buffer[first : first + CHUNK, :], axis=0, keepdims=True)
    g_pre = slab[CONV - 1 : CONV, :] * e
    for k in range(CONV - 1):
        first = CONV - 1 - k
        g_pre = g_pre + slab[k : k + 1, :] * e_buffer[first : first + CHUNK, :]
    gpre[:, channels : channels + size] = g_pre.astype(BF16)
    gpre[:, channels + size :] = g_dtin.astype(BF16)

    @pl.when(step == steps - 1)
    def _():
        grad_leaving[...] = grad[...]
        e_leaving[...] = e_buffer[0:HALO, :]


def fixed(shape):
    return pl.BlockSpec(shape, lambda i: (0,) * len(shape))


def mixer_forward(gate, rest, tail, start, slab, spread, heads):
    rows, width = rest.shape
    state_size, channels = start.shape
    size = channels + 2 * LANES
    steps = rows // CHUNK
    by_row = lambda cols: pl.BlockSpec((CHUNK, cols), lambda i: (i, 0))
    shape = jax.ShapeDtypeStruct

    def body(*refs):
        forward_kernel(*refs, channels=channels, heads=heads)

    return pl.pallas_call(
        body,
        grid=(steps,),
        in_specs=[
            by_row(channels),
            by_row(width),
            fixed((HALO, size)),
            fixed(start.shape),
            fixed(slab.shape),
            fixed(spread.shape),
        ],
        out_specs=[
            by_row(channels),
            by_row(1),
            by_row(channels),
            pl.BlockSpec((1, state_size, channels), lambda i: (i, 0, 0)),
            fixed(start.shape),
        ],
        out_shape=[
            shape((rows, channels), BF16),
            shape((rows, 1), F32),
            shape((rows, channels), F32),
            shape((steps, state_size, channels), F32),
            shape(start.shape, F32),
        ],
        scratch_shapes=[
            pltpu.VMEM((state_size, channels), F32),
            pltpu.VMEM((CHUNK + HALO, size), F32),
        ],
        compiler_params=pltpu.CompilerParams(
            dimension_semantics=("arbitrary",), vmem_limit_bytes=MIXER_VMEM
        ),
        cost_estimate=pl.CostEstimate(flops=1000, bytes_accessed=1000, transcendentals=0),
        name="mixer_forward",
    )(gate, rest, tail, start, slab, spread)


def mixer_backward(
    q, factor, gate, rest, tail, y, entering, grad, e_rows, slab, spread, gather, heads, grant
):
    rows, width = rest.shape
    state_size, channels = grad.shape
    size = channels + 2 * LANES
    steps = rows // CHUNK
    by_row = lambda cols: pl.BlockSpec((CHUNK, cols), lambda i: (steps - 1 - i, 0))
    shape = jax.ShapeDtypeStruct
    groups = CHUNK // HALO

    def body(*refs):
        backward_kernel(*refs, channels=channels, heads=heads)

    return pl.pallas_call(
        body,
        grid=(steps,),
        in_specs=[
            by_row(channels),
            by_row(2),
            by_row(channels),
            by_row(width),
            pl.BlockSpec(
                (HALO, width), lambda i: (jnp.maximum((steps - 1 - i) * groups - 1, 0), 0)
            ),
            fixed((HALO, size)),
            by_row(channels),
            pl.BlockSpec((1, state_size, channels), lambda i: (steps - 1 - i, 0, 0)),
            fixed(grad.shape),
            fixed(e_rows.shape),
            fixed(slab.shape),
            fixed(spread.shape),
            fixed(gather.shape),
        ],
        out_specs=[
            by_row(channels + width),
            fixed(grad.shape),
            fixed(e_rows.shape),
            fixed(slab.shape),
        ],
        out_shape=[
            shape((rows, channels + width), BF16),
            shape(grad.shape, F32),
            shape(e_rows.shape, F32),
            shape(slab.shape, F32),
        ],
        scratch_shapes=[
            pltpu.VMEM((state_size, channels), F32),
            pltpu.VMEM((CHUNK + HALO, size), F32),
            pltpu.VMEM((CHUNK + HALO, size), F32),
        ],
        compiler_params=pltpu.CompilerParams(
            dimension_semantics=("arbitrary",), vmem_limit_bytes=grant
        ),
        cost_estimate=pl.CostEstimate(flops=1000, bytes_accessed=1000, transcendentals=0),
        name="mixer_backward",
    )(q, factor, gate, rest, rest, tail, y, entering, grad, e_rows, slab, spread, gather)


def finish_kernel(first_own, first_other, second_own, second_other, gates, *, channels):
    core = lax.axis_index("section")

    def write(low, high):
        for half, source in enumerate((low, high)):
            value = source[...].astype(F32)
            for k in range(2):
                gates[:, k, half * channels : (half + 1) * channels] = value[
                    :, k * channels : (k + 1) * channels
                ]

    @pl.when(core == 0)
    def _():
        write(first_own, first_other)

    @pl.when(core == 1)
    def _():
        write(second_other, second_own)


def join_halves(first_own, first_other, second_own, second_other, channels):
    rows = first_own.shape[0]
    step = 32
    block = pl.BlockSpec((step, 2 * channels), lambda i: (i, 0))
    return pl.pallas_call(
        functools.partial(finish_kernel, channels=channels),
        grid=(rows // step,),
        in_specs=[block] * 4,
        out_specs=pl.BlockSpec((step, 2, 2 * channels), lambda i: (i, 0, 0)),
        out_shape=jax.ShapeDtypeStruct((rows, 2, 2 * channels), F32),
        compiler_params=pltpu.CompilerParams(
            dimension_semantics=("arbitrary",), vmem_limit_bytes=MIXER_VMEM
        ),
        cost_estimate=pl.CostEstimate(flops=1000, bytes_accessed=1000, transcendentals=0),
        name="join_halves",
    )(first_own, first_other, second_own, second_other)


MESH = pl.DeviceIdType.MESH
DEEP = 4
SIDEWAYS = 32


def place_in_line():
    core, line, half = lax.axis_index("section"), lax.axis_index("fsdp"), lax.axis_index("tp")
    deep, side = line // 2, line % 2

    def device(z, x):
        return (core, z * 2 + x, half)

    return deep, side, device


def greet_all():
    core, line, half = lax.axis_index("section"), lax.axis_index("fsdp"), lax.axis_index("tp")
    barrier = pltpu.get_barrier_semaphore()

    def greet(target):
        pl.semaphore_signal(barrier, inc=1, device_id=target, device_id_type=MESH)

    greet((core, line, 1 - half))
    greet((1 - core, line, half))
    for step in range(1, 2 * DEEP):
        greet((core, (line + step) % (2 * DEEP), half))
    pl.semaphore_wait(barrier, 2 * DEEP + 1)


def gather_steps(shards, wholes, sems, beside):
    count = len(shards)
    local_sem, x_send, x_recv, up_send, up_recv, down_send, down_recv = sems[:7]
    side_send, side_recv, pair_up_send, pair_up_recv, pair_down_send, pair_down_recv = sems[7:]
    deep, side, device = place_in_line()
    above, below = jnp.minimum(deep + 1, DEEP - 1), jnp.maximum(deep - 1, 0)
    has_above, has_below = deep < DEEP - 1, deep > 0
    main = [pl.ds(0, shard.shape[0] - SIDEWAYS) for shard in shards]
    rest = [pl.ds(shard.shape[0] - SIDEWAYS, SIDEWAYS) for shard in shards]

    def remote(source, place, send, recv, target):
        return pltpu.make_async_remote_copy(
            src_ref=source,
            dst_ref=place,
            send_sem=send,
            recv_sem=recv,
            device_id=target,
            device_id_type=MESH,
        )

    def own(i):
        return pltpu.make_async_copy(shards[i], wholes[i].at[deep * 2 + side], local_sem.at[i])

    def block(i, z, x=None):
        return wholes[i].at[z * 2 + (side if x is None else x), main[i]]

    def across(i, z, source=None):
        source = block(i, z) if source is None else source
        target = device(deep, 1 - side)
        return remote(source, block(i, z), x_send.at[i, z], x_recv.at[i, z], target)

    def upward(i, k, source=None):
        place = block(i, deep - k)
        source = place if source is None else source
        return remote(source, place, up_send.at[i, k], up_recv.at[i, k], device(above, side))

    def downward(i, k, source=None):
        place = block(i, deep + k)
        source = place if source is None else source
        return remote(source, place, down_send.at[i, k], down_recv.at[i, k], device(below, side))

    def sideways(i, x):
        place = wholes[i].at[deep * 2 + x, rest[i]]
        source = shards[i].at[rest[i]]
        return remote(source, place, side_send.at[i], side_recv.at[i], device(deep, 1 - side))

    def pair(i, z):
        return wholes[i].at[pl.ds(z * 2, 2), rest[i]]

    def pair_up(i, k):
        place = pair(i, deep - k)
        return remote(place, place, pair_up_send.at[i, k], pair_up_recv.at[i, k], device(above, side))

    def pair_down(i, k):
        place = pair(i, deep + k)
        return remote(
            place, place, pair_down_send.at[i, k], pair_down_recv.at[i, k], device(below, side)
        )

    for i in range(count):
        own(i).start()
        sideways(i, side).start()
    for i in range(count):
        source = shards[i].at[main[i]]

        @pl.when(has_above)
        def _(i=i, source=source):
            upward(i, 0, source).start()

        @pl.when(has_below)
        def _(i=i, source=source):
            downward(i, 0, source).start()

        across(i, deep, source).start()
    beside(0)
    here = device(deep, side)
    for k in range(1, DEEP):
        for i in range(count):

            @pl.when(deep >= k)
            def _(i=i, k=k):
                place = block(i, deep - k)
                remote(place, place, up_send.at[i, k - 1], up_recv.at[i, k - 1], here).wait_recv()

                @pl.when(has_above)
                def _():
                    upward(i, k).start()

                across(i, deep - k).start()

            @pl.when(deep + k <= DEEP - 1)
            def _(i=i, k=k):
                place = block(i, deep + k)
                remote(place, place, down_send.at[i, k - 1], down_recv.at[i, k - 1], here).wait_recv()

                @pl.when(has_below)
                def _():
                    downward(i, k).start()

                across(i, deep + k).start()

        if k == DEEP - 2:
            for i in range(count):
                own(i).wait()
                sideways(i, 1 - side).wait_recv()

                @pl.when(has_above)
                def _(i=i):
                    pair_up(i, 0).start()

                @pl.when(has_below)
                def _(i=i):
                    pair_down(i, 0).start()

        beside(k)

    for k in range(1, DEEP):
        for i in range(count):

            @pl.when(deep >= k)
            def _(i=i, k=k):
                place = pair(i, deep - k)
                remote(
                    place, place, pair_up_send.at[i, k - 1], pair_up_recv.at[i, k - 1], here
                ).wait_recv()

                @pl.when(has_above)
                def _():
                    pair_up(i, k).start()

            @pl.when(deep + k <= DEEP - 1)
            def _(i=i, k=k):
                place = pair(i, deep + k)
                remote(
                    place, place, pair_down_send.at[i, k - 1], pair_down_recv.at[i, k - 1], here
                ).wait_recv()

                @pl.when(has_below)
                def _():
                    pair_down(i, k).start()

    for i in range(count):
        sideways(i, side).wait_send()
        for z in range(DEEP):
            other = remote(
                block(i, z), block(i, z, 1 - side), x_send.at[i, z], x_recv.at[i, z], here
            )
            other.wait_send()
            other.wait_recv()
        for k in range(DEEP - 1):

            @pl.when(has_above & (deep >= k))
            def _(i=i, k=k):
                upward(i, k).wait_send()
                pair_up(i, k).wait_send()

            @pl.when(has_below & (deep + k <= DEEP - 1))
            def _(i=i, k=k):
                downward(i, k).wait_send()
                pair_down(i, k).wait_send()


def start_kernel(*refs, count, micros, heads, gain_rows):
    shards, (gain, own, cotangent) = refs[:count], refs[count : count + 3]
    params, spread = refs[count + 3 : count + 9], refs[count + 9]
    outs = refs[count + 10 :]
    wholes, (gains, slabs), targets = outs[:count], outs[count : count + 2], outs[count + 2 :]
    targets, scratch = targets[: 2 * micros], targets[2 * micros :]
    gain_send, gain_recv, own_sem, y_send, y_recv, core_send, core_recv, rows_out = scratch[13:21]
    other_slab, slab_send, slab_recv, line_send, line_recv = scratch[21:]
    core, line, half = lax.axis_index("section"), lax.axis_index("fsdp"), lax.axis_index("tp")
    lines = 2 * DEEP

    greet_all()
    across_tp, across_core = (core, line, 1 - half), (1 - core, line, half)

    def send_gain(step):
        return pltpu.make_async_remote_copy(
            src_ref=gain,
            dst_ref=gains.at[core, line],
            send_sem=gain_send.at[step],
            recv_sem=gain_recv.at[step],
            device_id=(core, (line + step) % lines, half),
            device_id_type=MESH,
        )

    for step in range(1, lines):
        send_gain(step).start()

    tokens = own.shape[0] // micros

    def token_copies(n):
        m, held = n % micros, (rows_out, cotangent)[n // micros]
        source = held.at[pl.ds(m * tokens, tokens)]
        place = targets[n].at[half, core]
        later = targets[n].at[1 - half, core]
        more = 2 * micros + n
        remote = functools.partial(pltpu.make_async_remote_copy, device_id_type=MESH)
        return (
            pltpu.make_async_copy(source, place, own_sem.at[n]),
            remote(source, place, y_send.at[n], y_recv.at[n], device_id=across_tp),
            remote(source, place, core_send.at[n], core_recv.at[n], device_id=across_core),
            remote(later, later, core_send.at[more], core_recv.at[more], device_id=across_core),
        )

    send_slab = pltpu.make_async_remote_copy(
        src_ref=other_slab,
        dst_ref=slabs.at[core],
        send_sem=slab_send.at[0],
        recv_sem=slab_recv.at[0],
        device_id=across_core,
        device_id_type=MESH,
    )
    send_line = pltpu.make_async_remote_copy(
        src_ref=gains.at[core],
        dst_ref=gains.at[core],
        send_sem=line_send.at[0],
        recv_sem=line_recv.at[0],
        device_id=across_core,
        device_id_type=MESH,
    )

    def write_slab(place, index):
        taps, bias, shared_taps, shared_bias, gate, per_head = (v[...] for v in params)
        channels = spread.shape[1]
        first = index == 0
        cut = lambda v: jnp.where(first, v[:, :channels], v[:, channels:])
        lane = lax.broadcasted_iota(jnp.int32, per_head.shape, 1)
        here = jnp.where(first, per_head, pltpu.roll(per_head, LANES - heads, 1))
        here = jnp.where(lane < heads, here, 0.0)
        skip = expand(here, spread[...], heads)
        decay = jnp.where(lane < heads, -jnp.exp(here), 0.0)
        place[...] = jnp.zeros(place.shape, F32)
        place[0:CONV, :channels] = cut(taps)
        place[0:CONV, channels:] = shared_taps
        place[CONV : CONV + 1, :channels] = cut(bias)
        place[CONV : CONV + 1, channels:] = shared_bias
        place[5:6, :channels] = cut(gate)
        place[5:6, channels : channels + LANES] = here[0:1]
        place[6:7, :channels] = skip[2:3]
        place[6:7, channels : channels + LANES] = decay[1:2]

    def send_tokens(stage):
        if stage == 0:
            send_first()
        elif stage <= 2:
            for n in range((stage - 1) * micros, stage * micros):
                token_copies(n)[1].wait_recv()
                token_copies(n)[3].start()
            if stage == 1:
                for n in range(micros, 2 * micros):
                    for copy in token_copies(n)[:3]:
                        copy.start()

    def send_first():
        write_slab(other_slab, 1 - core)
        send_slab.start()
        write_slab(slabs.at[core], core)
        gains[core, line] = gain[...]
        for step in range(1, lines):
            send_gain(step).wait()
        send_line.start()
        send_line.wait()
        gain_row = jnp.concatenate(
            [gains[0, f, j : j + 1, :] for f in range(lines) for j in range(gain_rows)], axis=1
        )
        h = own[...].astype(F32)
        scale = lax.rsqrt(jnp.mean(h * h, axis=1, keepdims=True) + EPS)
        rows_out[...] = (h * scale * gain_row).astype(BF16)

        for n in range(micros):
            for copy in token_copies(n)[:3]:
                copy.start()

    gather_steps(shards, wholes, scratch[:13], send_tokens)
    send_slab.wait()
    for n in range(2 * micros):
        own_copy, y_copy, core_copy, core_later = token_copies(n)
        own_copy.wait()
        y_copy.wait_send()
        core_copy.wait()
        core_later.wait()


def start_gather(shards, gain, own, cotangent, params, spread, micros, heads, gain_rows):
    count = len(shards)
    lines = 2 * DEEP
    pairs = pltpu.SemaphoreType.DMA((count, DEEP))
    dma = lambda n: pltpu.SemaphoreType.DMA((n,))
    shape = jax.ShapeDtypeStruct
    anywhere = pl.BlockSpec(memory_space=pl.ANY)
    vmem = pl.BlockSpec(memory_space=pltpu.VMEM)
    rows, width = own.shape
    slab = (8, spread.shape[1] + params[2].shape[1])
    return pl.pallas_call(
        functools.partial(
            start_kernel, count=count, micros=micros, heads=heads, gain_rows=gain_rows
        ),
        out_shape=[shape((lines,) + v.shape, v.dtype) for v in shards]
        + [
            shape((2, lines) + gain.shape, F32),
            shape((2,) + slab, F32),
        ]
        + [shape((2, 2, rows // micros, width), BF16)] * (2 * micros),
        in_specs=[anywhere] * count + [vmem, vmem, anywhere] + [vmem] * 7,
        out_specs=[anywhere] * count + [vmem, vmem] + [anywhere] * (2 * micros),
        scratch_shapes=[dma(count)]
        + [pairs] * 6
        + [dma(count)] * 2
        + [pairs] * 4
        + [dma(lines)] * 2
        + [dma(2 * micros)] * 3
        + [dma(4 * micros)] * 2
        + [pltpu.VMEM(own.shape, BF16), pltpu.VMEM(slab, F32)]
        + [dma(1)] * 4,
        compiler_params=pltpu.CompilerParams(
            collective_id=1, has_side_effects=True, vmem_limit_bytes=VMEM_LIMIT
        ),
        cost_estimate=pl.CostEstimate(flops=170_000_000_000, bytes_accessed=1000, transcendentals=0),
        name="start_gather",
    )(*shards, gain, own, cotangent, *params, spread)


def add_rows(out, *parts):
    rows = out.shape[0]
    step = 16

    def body(n, _):
        at = pl.ds(pl.multiple_of(n * step, step), step)
        total = parts[0][at].astype(F32)
        for part in parts[1:]:
            total = total + part[at].astype(F32)
        out[at] = total.astype(out.dtype)
        return 0

    lax.fori_loop(0, rows // step, body, 0)


X_ORDER = ((3, 2, 1, 0), (3, 0, 2, 1), (0, 3, 1, 2), (0, 1, 2, 3))


def reduce_kernel(*refs, count):
    parts, small, results = refs[:count], refs[count], refs[count + 1 : 2 * count + 1]
    others = refs[2 * count + 1 : 3 * count + 1]
    own_small, next_small, both_small = refs[3 * count + 1 : 3 * count + 4]
    scratch = refs[3 * count + 4 :]
    held, crossed, from_below, from_above, pairs, pairs_below, pairs_above, side_in = (
        scratch[n * count : (n + 1) * count] for n in range(8)
    )
    sems = scratch[8 * count : -5]
    load_sem, x_send, x_recv, up_send, up_recv, down_send, down_recv = sems[:7]
    pair_sem, pair_up_send, pair_up_recv, pair_down_send, pair_down_recv = sems[7:12]
    side_send, side_recv = sems[12:]
    small_buffer, small_send, small_recv, other_send, other_recv = scratch[-5:]
    main = [result.shape[0] - SIDEWAYS for result in results]
    deep, side, device = place_in_line()
    core, line, half = lax.axis_index("section"), lax.axis_index("fsdp"), lax.axis_index("tp")
    greet_all()
    across_core = (1 - core, line, half)
    partners = [
        device(deep, 1 - side),
        device(deep + 1 - 2 * (deep % 2), side),
        device((deep + 2) % DEEP, side),
        (core, line, 1 - half),
        across_core,
        across_core,
    ]

    def swap_small(n, source, target):
        return pltpu.make_async_remote_copy(
            src_ref=source,
            dst_ref=target,
            send_sem=small_send.at[n],
            recv_sem=small_recv.at[n],
            device_id=partners[n],
            device_id_type=MESH,
        )

    def sum_small():
        for n in range(3):
            copy = swap_small(n, small if n == 0 else small_buffer.at[n - 1], small_buffer.at[3 + n])
            if n > 0:
                copy.start()
            copy.wait()
            value = small[...] if n == 0 else small_buffer[n - 1]
            small_buffer[n] = value + small_buffer[3 + n]
        over_tp = swap_small(3, small_buffer.at[2], small_buffer.at[6])
        over_core = swap_small(4, small_buffer.at[2, 1 - core], next_small)
        over_tp.start()
        over_core.start()
        own_small[...] = small_buffer[2, core]
        over_tp.wait()
        small_buffer[7] = small_buffer[2] + small_buffer[6]
        last = swap_small(5, small_buffer.at[7, 1 - core], small_buffer.at[8, 0])
        last.start()
        last.wait()
        both_small[...] = small_buffer[7, core] + small_buffer[8, 0]
        over_core.wait()

    def rows(i, z, x):
        return parts[i].at[z * 2 + x, pl.ds(0, main[i])]

    def load_pair(i, z):
        source = parts[i].at[pl.ds(z * 2, 2), pl.ds(main[i], SIDEWAYS)]
        return pltpu.make_async_copy(source, pairs[i].at[z], pair_sem.at[i, z])

    def pair_along(i, k, z, here, up):
        send, recv = (pair_up_send, pair_up_recv) if up else (pair_down_send, pair_down_recv)
        target = min(here + 1, DEEP - 1) if up else max(here - 1, 0)
        return pltpu.make_async_remote_copy(
            src_ref=pairs[i].at[z],
            dst_ref=(pairs_below if up else pairs_above)[i].at[k - 1],
            send_sem=send.at[i, k - 1],
            recv_sem=recv.at[i, k - 1],
            device_id=device(target, side),
            device_id_type=MESH,
        )

    def sideways(i, here):
        return pltpu.make_async_remote_copy(
            src_ref=pairs[i].at[here, 1 - side],
            dst_ref=side_in[i],
            send_sem=side_send.at[i],
            recv_sem=side_recv.at[i],
            device_id=device(deep, 1 - side),
            device_id_type=MESH,
        )

    def load(i, z):
        return pltpu.make_async_copy(rows(i, z, side), held[i].at[z], load_sem.at[i, z])

    def across(i, z):
        return pltpu.make_async_remote_copy(
            src_ref=rows(i, z, 1 - side),
            dst_ref=crossed[i].at[z],
            send_sem=x_send.at[i, z],
            recv_sem=x_recv.at[i, z],
            device_id=device(deep, 1 - side),
            device_id_type=MESH,
        )

    def upward(i, k, z, here):
        return pltpu.make_async_remote_copy(
            src_ref=held[i].at[z],
            dst_ref=from_below[i].at[k - 1],
            send_sem=up_send.at[i, k - 1],
            recv_sem=up_recv.at[i, k - 1],
            device_id=device(min(here + 1, DEEP - 1), side),
            device_id_type=MESH,
        )

    def downward(i, k, z, here):
        return pltpu.make_async_remote_copy(
            src_ref=held[i].at[z],
            dst_ref=from_above[i].at[k - 1],
            send_sem=down_send.at[i, k - 1],
            recv_sem=down_recv.at[i, k - 1],
            device_id=device(max(here - 1, 0), side),
            device_id_type=MESH,
        )

    def to_other(i):
        return pltpu.make_async_remote_copy(
            src_ref=results[i],
            dst_ref=others[i],
            send_sem=other_send.at[i],
            recv_sem=other_recv.at[i],
            device_id=across_core,
            device_id_type=MESH,
        )

    def at_depth(here):
        order = X_ORDER[here]
        last = DEEP - 1
        started = []

        def send_across(number):
            for i in range(count):
                across(i, order[number]).start()

        def take(number):
            z = order[number]
            for i in range(count):
                across(i, z).wait_recv()
            if number + 2 < DEEP:
                send_across(number + 2)
            for i in range(count):
                load(i, z).wait()
                add_rows(held[i].at[z], held[i].at[z], crossed[i].at[z])

        def relay(k, up):
            z = DEEP - k + here if up else here + k - DEEP
            first = here == 0 if up else here == last
            for i in range(count):
                if not first:
                    make = upward if up else downward
                    back = from_below if up else from_above
                    make(i, k - 1, z, here).wait_recv()
                    add_rows(held[i].at[z], held[i].at[z], back[i].at[k - 2])
                copy = (upward if up else downward)(i, k, z, here)
                copy.start()
                started.append(copy)

        swap_small(0, small, small_buffer.at[3]).start()
        send_across(0)
        send_across(1)
        for number in range(DEEP):
            for i in range(count):
                load_pair(i, order[number]).start()
        for number in range(DEEP):
            for i in range(count):
                load(i, order[number]).start()

        def relay_pair(k, up):
            z = DEEP - k + here if up else here + k - DEEP
            if not 0 <= z < DEEP or z == here or (z < here) == up:
                return
            for i in range(count):
                load_pair(i, z).wait()
                if here != (0 if up else last):
                    pair_along(i, k - 1, z, here, up).wait_recv()
                    back = (pairs_below if up else pairs_above)[i]
                    for x in range(2):
                        add_rows(pairs[i].at[z, x], pairs[i].at[z, x], back.at[k - 2, x])
                copy = pair_along(i, k, z, here, up)
                copy.start()
                started.append(copy)

        for k in range(1, DEEP):
            relay_pair(k, True)
            relay_pair(k, False)
        sum_small()
        for i in range(count):
            load_pair(i, here).wait()
            for x in range(2):
                terms = [pairs[i].at[here, x]]
                if here > 0:
                    if x == 0:
                        pair_along(i, DEEP - 1, here, here, True).wait_recv()
                    terms.append(pairs_below[i].at[DEEP - 2, x])
                if here < last:
                    if x == 0:
                        pair_along(i, DEEP - 1, here, here, False).wait_recv()
                    terms.append(pairs_above[i].at[DEEP - 2, x])
                add_rows(pairs[i].at[here, x], *terms)
            sideways(i, here).start()
        if here in (0, last):
            up = here == 0
            for k in range(1, DEEP):
                take(k - 1)
                relay(k, up)
            take(DEEP - 1)
        else:
            up = here == 1
            take(0)
            take(1)
            relay(2, up)
            relay(3, not up)
            take(2)
            relay(3, up)
            take(3)
        for i in range(count):
            terms = [held[i].at[here]]
            if here > 0:
                upward(i, DEEP - 1, here, here).wait_recv()
                terms.append(from_below[i].at[DEEP - 2])
            if here < last:
                downward(i, DEEP - 1, here, here).wait_recv()
                terms.append(from_above[i].at[DEEP - 2])
            add_rows(results[i].at[pl.ds(0, main[i])], *terms)
            sideways(i, here).wait_recv()
            add_rows(
                results[i].at[pl.ds(main[i], SIDEWAYS)], pairs[i].at[here, side], side_in[i]
            )
            to_other(i).start()
        for i in range(count):
            to_other(i).wait()
            sideways(i, here).wait_send()
        for copy in started:
            copy.wait_send()
        for z in range(DEEP):
            for i in range(count):
                across(i, z).wait_send()

    for here in range(DEEP):

        @pl.when(deep == here)
        def _(here=here):
            at_depth(here)


def reduce_line(parts, small, name, collective_id):
    count = len(parts)
    shards = [(p.shape[0] // (2 * DEEP),) + p.shape[1:] for p in parts]
    pairs = pltpu.SemaphoreType.DMA((count, DEEP))
    sizes = sum(p.size for p in parts)
    blocks = lambda n: [pltpu.VMEM((n, shard[0] - SIDEWAYS, shard[1]), BF16) for shard in shards]
    doubles = lambda n: [pltpu.VMEM((n, 2, SIDEWAYS, shard[1]), BF16) for shard in shards]
    split_parts = [p.reshape((2 * DEEP, -1) + p.shape[1:]) for p in parts]
    shape = jax.ShapeDtypeStruct
    vmem = pl.BlockSpec(memory_space=pltpu.VMEM)
    return pl.pallas_call(
        functools.partial(reduce_kernel, count=count),
        out_shape=[shape(shard, F32) for shard in shards] * 2 + [shape(small.shape[1:], F32)] * 3,
        in_specs=[pl.BlockSpec(memory_space=pl.ANY)] * count + [vmem],
        out_specs=[vmem] * (2 * count + 3),
        scratch_shapes=blocks(DEEP)
        + blocks(DEEP)
        + blocks(DEEP - 1)
        + blocks(DEEP - 1)
        + doubles(DEEP)
        + doubles(DEEP - 1)
        + doubles(DEEP - 1)
        + [pltpu.VMEM((SIDEWAYS, shard[1]), BF16) for shard in shards]
        + [pairs] * 12
        + [pltpu.SemaphoreType.DMA((count,))] * 2
        + [
            pltpu.VMEM((9,) + small.shape, F32),
            pltpu.SemaphoreType.DMA((6,)),
            pltpu.SemaphoreType.DMA((6,)),
            pltpu.SemaphoreType.DMA((count,)),
            pltpu.SemaphoreType.DMA((count,)),
        ],
        compiler_params=pltpu.CompilerParams(
            collective_id=collective_id, has_side_effects=True, vmem_limit_bytes=VMEM_LIMIT
        ),
        cost_estimate=pl.CostEstimate(flops=1000, bytes_accessed=1000, transcendentals=0),
        name=name,
    )(*split_parts, small)


SWAP = [(0, 1), (1, 0)]


def swap_core(value):
    return lax.ppermute(value, "section", SWAP)


def swap_tp(value):
    return lax.ppermute(value, "tp", SWAP)


def by_index(index, own, other):
    first = index == 0
    return jnp.stack([jnp.where(first, own, other), jnp.where(first, other, own)])


def pick(pair, index):
    return lax.dynamic_index_in_dim(pair, index, 0, keepdims=False)


def gather_tokens(own, core, half, beside=()):
    both = by_index(half, own, after(swap_tp(own), *beside))
    whole = by_index(core, both, swap_core(both))
    whole = jnp.moveaxis(whole, 0, 1)
    return whole.reshape((4 * own.shape[0],) + own.shape[1:])


def after(value, *others):
    return lax.optimization_barrier((value,) + others)[0] if others else value


def over_cores(part, core, *beside):
    split_rows = part.reshape((2, 2, part.shape[0] // 4) + part.shape[1:])
    mine = lax.dynamic_index_in_dim(split_rows, core, 1, keepdims=False)
    theirs = lax.dynamic_index_in_dim(split_rows, 1 - core, 1, keepdims=False)
    return mine.astype(F32) + after(swap_core(theirs), *beside).astype(F32)


class Sum:
    def __init__(self, part, core, half, needed=(), beside=()):
        self.half = half
        self.total = over_cores(part, core, *beside)
        sent = after(pick(self.total, 1 - half), *needed)
        self.sent = sent.astype(BF16) if part.ndim > 1 else sent

    def done(self, *beside):
        return pick(self.total, self.half) + after(swap_tp(self.sent), *beside).astype(F32)


def local(
    inputs,
    cotangent,
    norm_gain,
    w_zx,
    w_bc,
    w_dt,
    conv_x,
    conv_xb,
    conv_bc,
    conv_bcb,
    dt_bias,
    a_log,
    d_skip,
    gate_gain,
    w_out,
):
    cores = lax.axis_size("section")
    core = lax.axis_index("section")
    half = lax.axis_index("tp")
    micros = inputs.shape[1]
    rows = inputs.shape[2] // cores
    channels = w_zx.shape[3] // cores
    heads = w_dt.shape[2] // cores
    width = channels // heads
    shared = w_bc.shape[2]
    depth = w_zx.shape[1]
    in_width = 2 * channels + shared + LANES
    def cut(tensor, index, size):
        return lax.dynamic_slice_in_dim(tensor, index * size, size, tensor.ndim - 1)

    def weight_shard(index):
        zx = cut(w_zx[0], index, channels).reshape(depth, 2 * channels)
        steps = jnp.pad(cut(w_dt[0], index, heads), ((0, 0), (0, LANES - heads)))
        return jnp.concatenate([zx, w_bc[0], steps, cut(w_out[0], index, channels)], axis=1)

    def slab_of(index):
        pad = jnp.zeros((LANES - heads,), F32)
        steps = jnp.concatenate([cut(dt_bias[0], index, heads), pad])
        decay = jnp.concatenate([-jnp.exp(cut(a_log[0], index, heads)), pad])
        skip = jnp.repeat(cut(d_skip[0], index, heads), width)
        rest = jnp.zeros((shared - LANES,), F32)
        taps = jnp.concatenate([cut(conv_x[0], index, channels), conv_bc[0]], axis=1)
        bias = jnp.concatenate([cut(conv_xb[0], index, channels), conv_bcb[0]])
        return jnp.concatenate(
            [
                taps,
                bias[None],
                jnp.concatenate([cut(gate_gain[0], index, channels), steps, rest])[None],
                jnp.concatenate([skip, decay, rest])[None],
                jnp.zeros((1, channels + shared), F32),
            ]
        )

    lane = np.arange(LANES)
    head_of = np.arange(channels) // width
    spread = (lane[:, None] % heads == head_of[None, :]) & (lane[:, None] < 2 * heads)
    spread = jnp.asarray(spread.astype(np.float32), BF16)
    gather = jnp.asarray((head_of[:, None] == lane[None, :]).astype(np.float32), BF16)

    own_shard = weight_shard(core)
    got_shard = swap_core(weight_shard(1 - core))
    in_line = lax.axis_size("fsdp") == 2 * DEEP and lax.axis_size("tp") == 2
    over_fsdp = functools.partial(lax.all_gather, axis_name="fsdp", tiled=True)
    shards = []
    for layer in range(2):
        shard = jnp.where(core == layer, own_shard, got_shard)
        shards.append((shard[:, :in_width], shard[:, in_width:]))

    def own_rows(tensor):
        return [
            lax.dynamic_slice_in_dim(tensor[0, m], core * rows, rows, 0) for m in range(micros)
        ]

    first, cotangents = own_rows(inputs), own_rows(cotangent)
    if in_line:
        gain_rows = depth // LANES
        packed = jnp.pad(norm_gain.astype(F32).reshape(-1, LANES), ((0, 8 - gain_rows), (0, 0)))
        per_head = jnp.concatenate([dt_bias, a_log, d_skip])
        per_head = jnp.pad(per_head, ((0, 5), (0, LANES - per_head.shape[1])))
        params = (conv_x[0], conv_xb, conv_bc[0], conv_bcb, gate_gain, per_head)
        second_gate, second_rest = shards[1][0][:, :channels], shards[1][0][:, channels:]
        w_in, w_back, second_rest, gains, slabs, *tokens = start_gather(
            shards[0] + (second_rest,),
            packed,
            jnp.concatenate(first),
            jnp.concatenate(cotangents),
            params,
            spread,
            micros,
            heads,
            gain_rows,
        )
        slabs = [slabs[0], slabs[1]]
        w_in, w_back, second_rest = (v.reshape(-1, v.shape[2]) for v in (w_in, w_back, second_rest))
        projections = [(w_in, w_back)]
        second = (over_fsdp(after(second_gate, gains), axis=0), second_rest)
        projections.append((second, over_fsdp(after(shards[1][1], gains), axis=0)))
        gains = gains[:, :, :gain_rows].reshape(2, -1)
        tokens = [v.reshape(4 * rows, -1) for v in tokens]
        first_normed, everyones = tokens[:micros], tokens[micros:]
    else:
        own_slab, got_slab = slab_of(core), swap_core(slab_of(1 - core))
        slabs = [jnp.where(core == layer, own_slab, got_slab) for layer in range(2)]
        gain_pair = by_index(core, norm_gain[0], swap_core(norm_gain[0])).astype(F32)
        projections = [tuple(over_fsdp(v, axis=0) for v in shards[0])]
        gains = over_fsdp(gain_pair.astype(BF16), axis=1).astype(F32)
        first_normed = None
        everyones = [gather_tokens(v, core, half) for v in cotangents]
    if not in_line:
        projections.append(tuple(over_fsdp(v, axis=0) for v in shards[1]))

    size = channels + shared
    zero_state = jnp.zeros((shared // 2, channels), F32)
    zero_halo = jnp.zeros((HALO, size), F32)
    last = micros - 1

    def scale_of(h):
        return lax.rsqrt(jnp.mean(h * h, axis=1, keepdims=True) + EPS)

    def norm(h, layer):
        return (h * scale_of(h) * gains[layer][None]).astype(BF16)

    hidden = [v.astype(F32) for v in first]
    normed = [None] * micros
    for m in range(micros):
        normed[m] = (
            first_normed[m] if in_line else gather_tokens(norm(hidden[m], 0), core, half)
        )

    hiddens, normeds, kept = [hidden, None], [normed, None], [[None] * micros for _ in range(2)]
    waiting = None

    def finish(pending, *beside):
        m, part, squares = pending
        r = lax.rsqrt(squares.done(*beside) / DI + EPS)[:, None]
        branch = r * part.done(*beside)
        kept[0][m].update(r=r, branch=branch)
        h = hiddens[0][m] + branch
        hiddens[1][m] = h
        return norm(h, 1)

    def spread_out(pending, own, *beside):
        normeds[1][pending[0]] = gather_tokens(own, core, half, beside)

    hiddens[1], normeds[1] = [None] * micros, [None] * micros
    for layer in range(2):
        w_in, w_back = projections[layer]
        state, tail = zero_state, zero_halo
        for m in range(micros):
            tokens = normeds[layer][m]
            if layer == 0 or not in_line:
                w_pair = (w_in[:, :channels], w_in[:, channels:])
            else:
                w_pair = w_in
            if waiting is not None and layer == 1:
                tokens = after(tokens, waiting[1].sent, waiting[2].sent)
            rest = dot_nn(tokens, w_pair[1])
            gate = dot_nn(tokens, w_pair[0])
            mixed_rest = rest
            if waiting is not None and layer == 1:
                own = finish(waiting, rest)
                gate = after(gate, own)
            elif waiting is not None:
                mixed_rest = after(rest, waiting[1].sent, waiting[2].sent)
            u, squares, y, entering, state_out = mixer_forward(
                gate, mixed_rest, tail, state, slabs[layer], spread, heads
            )
            if waiting is not None:
                spread_out(waiting, own if layer == 1 else finish(waiting, u), u)
            kept[layer][m] = dict(
                gate=gate, rest=rest, tail=tail, u=u, y=y, entering=entering, squares=squares
            )
            state, tail = state_out, rest[-HALO:, :size]
            waiting = None
            if layer == 0:
                part = Sum(dot_nt(u, w_back).astype(BF16), core, half)
                waiting = (m, part, Sum(squares[:, 0], core, half))

    over_tokens = (((0,), (0,)), ((), ()))

    def weight_grad(left, right):
        return lax.dot_general(
            jnp.concatenate(left), jnp.concatenate(right), over_tokens, preferred_element_type=F32
        ).astype(BF16)

    reduced, small = [None, None], [None, None]
    grads = [v.astype(F32) for v in cotangents]
    mixers_done = [kept[1][m]["u"] for m in range(micros)]
    w_in, w_back = projections[1]
    if in_line:
        w_in = jnp.concatenate([after(v, *mixers_done) for v in w_in], axis=1)
    w_back = after(w_back, w_in, *mixers_done)
    projections[1] = (w_in, w_back)
    backs, products, factors = list(everyones), [None] * micros, [None] * micros
    pairs = [None] * micros
    for m in reversed(range(micros)):
        k = kept[1][m]
        products[m] = dot_nn(backs[m], w_back)
        dots = jnp.sum(products[m] * k["u"].astype(F32), axis=1)
        pairs[m] = jnp.stack([k["squares"][:, 0], dots])
    pair = jnp.stack(pairs)
    pair = pair + swap_core(pair)
    pair = pair + swap_tp(pair)
    r = lax.rsqrt(pair[:, 0] / DI + EPS)
    factors = [jnp.stack([r[m], r[m] * r[m] * r[m] * pair[m, 1] / DI], axis=1) for m in range(micros)]
    gain_parts = [[], []]

    def finish_back(pending, *beside):
        layer, m, part = pending
        h = hiddens[layer][m]
        scale = scale_of(h)
        g_norm = part.done(*beside)
        gain_parts[layer].append(jnp.sum(g_norm * (h * scale), axis=0))
        g_norm = g_norm * gains[layer][None]
        mean = jnp.mean(g_norm * h, axis=1, keepdims=True)
        g = grads[m] + scale * g_norm - h * (scale * scale * scale) * mean
        grads[m] = g
        if layer == 0:
            return (g,)
        r, branch = kept[0][m]["r"], kept[0][m]["branch"]
        kappa = r * r * jnp.sum(g * branch, axis=1)[:, None] / DI
        return g.astype(BF16), jnp.concatenate([r, kappa], axis=1)

    def spread_back(pending, own, *beside):
        layer, m = pending[:2]
        if layer == 1:
            next_backs[m] = gather_tokens(own[0], core, half, beside)
            next_factors[m] = gather_tokens(own[1], core, half, beside)

    def reduce_rows(part):
        return lax.psum_scatter(part, "fsdp", scatter_dimension=0, tiled=True)

    def small_of(layer, totals):
        gain_rows = sum(gain_parts[layer]).reshape(2, -1)
        return jnp.concatenate(
            [totals[:6], jnp.concatenate([gain_rows, totals[6:, channels:]], axis=1)]
        )

    waiting, outs = None, [None] * micros
    next_backs, next_factors = [None] * micros, [None] * micros
    for layer in (1, 0):
        w_in, w_back = projections[layer]
        state, e_rows = zero_state, zero_halo
        totals = jnp.zeros(slabs[0].shape, F32)
        gpres = [None] * micros
        for m in reversed(range(micros)):
            k = kept[layer][m]
            q = products[m] if layer == 1 else dot_nn(backs[m], w_back)
            if m == last and layer == 1:
                mixed = [
                    (kept[1][j]["u"].astype(F32) * factors[j][:, :1]).astype(BF16)
                    for j in range(micros)
                ]
                reduced_back = weight_grad(backs, mixed)
                q = after(q, reduced_back)
                reduced_back = reduce_rows(reduced_back)
            if waiting is not None:
                q = after(q, waiting[2].sent)
            gpre, state, e_rows, sums = mixer_backward(
                q,
                factors[m],
                k["gate"],
                k["rest"],
                k["tail"],
                k["y"],
                k["entering"],
                state,
                e_rows,
                slabs[layer],
                spread,
                gather,
                heads,
                VMEM_LIMIT if layer == 1 and m == last else BACK_VMEM,
            )
            totals = totals + sums
            gpres[m] = gpre
            ready = gpre
            if waiting is not None:
                own = finish_back(waiting, gpre)
                ready = after(gpre, *own)
            if layer == 1 and m == 0:
                grad_in = weight_grad(normeds[1], gpres)
                ready = after(ready, grad_in)
            part = dot_nt(ready, w_in).astype(BF16)
            if waiting is not None:
                spread_back(waiting, own, part)
                if layer == 0 and waiting[0] == 1:
                    backs[0], factors[0] = next_backs[0], next_factors[0]
                    small[1] = small_of(1, above)
            beside = ()
            if layer == 1:
                outs[m] = dot_nt(after(k["u"], part), w_back).astype(BF16)
                beside = (outs[m],)
            waiting = (layer, m, Sum(part, core, half, (), beside))
            if layer == 0 and m == last:
                outs = [Sum(out, core, half, (waiting[2].sent,)) for out in outs]
        if layer == 0:
            grad_in = weight_grad(normeds[0], [after(v, waiting[2].sent) for v in gpres])
        if layer == 1 or not in_line:
            reduced[layer] = (reduce_rows(grad_in), reduced_back)
        if layer == 0:
            mixed = [
                (kept[0][j]["u"].astype(F32) * factors[j][:, :1]).astype(BF16) for j in range(micros)
            ]
            grad_back = weight_grad(backs, mixed)
            if not in_line:
                reduced[0] = (reduced[0][0], reduce_rows(grad_back))
        if layer == 1:
            second_factors, above = factors, totals
            backs, factors = list(next_backs), list(next_factors)
    finish_back(waiting, grad_in)
    small[0] = small_of(0, totals)

    outputs_rows = []
    for m in range(micros):
        r = lax.dynamic_slice_in_dim(second_factors[m], (2 * half + core) * rows, rows, 0)[:, :1]
        outputs_rows.append(hiddens[1][m] + r * outs[m].done(gpres[0]))

    def placed_rows(parts):
        own = jnp.where(core == 0, parts[0], parts[1])
        other = jnp.where(core == 0, parts[1], parts[0])
        return by_index(core, own, swap_core(other)).reshape(1, 1, 2 * rows, -1)

    outputs, input_grads = placed_rows(outputs_rows), placed_rows(grads)

    small_sums = after(jnp.stack(small), outputs, input_grads)
    if in_line:
        *both_parts, own_small, next_small, both_small = reduce_line(
            [grad_in, grad_back], small_sums, "grads_reduce", 2
        )
        first_own, first_other = both_parts[:2], both_parts[2:]
    else:
        small_sums = lax.psum(small_sums, "fsdp")
        own_small = pick(small_sums, core)
        next_small = swap_core(pick(small_sums, 1 - core))
        both_small = own_small + next_small
        both_small = both_small + swap_tp(both_small)
        first_own, first_other = reduced[0], [swap_core(v) for v in reduced[0]]
    low_small = jnp.where(core == 0, own_small, next_small)
    high_small = jnp.where(core == 0, next_small, own_small)
    wide = jnp.concatenate([low_small[:6, :channels], high_small[:6, :channels]], axis=1)
    narrow = jnp.concatenate(
        [v[5:, channels : channels + heads] for v in (low_small, high_small)], axis=1
    )
    conv_sum = both_small[:5, channels:]
    gain_sum = lax.dynamic_slice_in_dim(
        both_small[6:8, :channels].reshape(-1), lax.axis_index("fsdp") * depth, depth, 0
    )

    second_own = [after(v, own_small) for v in reduced[1]]
    second_other = [swap_core(v) for v in second_own]
    either = lambda one, two: jnp.where(core == 0, one.astype(F32), two.astype(F32))
    low_half = [either(first_own[i], second_other[i]) for i in range(2)]
    high_half = [either(first_other[i], second_own[i]) for i in range(2)]

    def joined(begin, end, i=0):
        return jnp.concatenate([low_half[i][:, begin:end], high_half[i][:, begin:end]], axis=1)

    g_zx = join_halves(first_own[0], first_other[0], second_own[0], second_other[0], channels)
    at = 2 * channels
    g_bc = low_half[0][:, at : at + shared] + high_half[0][:, at : at + shared]
    g_bc = g_bc + swap_tp(g_bc)
    g_dt = joined(at + shared, at + shared + heads)
    g_back = joined(0, channels, 1)

    return (
        outputs,
        input_grads,
        gain_sum[None],
        g_zx[None],
        g_bc[None],
        g_dt[None],
        wide[:4][None],
        wide[4][None],
        conv_sum[:4][None],
        conv_sum[4][None],
        narrow[0][None],
        narrow[1][None],
        narrow[2][None],
        wide[5][None],
        g_back[None],
    )


def solution(mesh):
    placed = (
        P("fsdp", None, "tp", None),
        P("fsdp", None, "tp", None),
        P("section", "fsdp"),
        P("section", "fsdp", None, "tp"),
        P("section", "fsdp", None),
        P("section", "fsdp", "tp"),
        P("section", None, "tp"),
        P("section", "tp"),
        P("section", None, None),
        P("section", None),
        P("section", "tp"),
        P("section", "tp"),
        P("section", "tp"),
        P("section", "tp"),
        P("section", "fsdp", "tp"),
    )
    return jax.shard_map(
        local,
        mesh=mesh,
        in_specs=placed,
        out_specs=(
            P("fsdp", "section", "tp", None),
            P("fsdp", "section", "tp", None),
        )
        + placed[2:],
        check_vma=False,
    )
```

```python
import functools

import jax
import jax.numpy as jnp
import numpy as np
from jax import lax
from jax.experimental import pallas as pl
from jax.experimental.pallas import tpu as pltpu
from jax.sharding import PartitionSpec as P

CONV = 4
DI = 4096
EPS = 1e-05
CHUNK = 128
LANES = 128
HALO = 8
NEG = -10000.0
F32 = jnp.float32
BF16 = jnp.bfloat16
VMEM_LIMIT = 56 * 1024 * 1024
MIXER_VMEM = 24 * 1024 * 1024
BACK_VMEM = 40 * 1024 * 1024


def sigmoid(v):
    return 0.5 * jnp.tanh(0.5 * v) + 0.5


def dot_nn(a, b):
    return lax.dot_general(a, b, (((1,), (0,)), ((), ())), preferred_element_type=F32)


def dot_nt(a, b):
    return lax.dot_general(a, b, (((1,), (1,)), ((), ())), preferred_element_type=F32)


def dot_sums(ones, columns, heads):
    high = columns.astype(BF16).astype(F32)
    middle = (columns - high).astype(BF16).astype(F32)
    low = columns - high - middle
    packed = high + pltpu.roll(middle, heads, 1) + pltpu.roll(low, 2 * heads, 1)
    sums = dot_nn(ones.astype(BF16), packed.astype(BF16))
    return sums + pltpu.roll(sums, LANES - heads, 1) + pltpu.roll(sums, LANES - 2 * heads, 1)


def split(a):
    high = a.astype(BF16)
    return high, (a - high.astype(F32)).astype(BF16)


def dot3(a, b, dot=dot_nn):
    return dot(a[0], b[0]) + (dot(a[1], b[0]) + dot(a[0], b[1]))


def tri(shape, keep):
    rows = lax.broadcasted_iota(jnp.int32, shape, 0)
    cols = lax.broadcasted_iota(jnp.int32, shape, 1)
    return keep(rows, cols)


def expand(columns, spread, heads):
    high = columns.astype(BF16).astype(F32)
    rest = columns - high
    packed = high + pltpu.roll(rest, heads, 1)
    return dot_nn(packed.astype(BF16), spread)


def step_terms(pre_dt, slab, channels, heads, spread):
    lane = lax.broadcasted_iota(jnp.int32, pre_dt.shape, 1)
    live = lane < heads
    arg = pre_dt + slab[5:6, channels : channels + LANES]
    dt = jnp.where(live, jnp.maximum(arg, 0.0) + jnp.log1p(jnp.exp(-jnp.abs(arg))), 0.0)
    decay = slab[6:7, channels : channels + LANES]
    lower = tri((CHUNK, CHUNK), lambda r, c: r >= c).astype(F32)
    cum = dot_sums(lower, dt * decay, heads)
    last = cum[CHUNK - 1 : CHUNK, :]
    grown = jnp.where(live, jnp.exp(cum), 0.0)
    left = jnp.where(live, jnp.exp(last - cum), 0.0)
    wide = expand(jnp.concatenate([dt, grown, left], axis=0), spread, heads)
    return arg, dt, decay, cum, wide[:CHUNK], wide[CHUNK : 2 * CHUNK], wide[2 * CHUNK :]


def conv_rows(buffer, slab):
    out = slab[4:5, :] + slab[CONV - 1 : CONV, :] * buffer[HALO : HALO + CHUNK, :]
    for k in range(CONV - 1):
        first = HALO - (CONV - 1) + k
        out = out + slab[k : k + 1, :] * buffer[first : first + CHUNK, :]
    return out


def forward_kernel(
    gate, rest, tail, start, slab, spread, u, sq, y, entering, leaving, state, buffer, *, channels, heads
):
    step = pl.program_id(0)
    size = channels + 2 * LANES

    @pl.when(step == 0)
    def _():
        state[...] = start[...]
        buffer[0:HALO, :] = tail[...]

    @pl.when(step > 0)
    def _():
        buffer[0:HALO, :] = buffer[CHUNK : CHUNK + HALO, :]

    buffer[HALO:, :] = rest[:, :size]
    entering[0] = state[...]
    conv = conv_rows(buffer, slab)
    act = conv * sigmoid(conv)
    xs = act[:, :channels]
    in_map = act[:, channels : channels + LANES]
    out_map = act[:, channels + LANES :]
    arg, dt, decay, cum, dt_w, grown_w, left_w = step_terms(
        rest[:, size:], slab, channels, heads, spread[...]
    )
    cum_t = cum.T
    xt = xs * dt_w
    xt_s = split(xt)
    out_s = split(out_map)
    scores = dot3(out_s, split(in_map), dot_nt)
    held = state[...]
    base = grown_w * dot3(out_s, split(held)) + slab[6:7, :channels] * xs
    state[...] = held * grown_w[CHUNK - 1 : CHUNK, :] + dot3(
        split(in_map.T), split(xt * left_w)
    )
    causal = tri((CHUNK, CHUNK), lambda r, c: r >= c)
    first_half = lax.broadcasted_iota(jnp.int32, (CHUNK, LANES), 1) < LANES // 2
    zero = jnp.zeros((CHUNK, LANES), BF16)
    for pair in range(channels // LANES):
        cols = slice(pair * LANES, (pair + 1) * LANES)
        mats = []
        for h in (2 * pair, 2 * pair + 1):
            gap = cum[:, h : h + 1] - cum_t[h : h + 1, :]
            mats.append(scores * jnp.exp(jnp.where(causal, gap, NEG)))
        stacked = tuple(
            jnp.concatenate(
                [jnp.where(first_half, xp[:, cols], zero), jnp.where(first_half, zero, xp[:, cols])],
                axis=0,
            )
            for xp in xt_s
        )
        y[:, cols] = base[:, cols] + dot3(split(jnp.concatenate(mats, axis=1)), stacked)
    z = gate[...]
    gated = y[...] * (z * sigmoid(z))
    sq[...] = jnp.sum(gated * gated, axis=1, keepdims=True)
    u[...] = (gated * slab[5:6, :channels]).astype(BF16)

    @pl.when(step == pl.num_programs(0) - 1)
    def _():
        leaving[...] = state[...]


def backward_kernel(
    q,
    factor,
    gate,
    rest,
    before,
    tail,
    y,
    entering,
    grad_start,
    e_start,
    slab,
    spread,
    gather,
    gpre,
    grad_leaving,
    e_leaving,
    sums,
    grad,
    buffer,
    e_buffer,
    *,
    channels,
    heads,
):
    step = pl.program_id(0)
    steps = pl.num_programs(0)
    size = channels + 2 * LANES

    @pl.when(step == 0)
    def _():
        grad[...] = grad_start[...]
        e_buffer[CHUNK:, :] = e_start[...]
        sums[...] = jnp.zeros_like(sums)

    @pl.when(step > 0)
    def _():
        e_buffer[CHUNK:, :] = e_buffer[0:HALO, :]

    @pl.when(step == steps - 1)
    def _():
        buffer[0:HALO, :] = tail[...]

    @pl.when(step < steps - 1)
    def _():
        buffer[0:HALO, :] = before[:, :size]

    buffer[HALO:, :] = rest[:, :size]
    conv = conv_rows(buffer, slab)
    sig = sigmoid(conv)
    act = conv * sig
    d_act = sig * (1.0 + conv * (1.0 - sig))
    xs = act[:, :channels]
    in_map = act[:, channels : channels + LANES]
    out_map = act[:, channels + LANES :]
    arg, dt, decay, cum, dt_w, grown_w, left_w = step_terms(
        rest[:, size:], slab, channels, heads, spread[...]
    )
    cum_t = cum.T

    z = gate[...]
    sig_z = sigmoid(z)
    silu_z = z * sig_z
    yv = y[...]
    gated = yv * silu_z
    qv = q[...] * factor[:, 0:1]
    sums[5:6, :channels] += jnp.sum(qv * gated, axis=0, keepdims=True)
    g_gated = qv * slab[5:6, :channels] - gated * factor[:, 1:2]
    gpre[:, :channels] = (g_gated * yv * (sig_z * (1.0 + z * (1.0 - sig_z)))).astype(BF16)
    gy = g_gated * silu_z
    gy_b = gy.astype(BF16)
    skip_row = jnp.sum(gy * xs, axis=0, keepdims=True)

    xt = xs * dt_w
    xt_b = xt.astype(BF16)
    in_b = in_map.astype(BF16)
    out_b = out_map.astype(BF16)
    held = entering[0]
    held_b = held.astype(BF16)
    g_state = grad[...]
    g_state_b = g_state.astype(BF16)
    grown_last = grown_w[CHUNK - 1 : CHUNK, :]

    from_state = grown_w * dot_nn(out_b, held_b)
    ge_b = (grown_w * gy).astype(BF16)
    g_out_map = dot_nt(ge_b, held_b)
    g_xt = left_w * dot_nn(in_b, g_state_b)
    g_in_map = dot_nt((xt * left_w).astype(BF16), g_state_b)
    through = jnp.sum(g_state * held, axis=0, keepdims=True) * grown_last
    grad[...] = g_state * grown_last + dot_nn(out_map.T.astype(BF16), ge_b)
    row_terms = gy * from_state
    col_terms = xt * g_xt

    scores_t = dot3(split(in_map), split(out_map), dot_nt)
    later = tri((CHUNK, CHUNK), lambda r, c: c >= r)
    first_half = lax.broadcasted_iota(jnp.int32, (CHUNK, LANES), 1) < LANES // 2
    lane = lax.broadcasted_iota(jnp.int32, (CHUNK, LANES), 1)
    zero = jnp.zeros((CHUNK, LANES), BF16)
    g_scores_t = jnp.zeros((CHUNK, CHUNK), F32)
    gap_rows = []
    gap_cols = jnp.zeros((CHUNK, LANES), F32)
    g_xt_parts = []
    for pair in range(channels // LANES):
        cols = slice(pair * LANES, (pair + 1) * LANES)
        gp = gy_b[:, cols]
        stacked = jnp.concatenate(
            [jnp.where(first_half, gp, zero), jnp.where(first_half, zero, gp)], axis=0
        )
        g_mats = dot_nt(xt_b[:, cols], stacked)
        mats = []
        for number in range(2):
            h = 2 * pair + number
            gap = cum_t[h : h + 1, :] - cum[:, h : h + 1]
            weight = jnp.exp(jnp.where(later, gap, NEG))
            mats.append((scores_t * weight).astype(BF16))
            g_score = g_mats[:, number * CHUNK : (number + 1) * CHUNK] * weight
            g_scores_t = g_scores_t + g_score
            g_gap = g_score * scores_t
            gap_rows.append(jnp.sum(g_gap, axis=0, keepdims=True))
            gap_cols = jnp.where(lane == h, jnp.sum(g_gap, axis=1, keepdims=True), gap_cols)
        g_xt_parts.append(g_xt[:, cols] + dot_nn(jnp.concatenate(mats, axis=1), stacked))
    g_xt = jnp.concatenate(g_xt_parts, axis=1)
    g_scores_b = g_scores_t.astype(BF16)
    g_in_map = g_in_map + dot_nn(g_scores_b, out_b)
    g_out_map = g_out_map + dot_nn(g_scores_t.T.astype(BF16), in_b)
    g_xs = slab[6:7, :channels] * gy + dt_w * g_xt

    pad = jnp.zeros((CHUNK - heads, CHUNK), F32)
    gap_rows_t = jnp.concatenate(gap_rows + [pad], axis=0).T
    packed = jnp.concatenate(
        [
            xs * g_xt,
            row_terms,
            col_terms,
            jnp.broadcast_to(through, (HALO, channels)),
            jnp.broadcast_to(skip_row, (HALO, channels)),
        ],
        axis=0,
    )
    high, rest = split(packed)
    grouped = dot_nn(high, gather[...]) + dot_nn(rest, gather[...])
    direct = grouped[:CHUNK]
    row_sum = grouped[CHUNK : 2 * CHUNK]
    col_sum = grouped[2 * CHUNK : 3 * CHUNK]
    through_sum = grouped[3 * CHUNK : 3 * CHUNK + 1]
    sums[7:8, channels : channels + LANES] += grouped[3 * CHUNK + HALO : 3 * CHUNK + HALO + 1]
    upper = tri((CHUNK, CHUNK), lambda r, c: c >= r).astype(F32)
    below = tri((CHUNK, CHUNK), lambda r, c: r > c).astype(F32)
    g_log = (
        dot_sums(upper, gap_rows_t - gap_cols + row_sum, heads)
        + dot_sums(below, col_sum, heads)
        + through_sum
    )
    g_dt = direct + g_log * decay
    g_dtin = jnp.where(lane < heads, g_dt * sigmoid(arg), 0.0)
    sums[5:6, channels : channels + LANES] += jnp.sum(g_dtin, axis=0, keepdims=True)
    sums[6:7, channels : channels + LANES] += decay * jnp.sum(dt * g_log, axis=0, keepdims=True)

    e = jnp.concatenate([g_xs, g_in_map, g_out_map], axis=1) * d_act
    e_buffer[0:CHUNK, :] = e
    sums[4:5, :] += jnp.sum(e, axis=0, keepdims=True)
    for k in range(CONV):
        first = HALO - (CONV - 1) + k
        sums[k : k + 1, :] += jnp.sum(e * buffer[first : first + CHUNK, :], axis=0, keepdims=True)
    g_pre = slab[CONV - 1 : CONV, :] * e
    for k in range(CONV - 1):
        first = CONV - 1 - k
        g_pre = g_pre + slab[k : k + 1, :] * e_buffer[first : first + CHUNK, :]
    gpre[:, channels : channels + size] = g_pre.astype(BF16)
    gpre[:, channels + size :] = g_dtin.astype(BF16)

    @pl.when(step == steps - 1)
    def _():
        grad_leaving[...] = grad[...]
        e_leaving[...] = e_buffer[0:HALO, :]


def fixed(shape):
    return pl.BlockSpec(shape, lambda i: (0,) * len(shape))


def mixer_forward(gate, rest, tail, start, slab, spread, heads):
    rows, width = rest.shape
    state_size, channels = start.shape
    size = channels + 2 * LANES
    steps = rows // CHUNK
    by_row = lambda cols: pl.BlockSpec((CHUNK, cols), lambda i: (i, 0))
    shape = jax.ShapeDtypeStruct

    def body(*refs):
        forward_kernel(*refs, channels=channels, heads=heads)

    return pl.pallas_call(
        body,
        grid=(steps,),
        in_specs=[
            by_row(channels),
            by_row(width),
            fixed((HALO, size)),
            fixed(start.shape),
            fixed(slab.shape),
            fixed(spread.shape),
        ],
        out_specs=[
            by_row(channels),
            by_row(1),
            by_row(channels),
            pl.BlockSpec((1, state_size, channels), lambda i: (i, 0, 0)),
            fixed(start.shape),
        ],
        out_shape=[
            shape((rows, channels), BF16),
            shape((rows, 1), F32),
            shape((rows, channels), F32),
            shape((steps, state_size, channels), F32),
            shape(start.shape, F32),
        ],
        scratch_shapes=[
            pltpu.VMEM((state_size, channels), F32),
            pltpu.VMEM((CHUNK + HALO, size), F32),
        ],
        compiler_params=pltpu.CompilerParams(
            dimension_semantics=("arbitrary",), vmem_limit_bytes=MIXER_VMEM
        ),
        cost_estimate=pl.CostEstimate(flops=1000, bytes_accessed=1000, transcendentals=0),
        name="mixer_forward",
    )(gate, rest, tail, start, slab, spread)


def mixer_backward(
    q, factor, gate, rest, tail, y, entering, grad, e_rows, slab, spread, gather, heads, grant
):
    rows, width = rest.shape
    state_size, channels = grad.shape
    size = channels + 2 * LANES
    steps = rows // CHUNK
    by_row = lambda cols: pl.BlockSpec((CHUNK, cols), lambda i: (steps - 1 - i, 0))
    shape = jax.ShapeDtypeStruct
    groups = CHUNK // HALO

    def body(*refs):
        backward_kernel(*refs, channels=channels, heads=heads)

    return pl.pallas_call(
        body,
        grid=(steps,),
        in_specs=[
            by_row(channels),
            by_row(2),
            by_row(channels),
            by_row(width),
            pl.BlockSpec(
                (HALO, width), lambda i: (jnp.maximum((steps - 1 - i) * groups - 1, 0), 0)
            ),
            fixed((HALO, size)),
            by_row(channels),
            pl.BlockSpec((1, state_size, channels), lambda i: (steps - 1 - i, 0, 0)),
            fixed(grad.shape),
            fixed(e_rows.shape),
            fixed(slab.shape),
            fixed(spread.shape),
            fixed(gather.shape),
        ],
        out_specs=[
            by_row(channels + width),
            fixed(grad.shape),
            fixed(e_rows.shape),
            fixed(slab.shape),
        ],
        out_shape=[
            shape((rows, channels + width), BF16),
            shape(grad.shape, F32),
            shape(e_rows.shape, F32),
            shape(slab.shape, F32),
        ],
        scratch_shapes=[
            pltpu.VMEM((state_size, channels), F32),
            pltpu.VMEM((CHUNK + HALO, size), F32),
            pltpu.VMEM((CHUNK + HALO, size), F32),
        ],
        compiler_params=pltpu.CompilerParams(
            dimension_semantics=("arbitrary",), vmem_limit_bytes=grant
        ),
        cost_estimate=pl.CostEstimate(flops=1000, bytes_accessed=1000, transcendentals=0),
        name="mixer_backward",
    )(q, factor, gate, rest, rest, tail, y, entering, grad, e_rows, slab, spread, gather)


def finish_kernel(first_own, first_other, second_own, second_other, gates, *, channels):
    core = lax.axis_index("section")

    def write(low, high):
        for half, source in enumerate((low, high)):
            value = source[...].astype(F32)
            for k in range(2):
                gates[:, k, half * channels : (half + 1) * channels] = value[
                    :, k * channels : (k + 1) * channels
                ]

    @pl.when(core == 0)
    def _():
        write(first_own, first_other)

    @pl.when(core == 1)
    def _():
        write(second_other, second_own)


def join_halves(first_own, first_other, second_own, second_other, channels):
    rows = first_own.shape[0]
    step = 32
    block = pl.BlockSpec((step, 2 * channels), lambda i: (i, 0))
    return pl.pallas_call(
        functools.partial(finish_kernel, channels=channels),
        grid=(rows // step,),
        in_specs=[block] * 4,
        out_specs=pl.BlockSpec((step, 2, 2 * channels), lambda i: (i, 0, 0)),
        out_shape=jax.ShapeDtypeStruct((rows, 2, 2 * channels), F32),
        compiler_params=pltpu.CompilerParams(
            dimension_semantics=("arbitrary",), vmem_limit_bytes=MIXER_VMEM
        ),
        cost_estimate=pl.CostEstimate(flops=1000, bytes_accessed=1000, transcendentals=0),
        name="join_halves",
    )(first_own, first_other, second_own, second_other)


MESH = pl.DeviceIdType.MESH
DEEP = 4
SIDEWAYS = 32
SIDE_ROWS = 48


def place_in_line():
    core, line, half = lax.axis_index("section"), lax.axis_index("fsdp"), lax.axis_index("tp")
    deep, side = line // 2, line % 2

    def device(z, x):
        return (core, z * 2 + x, half)

    return deep, side, device


def greet_all():
    core, line, half = lax.axis_index("section"), lax.axis_index("fsdp"), lax.axis_index("tp")
    barrier = pltpu.get_barrier_semaphore()

    def greet(target):
        pl.semaphore_signal(barrier, inc=1, device_id=target, device_id_type=MESH)

    greet((core, line, 1 - half))
    greet((1 - core, line, half))
    for step in range(1, 2 * DEEP):
        greet((core, (line + step) % (2 * DEEP), half))
    pl.semaphore_wait(barrier, 2 * DEEP + 1)


def gather_steps(shards, wholes, sems, beside):
    count = len(shards)
    local_sem, x_send, x_recv, up_send, up_recv, down_send, down_recv = sems[:7]
    side_send, side_recv, pair_up_send, pair_up_recv, pair_down_send, pair_down_recv = sems[7:]
    deep, side, device = place_in_line()
    above, below = jnp.minimum(deep + 1, DEEP - 1), jnp.maximum(deep - 1, 0)
    has_above, has_below = deep < DEEP - 1, deep > 0
    main = [pl.ds(0, shard.shape[0] - SIDE_ROWS) for shard in shards]
    rest = [pl.ds(shard.shape[0] - SIDE_ROWS, SIDE_ROWS) for shard in shards]

    def remote(source, place, send, recv, target):
        return pltpu.make_async_remote_copy(
            src_ref=source,
            dst_ref=place,
            send_sem=send,
            recv_sem=recv,
            device_id=target,
            device_id_type=MESH,
        )

    def own(i):
        return pltpu.make_async_copy(shards[i], wholes[i].at[deep * 2 + side], local_sem.at[i])

    def block(i, z, x=None):
        return wholes[i].at[z * 2 + (side if x is None else x), main[i]]

    def across(i, z, source=None):
        source = block(i, z) if source is None else source
        target = device(deep, 1 - side)
        return remote(source, block(i, z), x_send.at[i, z], x_recv.at[i, z], target)

    def upward(i, k, source=None):
        place = block(i, deep - k)
        source = place if source is None else source
        return remote(source, place, up_send.at[i, k], up_recv.at[i, k], device(above, side))

    def downward(i, k, source=None):
        place = block(i, deep + k)
        source = place if source is None else source
        return remote(source, place, down_send.at[i, k], down_recv.at[i, k], device(below, side))

    def sideways(i, x):
        place = wholes[i].at[deep * 2 + x, rest[i]]
        source = shards[i].at[rest[i]]
        return remote(source, place, side_send.at[i], side_recv.at[i], device(deep, 1 - side))

    def pair(i, z):
        return wholes[i].at[pl.ds(z * 2, 2), rest[i]]

    def pair_up(i, k):
        place = pair(i, deep - k)
        return remote(place, place, pair_up_send.at[i, k], pair_up_recv.at[i, k], device(above, side))

    def pair_down(i, k):
        place = pair(i, deep + k)
        return remote(
            place, place, pair_down_send.at[i, k], pair_down_recv.at[i, k], device(below, side)
        )

    for i in range(count):
        own(i).start()
        sideways(i, side).start()
    for i in range(count):
        source = shards[i].at[main[i]]

        @pl.when(has_above)
        def _(i=i, source=source):
            upward(i, 0, source).start()

        @pl.when(has_below)
        def _(i=i, source=source):
            downward(i, 0, source).start()

        across(i, deep, source).start()
    beside(0)
    here = device(deep, side)
    for k in range(1, DEEP):
        for i in range(count):

            @pl.when(deep >= k)
            def _(i=i, k=k):
                place = block(i, deep - k)
                remote(place, place, up_send.at[i, k - 1], up_recv.at[i, k - 1], here).wait_recv()

                @pl.when(has_above)
                def _():
                    upward(i, k).start()

                across(i, deep - k).start()

            @pl.when(deep + k <= DEEP - 1)
            def _(i=i, k=k):
                place = block(i, deep + k)
                remote(place, place, down_send.at[i, k - 1], down_recv.at[i, k - 1], here).wait_recv()

                @pl.when(has_below)
                def _():
                    downward(i, k).start()

                across(i, deep + k).start()

        if k == DEEP - 2:
            for i in range(count):
                own(i).wait()
                sideways(i, 1 - side).wait_recv()

                @pl.when(has_above)
                def _(i=i):
                    pair_up(i, 0).start()

                @pl.when(has_below)
                def _(i=i):
                    pair_down(i, 0).start()

        beside(k)

    for k in range(1, DEEP):
        for i in range(count):

            @pl.when(deep >= k)
            def _(i=i, k=k):
                place = pair(i, deep - k)
                remote(
                    place, place, pair_up_send.at[i, k - 1], pair_up_recv.at[i, k - 1], here
                ).wait_recv()

                @pl.when(has_above)
                def _():
                    pair_up(i, k).start()

            @pl.when(deep + k <= DEEP - 1)
            def _(i=i, k=k):
                place = pair(i, deep + k)
                remote(
                    place, place, pair_down_send.at[i, k - 1], pair_down_recv.at[i, k - 1], here
                ).wait_recv()

                @pl.when(has_below)
                def _():
                    pair_down(i, k).start()

    for i in range(count):
        sideways(i, side).wait_send()
        for z in range(DEEP):
            other = remote(
                block(i, z), block(i, z, 1 - side), x_send.at[i, z], x_recv.at[i, z], here
            )
            other.wait_send()
            other.wait_recv()
        for k in range(DEEP - 1):

            @pl.when(has_above & (deep >= k))
            def _(i=i, k=k):
                upward(i, k).wait_send()
                pair_up(i, k).wait_send()

            @pl.when(has_below & (deep + k <= DEEP - 1))
            def _(i=i, k=k):
                downward(i, k).wait_send()
                pair_down(i, k).wait_send()


def start_kernel(*refs, count, micros, heads, gain_rows):
    shards, (gain, own, cotangent) = refs[:count], refs[count : count + 3]
    params, spread = refs[count + 3 : count + 9], refs[count + 9]
    outs = refs[count + 10 :]
    wholes, (gains, slabs), targets = outs[:count], outs[count : count + 2], outs[count + 2 :]
    targets, scratch = targets[: 2 * micros], targets[2 * micros :]
    gain_send, gain_recv, own_sem, y_send, y_recv, core_send, core_recv, rows_out = scratch[13:21]
    other_slab, slab_send, slab_recv, line_send, line_recv = scratch[21:]
    core, line, half = lax.axis_index("section"), lax.axis_index("fsdp"), lax.axis_index("tp")
    lines = 2 * DEEP

    greet_all()
    across_tp, across_core = (core, line, 1 - half), (1 - core, line, half)

    def send_gain(step):
        return pltpu.make_async_remote_copy(
            src_ref=gain,
            dst_ref=gains.at[core, line],
            send_sem=gain_send.at[step],
            recv_sem=gain_recv.at[step],
            device_id=(core, (line + step) % lines, half),
            device_id_type=MESH,
        )

    for step in range(1, lines):
        send_gain(step).start()

    tokens = own.shape[1] // 2
    mine = pl.ds(pl.multiple_of(core * tokens, tokens), tokens)

    def token_copies(n):
        m = n % micros
        source = rows_out.at[pl.ds(m * tokens, tokens)] if n < micros else cotangent.at[m, mine]
        place = targets[n].at[half, core]
        later = targets[n].at[1 - half, core]
        more = 2 * micros + n
        remote = functools.partial(pltpu.make_async_remote_copy, device_id_type=MESH)
        return (
            pltpu.make_async_copy(source, place, own_sem.at[n]),
            remote(source, place, y_send.at[n], y_recv.at[n], device_id=across_tp),
            remote(source, place, core_send.at[n], core_recv.at[n], device_id=across_core),
            remote(later, later, core_send.at[more], core_recv.at[more], device_id=across_core),
        )

    send_slab = pltpu.make_async_remote_copy(
        src_ref=other_slab,
        dst_ref=slabs.at[core],
        send_sem=slab_send.at[0],
        recv_sem=slab_recv.at[0],
        device_id=across_core,
        device_id_type=MESH,
    )
    send_line = pltpu.make_async_remote_copy(
        src_ref=gains.at[core],
        dst_ref=gains.at[core],
        send_sem=line_send.at[0],
        recv_sem=line_recv.at[0],
        device_id=across_core,
        device_id_type=MESH,
    )

    def write_slab(place, index):
        taps, bias, shared_taps, shared_bias, gate, per_head = (v[...] for v in params)
        channels = spread.shape[1]
        first = index == 0
        cut = lambda v: jnp.where(first, v[:, :channels], v[:, channels:])
        lane = lax.broadcasted_iota(jnp.int32, per_head.shape, 1)
        here = jnp.where(first, per_head, pltpu.roll(per_head, LANES - heads, 1))
        here = jnp.where(lane < heads, here, 0.0)
        skip = expand(here, spread[...], heads)
        decay = jnp.where(lane < heads, -jnp.exp(here), 0.0)
        place[...] = jnp.zeros(place.shape, F32)
        place[0:CONV, :channels] = cut(taps)
        place[0:CONV, channels:] = shared_taps
        place[CONV : CONV + 1, :channels] = cut(bias)
        place[CONV : CONV + 1, channels:] = shared_bias
        place[5:6, :channels] = cut(gate)
        place[5:6, channels : channels + LANES] = here[0:1]
        place[6:7, :channels] = skip[2:3]
        place[6:7, channels : channels + LANES] = decay[1:2]

    def send_tokens(stage):
        if stage == 0:
            send_first()
        elif stage <= 2:
            for n in range((stage - 1) * micros, stage * micros):
                token_copies(n)[1].wait_recv()
                token_copies(n)[3].start()
            if stage == 1:
                for n in range(micros, 2 * micros):
                    for copy in token_copies(n)[:3]:
                        copy.start()

    def send_first():
        write_slab(other_slab, 1 - core)
        send_slab.start()
        write_slab(slabs.at[core], core)
        gains[core, line] = gain[...]
        for step in range(1, lines):
            send_gain(step).wait()
        send_line.start()
        send_line.wait()
        gain_row = jnp.concatenate(
            [gains[0, f, j : j + 1, :] for f in range(lines) for j in range(gain_rows)], axis=1
        )
        for m in range(micros):
            h = own[m, mine].astype(F32)
            scale = lax.rsqrt(jnp.mean(h * h, axis=1, keepdims=True) + EPS)
            rows_out[m * tokens : (m + 1) * tokens] = (h * scale * gain_row).astype(BF16)

        for n in range(micros):
            for copy in token_copies(n)[:3]:
                copy.start()

    gather_steps(shards, wholes, scratch[:13], send_tokens)
    send_slab.wait()
    for n in range(2 * micros):
        own_copy, y_copy, core_copy, core_later = token_copies(n)
        own_copy.wait()
        y_copy.wait_send()
        core_copy.wait()
        core_later.wait()


def start_gather(shards, gain, own, cotangent, params, spread, micros, heads, gain_rows):
    count = len(shards)
    lines = 2 * DEEP
    pairs = pltpu.SemaphoreType.DMA((count, DEEP))
    dma = lambda n: pltpu.SemaphoreType.DMA((n,))
    shape = jax.ShapeDtypeStruct
    anywhere = pl.BlockSpec(memory_space=pl.ANY)
    vmem = pl.BlockSpec(memory_space=pltpu.VMEM)
    rows, width = own.shape[0] * own.shape[1] // 2, own.shape[2]
    slab = (8, spread.shape[1] + params[2].shape[1])
    return pl.pallas_call(
        functools.partial(
            start_kernel, count=count, micros=micros, heads=heads, gain_rows=gain_rows
        ),
        out_shape=[shape((lines,) + v.shape, v.dtype) for v in shards]
        + [
            shape((2, lines) + gain.shape, F32),
            shape((2,) + slab, F32),
        ]
        + [shape((2, 2, rows // micros, width), BF16)] * (2 * micros),
        in_specs=[anywhere] * count + [vmem, vmem, anywhere] + [vmem] * 7,
        out_specs=[anywhere] * count + [vmem, vmem] + [anywhere] * (2 * micros),
        scratch_shapes=[dma(count)]
        + [pairs] * 6
        + [dma(count)] * 2
        + [pairs] * 4
        + [dma(lines)] * 2
        + [dma(2 * micros)] * 3
        + [dma(4 * micros)] * 2
        + [pltpu.VMEM((rows, width), BF16), pltpu.VMEM(slab, F32)]
        + [dma(1)] * 4,
        compiler_params=pltpu.CompilerParams(
            collective_id=1, has_side_effects=True, vmem_limit_bytes=VMEM_LIMIT
        ),
        cost_estimate=pl.CostEstimate(flops=170_000_000_000, bytes_accessed=1000, transcendentals=0),
        name="start_gather",
    )(*shards, gain, own, cotangent, *params, spread)


def add_rows(out, *parts):
    rows = out.shape[0]
    step = 16

    def body(n, _):
        at = pl.ds(pl.multiple_of(n * step, step), step)
        total = parts[0][at].astype(F32)
        for part in parts[1:]:
            total = total + part[at].astype(F32)
        out[at] = total.astype(out.dtype)
        return 0

    lax.fori_loop(0, rows // step, body, 0)


X_ORDER = ((3, 2, 1, 0), (3, 0, 2, 1), (0, 3, 1, 2), (0, 1, 2, 3))


def reduce_kernel(*refs, count):
    parts, small, results = refs[:count], refs[count], refs[count + 1 : 2 * count + 1]
    others = refs[2 * count + 1 : 3 * count + 1]
    own_small, next_small, both_small = refs[3 * count + 1 : 3 * count + 4]
    scratch = refs[3 * count + 4 :]
    held, crossed, from_below, from_above, pairs, pairs_below, pairs_above, side_in = (
        scratch[n * count : (n + 1) * count] for n in range(8)
    )
    sems = scratch[8 * count : -5]
    load_sem, x_send, x_recv, up_send, up_recv, down_send, down_recv = sems[:7]
    pair_sem, pair_up_send, pair_up_recv, pair_down_send, pair_down_recv = sems[7:12]
    side_send, side_recv = sems[12:]
    small_buffer, small_send, small_recv, other_send, other_recv = scratch[-5:]
    main = [result.shape[0] - SIDEWAYS for result in results]
    deep, side, device = place_in_line()
    core, line, half = lax.axis_index("section"), lax.axis_index("fsdp"), lax.axis_index("tp")
    greet_all()
    across_core = (1 - core, line, half)
    partners = [
        device(deep, 1 - side),
        device(deep + 1 - 2 * (deep % 2), side),
        device((deep + 2) % DEEP, side),
        (core, line, 1 - half),
        across_core,
        across_core,
    ]

    def swap_small(n, source, target):
        return pltpu.make_async_remote_copy(
            src_ref=source,
            dst_ref=target,
            send_sem=small_send.at[n],
            recv_sem=small_recv.at[n],
            device_id=partners[n],
            device_id_type=MESH,
        )

    def sum_small():
        for n in range(3):
            copy = swap_small(n, small if n == 0 else small_buffer.at[n - 1], small_buffer.at[3 + n])
            if n > 0:
                copy.start()
            copy.wait()
            value = small[...] if n == 0 else small_buffer[n - 1]
            small_buffer[n] = value + small_buffer[3 + n]
        over_tp = swap_small(3, small_buffer.at[2], small_buffer.at[6])
        over_core = swap_small(4, small_buffer.at[2, 1 - core], next_small)
        over_tp.start()
        over_core.start()
        own_small[...] = small_buffer[2, core]
        over_tp.wait()
        small_buffer[7] = small_buffer[2] + small_buffer[6]
        last = swap_small(5, small_buffer.at[7, 1 - core], small_buffer.at[8, 0])
        last.start()
        last.wait()
        both_small[...] = small_buffer[7, core] + small_buffer[8, 0]
        over_core.wait()

    def rows(i, z, x):
        return parts[i].at[z * 2 + x, pl.ds(0, main[i])]

    def load_pair(i, z):
        source = parts[i].at[pl.ds(z * 2, 2), pl.ds(main[i], SIDEWAYS)]
        return pltpu.make_async_copy(source, pairs[i].at[z], pair_sem.at[i, z])

    def pair_along(i, k, z, here, up):
        send, recv = (pair_up_send, pair_up_recv) if up else (pair_down_send, pair_down_recv)
        target = min(here + 1, DEEP - 1) if up else max(here - 1, 0)
        return pltpu.make_async_remote_copy(
            src_ref=pairs[i].at[z],
            dst_ref=(pairs_below if up else pairs_above)[i].at[k - 1],
            send_sem=send.at[i, k - 1],
            recv_sem=recv.at[i, k - 1],
            device_id=device(target, side),
            device_id_type=MESH,
        )

    def sideways(i, here):
        return pltpu.make_async_remote_copy(
            src_ref=pairs[i].at[here, 1 - side],
            dst_ref=side_in[i],
            send_sem=side_send.at[i],
            recv_sem=side_recv.at[i],
            device_id=device(deep, 1 - side),
            device_id_type=MESH,
        )

    def load(i, z):
        return pltpu.make_async_copy(rows(i, z, side), held[i].at[z], load_sem.at[i, z])

    def across(i, z):
        return pltpu.make_async_remote_copy(
            src_ref=rows(i, z, 1 - side),
            dst_ref=crossed[i].at[z],
            send_sem=x_send.at[i, z],
            recv_sem=x_recv.at[i, z],
            device_id=device(deep, 1 - side),
            device_id_type=MESH,
        )

    def upward(i, k, z, here):
        return pltpu.make_async_remote_copy(
            src_ref=held[i].at[z],
            dst_ref=from_below[i].at[k - 1],
            send_sem=up_send.at[i, k - 1],
            recv_sem=up_recv.at[i, k - 1],
            device_id=device(min(here + 1, DEEP - 1), side),
            device_id_type=MESH,
        )

    def downward(i, k, z, here):
        return pltpu.make_async_remote_copy(
            src_ref=held[i].at[z],
            dst_ref=from_above[i].at[k - 1],
            send_sem=down_send.at[i, k - 1],
            recv_sem=down_recv.at[i, k - 1],
            device_id=device(max(here - 1, 0), side),
            device_id_type=MESH,
        )

    def to_other(i):
        return pltpu.make_async_remote_copy(
            src_ref=results[i],
            dst_ref=others[i],
            send_sem=other_send.at[i],
            recv_sem=other_recv.at[i],
            device_id=across_core,
            device_id_type=MESH,
        )

    def at_depth(here):
        order = X_ORDER[here]
        last = DEEP - 1
        started = []

        def send_across(number):
            for i in range(count):
                across(i, order[number]).start()

        def take(number):
            z = order[number]
            for i in range(count):
                across(i, z).wait_recv()
            if number + 2 < DEEP:
                send_across(number + 2)
            for i in range(count):
                load(i, z).wait()
                add_rows(held[i].at[z], held[i].at[z], crossed[i].at[z])

        def relay(k, up):
            z = DEEP - k + here if up else here + k - DEEP
            first = here == 0 if up else here == last
            for i in range(count):
                if not first:
                    make = upward if up else downward
                    back = from_below if up else from_above
                    make(i, k - 1, z, here).wait_recv()
                    add_rows(held[i].at[z], held[i].at[z], back[i].at[k - 2])
                copy = (upward if up else downward)(i, k, z, here)
                copy.start()
                started.append(copy)

        swap_small(0, small, small_buffer.at[3]).start()
        send_across(0)
        send_across(1)
        for number in range(DEEP):
            for i in range(count):
                load_pair(i, order[number]).start()
        for number in range(DEEP):
            for i in range(count):
                load(i, order[number]).start()

        def relay_pair(k, up):
            z = DEEP - k + here if up else here + k - DEEP
            if not 0 <= z < DEEP or z == here or (z < here) == up:
                return
            for i in range(count):
                load_pair(i, z).wait()
                if here != (0 if up else last):
                    pair_along(i, k - 1, z, here, up).wait_recv()
                    back = (pairs_below if up else pairs_above)[i]
                    for x in range(2):
                        add_rows(pairs[i].at[z, x], pairs[i].at[z, x], back.at[k - 2, x])
                copy = pair_along(i, k, z, here, up)
                copy.start()
                started.append(copy)

        for k in range(1, DEEP):
            relay_pair(k, True)
            relay_pair(k, False)
        sum_small()
        for i in range(count):
            load_pair(i, here).wait()
            for x in range(2):
                terms = [pairs[i].at[here, x]]
                if here > 0:
                    if x == 0:
                        pair_along(i, DEEP - 1, here, here, True).wait_recv()
                    terms.append(pairs_below[i].at[DEEP - 2, x])
                if here < last:
                    if x == 0:
                        pair_along(i, DEEP - 1, here, here, False).wait_recv()
                    terms.append(pairs_above[i].at[DEEP - 2, x])
                add_rows(pairs[i].at[here, x], *terms)
            sideways(i, here).start()
        if here in (0, last):
            up = here == 0
            for k in range(1, DEEP):
                take(k - 1)
                relay(k, up)
            take(DEEP - 1)
        else:
            up = here == 1
            take(0)
            take(1)
            relay(2, up)
            relay(3, not up)
            take(2)
            relay(3, up)
            take(3)
        for i in range(count):
            terms = [held[i].at[here]]
            if here > 0:
                upward(i, DEEP - 1, here, here).wait_recv()
                terms.append(from_below[i].at[DEEP - 2])
            if here < last:
                downward(i, DEEP - 1, here, here).wait_recv()
                terms.append(from_above[i].at[DEEP - 2])
            add_rows(results[i].at[pl.ds(0, main[i])], *terms)
            sideways(i, here).wait_recv()
            add_rows(
                results[i].at[pl.ds(main[i], SIDEWAYS)], pairs[i].at[here, side], side_in[i]
            )
            to_other(i).start()
        for i in range(count):
            to_other(i).wait()
            sideways(i, here).wait_send()
        for copy in started:
            copy.wait_send()
        for z in range(DEEP):
            for i in range(count):
                across(i, z).wait_send()

    for here in range(DEEP):

        @pl.when(deep == here)
        def _(here=here):
            at_depth(here)


def reduce_line(parts, small, name, collective_id):
    count = len(parts)
    shards = [(p.shape[0] // (2 * DEEP),) + p.shape[1:] for p in parts]
    pairs = pltpu.SemaphoreType.DMA((count, DEEP))
    sizes = sum(p.size for p in parts)
    blocks = lambda n: [pltpu.VMEM((n, shard[0] - SIDEWAYS, shard[1]), BF16) for shard in shards]
    doubles = lambda n: [pltpu.VMEM((n, 2, SIDEWAYS, shard[1]), BF16) for shard in shards]
    split_parts = [p.reshape((2 * DEEP, -1) + p.shape[1:]) for p in parts]
    shape = jax.ShapeDtypeStruct
    vmem = pl.BlockSpec(memory_space=pltpu.VMEM)
    return pl.pallas_call(
        functools.partial(reduce_kernel, count=count),
        out_shape=[shape(shard, BF16) for shard in shards] * 2 + [shape(small.shape[1:], F32)] * 3,
        in_specs=[pl.BlockSpec(memory_space=pl.ANY)] * count + [vmem],
        out_specs=[vmem] * (2 * count + 3),
        scratch_shapes=blocks(DEEP)
        + blocks(DEEP)
        + blocks(DEEP - 1)
        + blocks(DEEP - 1)
        + doubles(DEEP)
        + doubles(DEEP - 1)
        + doubles(DEEP - 1)
        + [pltpu.VMEM((SIDEWAYS, shard[1]), BF16) for shard in shards]
        + [pairs] * 12
        + [pltpu.SemaphoreType.DMA((count,))] * 2
        + [
            pltpu.VMEM((9,) + small.shape, F32),
            pltpu.SemaphoreType.DMA((6,)),
            pltpu.SemaphoreType.DMA((6,)),
            pltpu.SemaphoreType.DMA((count,)),
            pltpu.SemaphoreType.DMA((count,)),
        ],
        compiler_params=pltpu.CompilerParams(
            collective_id=collective_id, has_side_effects=True, vmem_limit_bytes=VMEM_LIMIT
        ),
        cost_estimate=pl.CostEstimate(flops=1000, bytes_accessed=1000, transcendentals=0),
        name=name,
    )(*split_parts, small)


SWAP = [(0, 1), (1, 0)]


def swap_core(value):
    return lax.ppermute(value, "section", SWAP)


def swap_tp(value):
    return lax.ppermute(value, "tp", SWAP)


def by_index(index, own, other):
    first = index == 0
    return jnp.stack([jnp.where(first, own, other), jnp.where(first, other, own)])


def pick(pair, index):
    return lax.dynamic_index_in_dim(pair, index, 0, keepdims=False)


def gather_tokens(own, core, half, beside=()):
    both = by_index(half, own, after(swap_tp(own), *beside))
    whole = by_index(core, both, swap_core(both))
    whole = jnp.moveaxis(whole, 0, 1)
    return whole.reshape((4 * own.shape[0],) + own.shape[1:])


def after(value, *others):
    return lax.optimization_barrier((value,) + others)[0] if others else value


def over_cores(part, core, *beside):
    split_rows = part.reshape((2, 2, part.shape[0] // 4) + part.shape[1:])
    mine = lax.dynamic_index_in_dim(split_rows, core, 1, keepdims=False)
    theirs = lax.dynamic_index_in_dim(split_rows, 1 - core, 1, keepdims=False)
    return mine.astype(F32) + after(swap_core(theirs), *beside).astype(F32)


class Sum:
    def __init__(self, part, core, half, needed=(), beside=()):
        self.half = half
        self.total = over_cores(part, core, *beside)
        sent = after(pick(self.total, 1 - half), *needed)
        self.sent = sent.astype(BF16) if part.ndim > 1 else sent

    def done(self, *beside):
        return pick(self.total, self.half) + after(swap_tp(self.sent), *beside).astype(F32)


def local(
    inputs,
    cotangent,
    norm_gain,
    w_zx,
    w_bc,
    w_dt,
    conv_x,
    conv_xb,
    conv_bc,
    conv_bcb,
    dt_bias,
    a_log,
    d_skip,
    gate_gain,
    w_out,
):
    cores = lax.axis_size("section")
    core = lax.axis_index("section")
    half = lax.axis_index("tp")
    micros = inputs.shape[1]
    rows = inputs.shape[2] // cores
    channels = w_zx.shape[3] // cores
    heads = w_dt.shape[2] // cores
    width = channels // heads
    shared = w_bc.shape[2]
    depth = w_zx.shape[1]
    in_width = 2 * channels + shared + LANES
    def cut(tensor, index, size):
        return lax.dynamic_slice_in_dim(tensor, index * size, size, tensor.ndim - 1)

    def weight_shard(index):
        zx = cut(w_zx[0], index, channels).reshape(depth, 2 * channels)
        steps = jnp.pad(cut(w_dt[0], index, heads), ((0, 0), (0, LANES - heads)))
        return jnp.concatenate([zx, w_bc[0], steps, cut(w_out[0], index, channels)], axis=1)

    def slab_of(index):
        pad = jnp.zeros((LANES - heads,), F32)
        steps = jnp.concatenate([cut(dt_bias[0], index, heads), pad])
        decay = jnp.concatenate([-jnp.exp(cut(a_log[0], index, heads)), pad])
        skip = jnp.repeat(cut(d_skip[0], index, heads), width)
        rest = jnp.zeros((shared - LANES,), F32)
        taps = jnp.concatenate([cut(conv_x[0], index, channels), conv_bc[0]], axis=1)
        bias = jnp.concatenate([cut(conv_xb[0], index, channels), conv_bcb[0]])
        return jnp.concatenate(
            [
                taps,
                bias[None],
                jnp.concatenate([cut(gate_gain[0], index, channels), steps, rest])[None],
                jnp.concatenate([skip, decay, rest])[None],
                jnp.zeros((1, channels + shared), F32),
            ]
        )

    lane = np.arange(LANES)
    head_of = np.arange(channels) // width
    spread = (lane[:, None] % heads == head_of[None, :]) & (lane[:, None] < 2 * heads)
    spread = jnp.asarray(spread.astype(np.float32), BF16)
    gather = jnp.asarray((head_of[:, None] == lane[None, :]).astype(np.float32), BF16)

    own_shard = weight_shard(core)
    got_shard = swap_core(weight_shard(1 - core))
    in_line = lax.axis_size("fsdp") == 2 * DEEP and lax.axis_size("tp") == 2
    over_fsdp = functools.partial(lax.all_gather, axis_name="fsdp", tiled=True)
    def shard_of(layer, begin, end):
        return jnp.where(core == layer, own_shard[:, begin:end], got_shard[:, begin:end])

    def own_rows(tensor):
        return [
            lax.dynamic_slice_in_dim(tensor[0, m], core * rows, rows, 0) for m in range(micros)
        ]

    first, cotangents = own_rows(inputs), own_rows(cotangent)
    if in_line:
        gain_rows = depth // LANES
        packed = jnp.pad(norm_gain.astype(F32).reshape(-1, LANES), ((0, 8 - gain_rows), (0, 0)))
        per_head = jnp.concatenate([dt_bias, a_log, d_skip])
        per_head = jnp.pad(per_head, ((0, 5), (0, LANES - per_head.shape[1])))
        params = (conv_x[0], conv_xb, conv_bc[0], conv_bcb, gate_gain, per_head)
        second_gate, second_back = shard_of(1, 0, channels), shard_of(1, in_width, None)
        w_in, w_back, second_rest, gains, slabs, *tokens = start_gather(
            (shard_of(0, 0, in_width), shard_of(0, in_width, None), shard_of(1, channels, in_width)),
            packed,
            inputs[0],
            cotangent[0],
            params,
            spread,
            micros,
            heads,
            gain_rows,
        )
        slabs = [slabs[0], slabs[1]]
        w_in, w_back, second_rest = (v.reshape(-1, v.shape[2]) for v in (w_in, w_back, second_rest))
        projections = [(w_in, w_back)]
        second = (over_fsdp(after(second_gate, gains), axis=0), second_rest)
        projections.append((second, over_fsdp(after(second_back, gains), axis=0)))
        gains = gains[:, :, :gain_rows].reshape(2, -1)
        tokens = [v.reshape(4 * rows, -1) for v in tokens]
        first_normed, everyones = tokens[:micros], tokens[micros:]
    else:
        own_slab, got_slab = slab_of(core), swap_core(slab_of(1 - core))
        slabs = [jnp.where(core == layer, own_slab, got_slab) for layer in range(2)]
        gain_pair = by_index(core, norm_gain[0], swap_core(norm_gain[0])).astype(F32)
        projections = [
            (
                over_fsdp(shard_of(layer, 0, in_width), axis=0),
                over_fsdp(shard_of(layer, in_width, None), axis=0),
            )
            for layer in range(2)
        ]
        gains = over_fsdp(gain_pair.astype(BF16), axis=1).astype(F32)
        first_normed = None
        everyones = [gather_tokens(v, core, half) for v in cotangents]

    size = channels + shared
    zero_state = jnp.zeros((shared // 2, channels), F32)
    zero_halo = jnp.zeros((HALO, size), F32)
    last = micros - 1

    def scale_of(h):
        return lax.rsqrt(jnp.mean(h * h, axis=1, keepdims=True) + EPS)

    def norm(h, layer):
        return (h * scale_of(h) * gains[layer][None]).astype(BF16)

    hidden = [v.astype(F32) for v in first]
    normed = [None] * micros
    for m in range(micros):
        normed[m] = (
            first_normed[m] if in_line else gather_tokens(norm(hidden[m], 0), core, half)
        )

    hiddens, normeds, kept = [hidden, None], [normed, None], [[None] * micros for _ in range(2)]
    waiting = None

    def finish(pending, *beside):
        m, part, squares = pending
        r = lax.rsqrt(squares.done(*beside) / DI + EPS)[:, None]
        branch = r * part.done(*beside)
        kept[0][m].update(r=r, branch=branch)
        h = hiddens[0][m] + branch
        hiddens[1][m] = h
        return norm(h, 1)

    def spread_out(pending, own, *beside):
        normeds[1][pending[0]] = gather_tokens(own, core, half, beside)

    hiddens[1], normeds[1] = [None] * micros, [None] * micros
    for layer in range(2):
        w_in, w_back = projections[layer]
        state, tail = zero_state, zero_halo
        for m in range(micros):
            tokens = normeds[layer][m]
            if layer == 0 or not in_line:
                w_pair = (w_in[:, :channels], w_in[:, channels:])
            else:
                w_pair = w_in
            if waiting is not None and layer == 1:
                tokens = after(tokens, waiting[1].sent, waiting[2].sent)
            rest = dot_nn(tokens, w_pair[1])
            gate = dot_nn(tokens, w_pair[0])
            mixed_rest = rest
            if waiting is not None and layer == 1:
                own = finish(waiting, rest)
                gate = after(gate, own)
            elif waiting is not None:
                mixed_rest = after(rest, waiting[1].sent, waiting[2].sent)
            u, squares, y, entering, state_out = mixer_forward(
                gate, mixed_rest, tail, state, slabs[layer], spread, heads
            )
            if waiting is not None:
                spread_out(waiting, own if layer == 1 else finish(waiting, u), u)
            kept[layer][m] = dict(
                gate=gate, rest=rest, tail=tail, u=u, y=y, entering=entering, squares=squares
            )
            state, tail = state_out, rest[-HALO:, :size]
            waiting = None
            if layer == 0:
                part = Sum(dot_nt(u, w_back).astype(BF16), core, half)
                waiting = (m, part, Sum(squares[:, 0], core, half))

    over_tokens = (((0,), (0,)), ((), ()))

    def weight_grad(left, right):
        return lax.dot_general(
            jnp.concatenate(left), jnp.concatenate(right), over_tokens, preferred_element_type=F32
        ).astype(BF16)

    reduced, small = [None, None], [None, None]
    grads = [v.astype(F32) for v in cotangents]
    mixers_done = [kept[1][m]["u"] for m in range(micros)]
    w_in, w_back = projections[1]
    if in_line:
        w_in = jnp.concatenate([after(v, *mixers_done) for v in w_in], axis=1)
    w_back = after(w_back, w_in, *mixers_done)
    projections[1] = (w_in, w_back)
    backs, products, factors = list(everyones), [None] * micros, [None] * micros
    pairs = [None] * micros
    for m in reversed(range(micros)):
        k = kept[1][m]
        products[m] = dot_nn(backs[m], w_back)
        dots = jnp.sum(products[m] * k["u"].astype(F32), axis=1)
        pairs[m] = jnp.stack([k["squares"][:, 0], dots])
    pair = jnp.stack(pairs)
    pair = pair + swap_core(pair)
    pair = pair + swap_tp(pair)
    r = lax.rsqrt(pair[:, 0] / DI + EPS)
    factors = [jnp.stack([r[m], r[m] * r[m] * r[m] * pair[m, 1] / DI], axis=1) for m in range(micros)]
    gain_parts = [[], []]

    def finish_back(pending, *beside):
        layer, m, part = pending
        h = hiddens[layer][m]
        scale = scale_of(h)
        g_norm = part.done(*beside)
        gain_parts[layer].append(jnp.sum(g_norm * (h * scale), axis=0))
        g_norm = g_norm * gains[layer][None]
        mean = jnp.mean(g_norm * h, axis=1, keepdims=True)
        g = grads[m] + scale * g_norm - h * (scale * scale * scale) * mean
        grads[m] = g
        if layer == 0:
            return (g,)
        r, branch = kept[0][m]["r"], kept[0][m]["branch"]
        kappa = r * r * jnp.sum(g * branch, axis=1)[:, None] / DI
        return g.astype(BF16), jnp.concatenate([r, kappa], axis=1)

    def spread_back(pending, own, *beside):
        layer, m = pending[:2]
        if layer == 1:
            next_backs[m] = gather_tokens(own[0], core, half, beside)
            next_factors[m] = gather_tokens(own[1], core, half, beside)

    def reduce_rows(part):
        return lax.psum_scatter(part, "fsdp", scatter_dimension=0, tiled=True)

    def small_of(layer, totals):
        gain_rows = sum(gain_parts[layer]).reshape(2, -1)
        return jnp.concatenate(
            [totals[:6], jnp.concatenate([gain_rows, totals[6:, channels:]], axis=1)]
        )

    waiting, outs = None, [None] * micros
    next_backs, next_factors = [None] * micros, [None] * micros
    for layer in (1, 0):
        w_in, w_back = projections[layer]
        state, e_rows = zero_state, zero_halo
        totals = jnp.zeros(slabs[0].shape, F32)
        gpres = [None] * micros
        for m in reversed(range(micros)):
            k = kept[layer][m]
            q = products[m] if layer == 1 else dot_nn(backs[m], w_back)
            if m == last and layer == 1:
                mixed = [
                    (kept[1][j]["u"].astype(F32) * factors[j][:, :1]).astype(BF16)
                    for j in range(micros)
                ]
                reduced_back = weight_grad(backs, mixed)
                q = after(q, reduced_back)
                reduced_back = reduce_rows(reduced_back)
            if waiting is not None and not (layer == 0 and m == 0):
                q = after(q, waiting[2].sent)
            gpre, state, e_rows, sums = mixer_backward(
                q,
                factors[m],
                k["gate"],
                k["rest"],
                k["tail"],
                k["y"],
                k["entering"],
                state,
                e_rows,
                slabs[layer],
                spread,
                gather,
                heads,
                VMEM_LIMIT if layer == 1 and m == last else BACK_VMEM,
            )
            totals = totals + sums
            gpres[m] = gpre
            ready = gpre
            if waiting is not None:
                own = finish_back(waiting, gpre)
                ready = after(gpre, *own)
            if layer == 1 and m == 0:
                grad_in = weight_grad(normeds[1], gpres)
                ready = after(ready, grad_in)
            part = dot_nt(ready, w_in).astype(BF16)
            if waiting is not None:
                spread_back(waiting, own, part)
                if layer == 0 and waiting[0] == 1:
                    backs[0], factors[0] = next_backs[0], next_factors[0]
                    small[1] = small_of(1, above)
            beside = ()
            if layer == 1:
                outs[m] = dot_nt(after(k["u"], part), w_back).astype(BF16)
                beside = (outs[m],)
            waiting = (layer, m, Sum(part, core, half, (), beside))
            if layer == 0 and m == last:
                outs = [Sum(out, core, half, (waiting[2].sent,)) for out in outs]
        if layer == 0:
            grad_in = weight_grad(normeds[0], [after(v, waiting[2].sent) for v in gpres])
        if layer == 1 or not in_line:
            reduced[layer] = (reduce_rows(grad_in), reduced_back)
        if layer == 0:
            mixed = [
                (kept[0][j]["u"].astype(F32) * factors[j][:, :1]).astype(BF16) for j in range(micros)
            ]
            grad_back = weight_grad(backs, mixed)
            if not in_line:
                reduced[0] = (reduced[0][0], reduce_rows(grad_back))
        if layer == 1:
            second_factors, above = factors, totals
            backs, factors = list(next_backs), list(next_factors)
    finish_back(waiting, grad_in)
    small[0] = small_of(0, totals)

    outputs_rows = []
    for m in range(micros):
        r = lax.dynamic_slice_in_dim(second_factors[m], (2 * half + core) * rows, rows, 0)[:, :1]
        outputs_rows.append(hiddens[1][m] + r * outs[m].done(gpres[0]))

    def placed_rows(parts):
        own = jnp.where(core == 0, parts[0], parts[1])
        other = jnp.where(core == 0, parts[1], parts[0])
        return by_index(core, own, swap_core(other)).reshape(1, 1, 2 * rows, -1)

    outputs, input_grads = placed_rows(outputs_rows), placed_rows(grads)

    small_sums = after(jnp.stack(small), outputs, input_grads)
    if in_line:
        *both_parts, own_small, next_small, both_small = reduce_line(
            [grad_in, grad_back], small_sums, "grads_reduce", 2
        )
        first_own, first_other = both_parts[:2], both_parts[2:]
    else:
        small_sums = lax.psum(small_sums, "fsdp")
        own_small = pick(small_sums, core)
        next_small = swap_core(pick(small_sums, 1 - core))
        both_small = own_small + next_small
        both_small = both_small + swap_tp(both_small)
        first_own, first_other = reduced[0], [swap_core(v) for v in reduced[0]]
    low_small = jnp.where(core == 0, own_small, next_small)
    high_small = jnp.where(core == 0, next_small, own_small)
    wide = jnp.concatenate([low_small[:6, :channels], high_small[:6, :channels]], axis=1)
    narrow = jnp.concatenate(
        [v[5:, channels : channels + heads] for v in (low_small, high_small)], axis=1
    )
    conv_sum = both_small[:5, channels:]
    gain_sum = lax.dynamic_slice_in_dim(
        both_small[6:8, :channels].reshape(-1), lax.axis_index("fsdp") * depth, depth, 0
    )

    second_own = [after(v, own_small) for v in reduced[1]]
    second_other = [swap_core(v) for v in second_own]
    either = lambda one, two: jnp.where(core == 0, one.astype(F32), two.astype(F32))
    low_half = [either(first_own[i], second_other[i]) for i in range(2)]
    high_half = [either(first_other[i], second_own[i]) for i in range(2)]

    def joined(begin, end, i=0):
        return jnp.concatenate([low_half[i][:, begin:end], high_half[i][:, begin:end]], axis=1)

    g_zx = join_halves(first_own[0], first_other[0], second_own[0], second_other[0], channels)
    at = 2 * channels
    g_bc = low_half[0][:, at : at + shared] + high_half[0][:, at : at + shared]
    g_bc = g_bc + swap_tp(g_bc)
    g_dt = joined(at + shared, at + shared + heads)
    g_back = joined(0, channels, 1)

    return (
        outputs,
        input_grads,
        gain_sum[None],
        g_zx[None],
        g_bc[None],
        g_dt[None],
        wide[:4][None],
        wide[4][None],
        conv_sum[:4][None],
        conv_sum[4][None],
        narrow[0][None],
        narrow[1][None],
        narrow[2][None],
        wide[5][None],
        g_back[None],
    )


def solution(mesh):
    placed = (
        P("fsdp", None, "tp", None),
        P("fsdp", None, "tp", None),
        P("section", "fsdp"),
        P("section", "fsdp", None, "tp"),
        P("section", "fsdp", None),
        P("section", "fsdp", "tp"),
        P("section", None, "tp"),
        P("section", "tp"),
        P("section", None, None),
        P("section", None),
        P("section", "tp"),
        P("section", "tp"),
        P("section", "tp"),
        P("section", "tp"),
        P("section", "fsdp", "tp"),
    )
    return jax.shard_map(
        local,
        mesh=mesh,
        in_specs=placed,
        out_specs=(
            P("fsdp", "section", "tp", None),
            P("fsdp", "section", "tp", None),
        )
        + placed[2:],
        check_vma=False,
    )
```

```python
import functools

import jax
import jax.numpy as jnp
import numpy as np
from jax import lax
from jax.experimental import pallas as pl
from jax.experimental.pallas import tpu as pltpu
from jax.sharding import PartitionSpec as P

CONV = 4
DI = 4096
EPS = 1e-05
CHUNK = 128
LANES = 128
HALO = 8
NEG = -10000.0
F32 = jnp.float32
BF16 = jnp.bfloat16
VMEM_LIMIT = 56 * 1024 * 1024
MIXER_VMEM = 24 * 1024 * 1024
BACK_VMEM = 40 * 1024 * 1024


def sigmoid(v):
    return 0.5 * jnp.tanh(0.5 * v) + 0.5


def dot_nn(a, b):
    return lax.dot_general(a, b, (((1,), (0,)), ((), ())), preferred_element_type=F32)


def dot_nt(a, b):
    return lax.dot_general(a, b, (((1,), (1,)), ((), ())), preferred_element_type=F32)


def dot_sums(ones, columns, heads):
    high = columns.astype(BF16).astype(F32)
    middle = (columns - high).astype(BF16).astype(F32)
    low = columns - high - middle
    packed = high + pltpu.roll(middle, heads, 1) + pltpu.roll(low, 2 * heads, 1)
    sums = dot_nn(ones.astype(BF16), packed.astype(BF16))
    return sums + pltpu.roll(sums, LANES - heads, 1) + pltpu.roll(sums, LANES - 2 * heads, 1)


def split(a):
    high = a.astype(BF16)
    return high, (a - high.astype(F32)).astype(BF16)


def dot3(a, b, dot=dot_nn):
    return dot(a[0], b[0]) + (dot(a[1], b[0]) + dot(a[0], b[1]))


def tri(shape, keep):
    rows = lax.broadcasted_iota(jnp.int32, shape, 0)
    cols = lax.broadcasted_iota(jnp.int32, shape, 1)
    return keep(rows, cols)


def expand(columns, spread, heads):
    high = columns.astype(BF16).astype(F32)
    rest = columns - high
    packed = high + pltpu.roll(rest, heads, 1)
    return dot_nn(packed.astype(BF16), spread)


def step_terms(pre_dt, slab, channels, heads, spread):
    lane = lax.broadcasted_iota(jnp.int32, pre_dt.shape, 1)
    live = lane < heads
    arg = pre_dt + slab[5:6, channels : channels + LANES]
    dt = jnp.where(live, jnp.maximum(arg, 0.0) + jnp.log1p(jnp.exp(-jnp.abs(arg))), 0.0)
    decay = slab[6:7, channels : channels + LANES]
    lower = tri((CHUNK, CHUNK), lambda r, c: r >= c).astype(F32)
    cum = dot_sums(lower, dt * decay, heads)
    last = cum[CHUNK - 1 : CHUNK, :]
    grown = jnp.where(live, jnp.exp(cum), 0.0)
    left = jnp.where(live, jnp.exp(last - cum), 0.0)
    wide = expand(jnp.concatenate([dt, grown, left], axis=0), spread, heads)
    return arg, dt, decay, cum, wide[:CHUNK], wide[CHUNK : 2 * CHUNK], wide[2 * CHUNK :]


def conv_rows(buffer, slab):
    out = slab[4:5, :] + slab[CONV - 1 : CONV, :] * buffer[HALO : HALO + CHUNK, :]
    for k in range(CONV - 1):
        first = HALO - (CONV - 1) + k
        out = out + slab[k : k + 1, :] * buffer[first : first + CHUNK, :]
    return out


def forward_kernel(
    gate, rest, tail, start, slab, spread, u, sq, y, entering, leaving, state, buffer, *, channels, heads
):
    step = pl.program_id(0)
    size = channels + 2 * LANES

    @pl.when(step == 0)
    def _():
        state[...] = start[...]
        buffer[0:HALO, :] = tail[...]

    @pl.when(step > 0)
    def _():
        buffer[0:HALO, :] = buffer[CHUNK : CHUNK + HALO, :]

    buffer[HALO:, :] = rest[:, :size]
    entering[0] = state[...]
    conv = conv_rows(buffer, slab)
    act = conv * sigmoid(conv)
    xs = act[:, :channels]
    in_map = act[:, channels : channels + LANES]
    out_map = act[:, channels + LANES :]
    arg, dt, decay, cum, dt_w, grown_w, left_w = step_terms(
        rest[:, size:], slab, channels, heads, spread[...]
    )
    cum_t = cum.T
    xt = xs * dt_w
    xt_s = split(xt)
    out_s = split(out_map)
    scores = dot3(out_s, split(in_map), dot_nt)
    held = state[...]
    base = grown_w * dot3(out_s, split(held)) + slab[6:7, :channels] * xs
    state[...] = held * grown_w[CHUNK - 1 : CHUNK, :] + dot3(
        split(in_map.T), split(xt * left_w)
    )
    causal = tri((CHUNK, CHUNK), lambda r, c: r >= c)
    first_half = lax.broadcasted_iota(jnp.int32, (CHUNK, LANES), 1) < LANES // 2
    zero = jnp.zeros((CHUNK, LANES), BF16)
    for pair in range(channels // LANES):
        cols = slice(pair * LANES, (pair + 1) * LANES)
        mats = []
        for h in (2 * pair, 2 * pair + 1):
            gap = cum[:, h : h + 1] - cum_t[h : h + 1, :]
            mats.append(scores * jnp.exp(jnp.where(causal, gap, NEG)))
        stacked = tuple(
            jnp.concatenate(
                [jnp.where(first_half, xp[:, cols], zero), jnp.where(first_half, zero, xp[:, cols])],
                axis=0,
            )
            for xp in xt_s
        )
        y[:, cols] = base[:, cols] + dot3(split(jnp.concatenate(mats, axis=1)), stacked)
    z = gate[...]
    gated = y[...] * (z * sigmoid(z))
    sq[...] = jnp.sum(gated * gated, axis=1, keepdims=True)
    u[...] = (gated * slab[5:6, :channels]).astype(BF16)

    @pl.when(step == pl.num_programs(0) - 1)
    def _():
        leaving[...] = state[...]


def backward_kernel(
    q,
    factor,
    gate,
    rest,
    before,
    tail,
    y,
    entering,
    grad_start,
    e_start,
    slab,
    spread,
    gather,
    gpre,
    grad_leaving,
    e_leaving,
    sums,
    grad,
    buffer,
    e_buffer,
    *,
    channels,
    heads,
):
    step = pl.program_id(0)
    steps = pl.num_programs(0)
    size = channels + 2 * LANES

    @pl.when(step == 0)
    def _():
        grad[...] = grad_start[...]
        e_buffer[CHUNK:, :] = e_start[...]
        sums[...] = jnp.zeros_like(sums)

    @pl.when(step > 0)
    def _():
        e_buffer[CHUNK:, :] = e_buffer[0:HALO, :]

    @pl.when(step == steps - 1)
    def _():
        buffer[0:HALO, :] = tail[...]

    @pl.when(step < steps - 1)
    def _():
        buffer[0:HALO, :] = before[:, :size]

    buffer[HALO:, :] = rest[:, :size]
    conv = conv_rows(buffer, slab)
    sig = sigmoid(conv)
    act = conv * sig
    d_act = sig * (1.0 + conv * (1.0 - sig))
    xs = act[:, :channels]
    in_map = act[:, channels : channels + LANES]
    out_map = act[:, channels + LANES :]
    arg, dt, decay, cum, dt_w, grown_w, left_w = step_terms(
        rest[:, size:], slab, channels, heads, spread[...]
    )
    cum_t = cum.T

    z = gate[...]
    sig_z = sigmoid(z)
    silu_z = z * sig_z
    yv = y[...]
    gated = yv * silu_z
    qv = q[...] * factor[:, 0:1]
    sums[5:6, :channels] += jnp.sum(qv * gated, axis=0, keepdims=True)
    g_gated = qv * slab[5:6, :channels] - gated * factor[:, 1:2]
    gpre[:, :channels] = (g_gated * yv * (sig_z * (1.0 + z * (1.0 - sig_z)))).astype(BF16)
    gy = g_gated * silu_z
    gy_b = gy.astype(BF16)
    skip_row = jnp.sum(gy * xs, axis=0, keepdims=True)

    xt = xs * dt_w
    xt_b = xt.astype(BF16)
    in_b = in_map.astype(BF16)
    out_b = out_map.astype(BF16)
    held = entering[0]
    held_b = held.astype(BF16)
    g_state = grad[...]
    g_state_b = g_state.astype(BF16)
    grown_last = grown_w[CHUNK - 1 : CHUNK, :]

    from_state = grown_w * dot_nn(out_b, held_b)
    ge_b = (grown_w * gy).astype(BF16)
    g_out_map = dot_nt(ge_b, held_b)
    g_xt = left_w * dot_nn(in_b, g_state_b)
    g_in_map = dot_nt((xt * left_w).astype(BF16), g_state_b)
    through = jnp.sum(g_state * held, axis=0, keepdims=True) * grown_last
    grad[...] = g_state * grown_last + dot_nn(out_map.T.astype(BF16), ge_b)
    row_terms = gy * from_state
    col_terms = xt * g_xt

    scores_t = dot3(split(in_map), split(out_map), dot_nt)
    later = tri((CHUNK, CHUNK), lambda r, c: c >= r)
    first_half = lax.broadcasted_iota(jnp.int32, (CHUNK, LANES), 1) < LANES // 2
    lane = lax.broadcasted_iota(jnp.int32, (CHUNK, LANES), 1)
    zero = jnp.zeros((CHUNK, LANES), BF16)
    g_scores_t = jnp.zeros((CHUNK, CHUNK), F32)
    gap_rows = []
    gap_cols = jnp.zeros((CHUNK, LANES), F32)
    g_xt_parts = []
    for pair in range(channels // LANES):
        cols = slice(pair * LANES, (pair + 1) * LANES)
        gp = gy_b[:, cols]
        stacked = jnp.concatenate(
            [jnp.where(first_half, gp, zero), jnp.where(first_half, zero, gp)], axis=0
        )
        g_mats = dot_nt(xt_b[:, cols], stacked)
        mats = []
        for number in range(2):
            h = 2 * pair + number
            gap = cum_t[h : h + 1, :] - cum[:, h : h + 1]
            weight = jnp.exp(jnp.where(later, gap, NEG))
            mats.append((scores_t * weight).astype(BF16))
            g_score = g_mats[:, number * CHUNK : (number + 1) * CHUNK] * weight
            g_scores_t = g_scores_t + g_score
            g_gap = g_score * scores_t
            gap_rows.append(jnp.sum(g_gap, axis=0, keepdims=True))
            gap_cols = jnp.where(lane == h, jnp.sum(g_gap, axis=1, keepdims=True), gap_cols)
        g_xt_parts.append(g_xt[:, cols] + dot_nn(jnp.concatenate(mats, axis=1), stacked))
    g_xt = jnp.concatenate(g_xt_parts, axis=1)
    g_scores_b = g_scores_t.astype(BF16)
    g_in_map = g_in_map + dot_nn(g_scores_b, out_b)
    g_out_map = g_out_map + dot_nn(g_scores_t.T.astype(BF16), in_b)
    g_xs = slab[6:7, :channels] * gy + dt_w * g_xt

    pad = jnp.zeros((CHUNK - heads, CHUNK), F32)
    gap_rows_t = jnp.concatenate(gap_rows + [pad], axis=0).T
    packed = jnp.concatenate(
        [
            xs * g_xt,
            row_terms,
            col_terms,
            jnp.broadcast_to(through, (HALO, channels)),
            jnp.broadcast_to(skip_row, (HALO, channels)),
        ],
        axis=0,
    )
    high, rest = split(packed)
    grouped = dot_nn(high, gather[...]) + dot_nn(rest, gather[...])
    direct = grouped[:CHUNK]
    row_sum = grouped[CHUNK : 2 * CHUNK]
    col_sum = grouped[2 * CHUNK : 3 * CHUNK]
    through_sum = grouped[3 * CHUNK : 3 * CHUNK + 1]
    sums[7:8, channels : channels + LANES] += grouped[3 * CHUNK + HALO : 3 * CHUNK + HALO + 1]
    upper = tri((CHUNK, CHUNK), lambda r, c: c >= r).astype(F32)
    below = tri((CHUNK, CHUNK), lambda r, c: r > c).astype(F32)
    g_log = (
        dot_sums(upper, gap_rows_t - gap_cols + row_sum, heads)
        + dot_sums(below, col_sum, heads)
        + through_sum
    )
    g_dt = direct + g_log * decay
    g_dtin = jnp.where(lane < heads, g_dt * sigmoid(arg), 0.0)
    sums[5:6, channels : channels + LANES] += jnp.sum(g_dtin, axis=0, keepdims=True)
    sums[6:7, channels : channels + LANES] += decay * jnp.sum(dt * g_log, axis=0, keepdims=True)

    e = jnp.concatenate([g_xs, g_in_map, g_out_map], axis=1) * d_act
    e_buffer[0:CHUNK, :] = e
    sums[4:5, :] += jnp.sum(e, axis=0, keepdims=True)
    for k in range(CONV):
        first = HALO - (CONV - 1) + k
        sums[k : k + 1, :] += jnp.sum(e * buffer[first : first + CHUNK, :], axis=0, keepdims=True)
    g_pre = slab[CONV - 1 : CONV, :] * e
    for k in range(CONV - 1):
        first = CONV - 1 - k
        g_pre = g_pre + slab[k : k + 1, :] * e_buffer[first : first + CHUNK, :]
    gpre[:, channels : channels + size] = g_pre.astype(BF16)
    gpre[:, channels + size :] = g_dtin.astype(BF16)

    @pl.when(step == steps - 1)
    def _():
        grad_leaving[...] = grad[...]
        e_leaving[...] = e_buffer[0:HALO, :]


def fixed(shape):
    return pl.BlockSpec(shape, lambda i: (0,) * len(shape))


def mixer_forward(gate, rest, tail, start, slab, spread, heads):
    rows, width = rest.shape
    state_size, channels = start.shape
    size = channels + 2 * LANES
    steps = rows // CHUNK
    by_row = lambda cols: pl.BlockSpec((CHUNK, cols), lambda i: (i, 0))
    shape = jax.ShapeDtypeStruct

    def body(*refs):
        forward_kernel(*refs, channels=channels, heads=heads)

    return pl.pallas_call(
        body,
        grid=(steps,),
        in_specs=[
            by_row(channels),
            by_row(width),
            fixed((HALO, size)),
            fixed(start.shape),
            fixed(slab.shape),
            fixed(spread.shape),
        ],
        out_specs=[
            by_row(channels),
            by_row(1),
            by_row(channels),
            pl.BlockSpec((1, state_size, channels), lambda i: (i, 0, 0)),
            fixed(start.shape),
        ],
        out_shape=[
            shape((rows, channels), BF16),
            shape((rows, 1), F32),
            shape((rows, channels), F32),
            shape((steps, state_size, channels), F32),
            shape(start.shape, F32),
        ],
        scratch_shapes=[
            pltpu.VMEM((state_size, channels), F32),
            pltpu.VMEM((CHUNK + HALO, size), F32),
        ],
        compiler_params=pltpu.CompilerParams(
            dimension_semantics=("arbitrary",), vmem_limit_bytes=MIXER_VMEM
        ),
        cost_estimate=pl.CostEstimate(flops=1000, bytes_accessed=1000, transcendentals=0),
        name="mixer_forward",
    )(gate, rest, tail, start, slab, spread)


def mixer_backward(
    q, factor, gate, rest, tail, y, entering, grad, e_rows, slab, spread, gather, heads, grant
):
    rows, width = rest.shape
    state_size, channels = grad.shape
    size = channels + 2 * LANES
    steps = rows // CHUNK
    by_row = lambda cols: pl.BlockSpec((CHUNK, cols), lambda i: (steps - 1 - i, 0))
    shape = jax.ShapeDtypeStruct
    groups = CHUNK // HALO

    def body(*refs):
        backward_kernel(*refs, channels=channels, heads=heads)

    return pl.pallas_call(
        body,
        grid=(steps,),
        in_specs=[
            by_row(channels),
            by_row(2),
            by_row(channels),
            by_row(width),
            pl.BlockSpec(
                (HALO, width), lambda i: (jnp.maximum((steps - 1 - i) * groups - 1, 0), 0)
            ),
            fixed((HALO, size)),
            by_row(channels),
            pl.BlockSpec((1, state_size, channels), lambda i: (steps - 1 - i, 0, 0)),
            fixed(grad.shape),
            fixed(e_rows.shape),
            fixed(slab.shape),
            fixed(spread.shape),
            fixed(gather.shape),
        ],
        out_specs=[
            by_row(channels + width),
            fixed(grad.shape),
            fixed(e_rows.shape),
            fixed(slab.shape),
        ],
        out_shape=[
            shape((rows, channels + width), BF16),
            shape(grad.shape, F32),
            shape(e_rows.shape, F32),
            shape(slab.shape, F32),
        ],
        scratch_shapes=[
            pltpu.VMEM((state_size, channels), F32),
            pltpu.VMEM((CHUNK + HALO, size), F32),
            pltpu.VMEM((CHUNK + HALO, size), F32),
        ],
        compiler_params=pltpu.CompilerParams(
            dimension_semantics=("arbitrary",), vmem_limit_bytes=grant
        ),
        cost_estimate=pl.CostEstimate(flops=1000, bytes_accessed=1000, transcendentals=0),
        name="mixer_backward",
    )(q, factor, gate, rest, rest, tail, y, entering, grad, e_rows, slab, spread, gather)


def finish_kernel(first_own, first_other, second_own, second_other, gates, *, channels):
    core = lax.axis_index("section")

    def write(low, high):
        for half, source in enumerate((low, high)):
            value = source[...].astype(F32)
            for k in range(2):
                gates[:, k, half * channels : (half + 1) * channels] = value[
                    :, k * channels : (k + 1) * channels
                ]

    @pl.when(core == 0)
    def _():
        write(first_own, first_other)

    @pl.when(core == 1)
    def _():
        write(second_other, second_own)


def join_halves(first_own, first_other, second_own, second_other, channels):
    rows = first_own.shape[0]
    step = 32
    block = pl.BlockSpec((step, 2 * channels), lambda i: (i, 0))
    return pl.pallas_call(
        functools.partial(finish_kernel, channels=channels),
        grid=(rows // step,),
        in_specs=[block] * 4,
        out_specs=pl.BlockSpec((step, 2, 2 * channels), lambda i: (i, 0, 0)),
        out_shape=jax.ShapeDtypeStruct((rows, 2, 2 * channels), F32),
        compiler_params=pltpu.CompilerParams(
            dimension_semantics=("arbitrary",), vmem_limit_bytes=MIXER_VMEM
        ),
        cost_estimate=pl.CostEstimate(flops=1000, bytes_accessed=1000, transcendentals=0),
        name="join_halves",
    )(first_own, first_other, second_own, second_other)


MESH = pl.DeviceIdType.MESH
DEEP = 4
SIDEWAYS = 32
SIDE_ROWS = 48


def place_in_line():
    core, line, half = lax.axis_index("section"), lax.axis_index("fsdp"), lax.axis_index("tp")
    deep, side = line // 2, line % 2

    def device(z, x):
        return (core, z * 2 + x, half)

    return deep, side, device


def greet_all():
    core, line, half = lax.axis_index("section"), lax.axis_index("fsdp"), lax.axis_index("tp")
    barrier = pltpu.get_barrier_semaphore()

    def greet(target):
        pl.semaphore_signal(barrier, inc=1, device_id=target, device_id_type=MESH)

    greet((core, line, 1 - half))
    greet((1 - core, line, half))
    for step in range(1, 2 * DEEP):
        greet((core, (line + step) % (2 * DEEP), half))
    pl.semaphore_wait(barrier, 2 * DEEP + 1)


def gather_steps(shards, wholes, sems, beside):
    count = len(shards)
    local_sem, x_send, x_recv, up_send, up_recv, down_send, down_recv = sems[:7]
    side_send, side_recv, pair_up_send, pair_up_recv, pair_down_send, pair_down_recv = sems[7:]
    deep, side, device = place_in_line()
    above, below = jnp.minimum(deep + 1, DEEP - 1), jnp.maximum(deep - 1, 0)
    has_above, has_below = deep < DEEP - 1, deep > 0
    main = [pl.ds(0, shard.shape[0] - SIDE_ROWS) for shard in shards]
    rest = [pl.ds(shard.shape[0] - SIDE_ROWS, SIDE_ROWS) for shard in shards]

    def remote(source, place, send, recv, target):
        return pltpu.make_async_remote_copy(
            src_ref=source,
            dst_ref=place,
            send_sem=send,
            recv_sem=recv,
            device_id=target,
            device_id_type=MESH,
        )

    def own(i):
        return pltpu.make_async_copy(shards[i], wholes[i].at[deep * 2 + side], local_sem.at[i])

    def block(i, z, x=None):
        return wholes[i].at[z * 2 + (side if x is None else x), main[i]]

    def across(i, z, source=None):
        source = block(i, z) if source is None else source
        target = device(deep, 1 - side)
        return remote(source, block(i, z), x_send.at[i, z], x_recv.at[i, z], target)

    def upward(i, k, source=None):
        place = block(i, deep - k)
        source = place if source is None else source
        return remote(source, place, up_send.at[i, k], up_recv.at[i, k], device(above, side))

    def downward(i, k, source=None):
        place = block(i, deep + k)
        source = place if source is None else source
        return remote(source, place, down_send.at[i, k], down_recv.at[i, k], device(below, side))

    def sideways(i, x):
        place = wholes[i].at[deep * 2 + x, rest[i]]
        source = shards[i].at[rest[i]]
        return remote(source, place, side_send.at[i], side_recv.at[i], device(deep, 1 - side))

    def pair(i, z):
        return wholes[i].at[pl.ds(z * 2, 2), rest[i]]

    def pair_up(i, k):
        place = pair(i, deep - k)
        return remote(place, place, pair_up_send.at[i, k], pair_up_recv.at[i, k], device(above, side))

    def pair_down(i, k):
        place = pair(i, deep + k)
        return remote(
            place, place, pair_down_send.at[i, k], pair_down_recv.at[i, k], device(below, side)
        )

    for i in range(count):
        own(i).start()
        sideways(i, side).start()
    for i in range(count):
        source = shards[i].at[main[i]]

        @pl.when(has_above)
        def _(i=i, source=source):
            upward(i, 0, source).start()

        @pl.when(has_below)
        def _(i=i, source=source):
            downward(i, 0, source).start()

        across(i, deep, source).start()
    beside(0)
    here = device(deep, side)
    for k in range(1, DEEP):
        for i in range(count):

            @pl.when(deep >= k)
            def _(i=i, k=k):
                place = block(i, deep - k)
                remote(place, place, up_send.at[i, k - 1], up_recv.at[i, k - 1], here).wait_recv()

                @pl.when(has_above)
                def _():
                    upward(i, k).start()

                across(i, deep - k).start()

            @pl.when(deep + k <= DEEP - 1)
            def _(i=i, k=k):
                place = block(i, deep + k)
                remote(place, place, down_send.at[i, k - 1], down_recv.at[i, k - 1], here).wait_recv()

                @pl.when(has_below)
                def _():
                    downward(i, k).start()

                across(i, deep + k).start()

        if k == DEEP - 2:
            for i in range(count):
                own(i).wait()
                sideways(i, 1 - side).wait_recv()

                @pl.when(has_above)
                def _(i=i):
                    pair_up(i, 0).start()

                @pl.when(has_below)
                def _(i=i):
                    pair_down(i, 0).start()

        beside(k)

    for k in range(1, DEEP):
        for i in range(count):

            @pl.when(deep >= k)
            def _(i=i, k=k):
                place = pair(i, deep - k)
                remote(
                    place, place, pair_up_send.at[i, k - 1], pair_up_recv.at[i, k - 1], here
                ).wait_recv()

                @pl.when(has_above)
                def _():
                    pair_up(i, k).start()

            @pl.when(deep + k <= DEEP - 1)
            def _(i=i, k=k):
                place = pair(i, deep + k)
                remote(
                    place, place, pair_down_send.at[i, k - 1], pair_down_recv.at[i, k - 1], here
                ).wait_recv()

                @pl.when(has_below)
                def _():
                    pair_down(i, k).start()

    for i in range(count):
        sideways(i, side).wait_send()
        for z in range(DEEP):
            other = remote(
                block(i, z), block(i, z, 1 - side), x_send.at[i, z], x_recv.at[i, z], here
            )
            other.wait_send()
            other.wait_recv()
        for k in range(DEEP - 1):

            @pl.when(has_above & (deep >= k))
            def _(i=i, k=k):
                upward(i, k).wait_send()
                pair_up(i, k).wait_send()

            @pl.when(has_below & (deep + k <= DEEP - 1))
            def _(i=i, k=k):
                downward(i, k).wait_send()
                pair_down(i, k).wait_send()


def start_kernel(*refs, count, micros, heads, gain_rows):
    shards, (gain, own, cotangent) = refs[:count], refs[count : count + 3]
    params, spread = refs[count + 3 : count + 9], refs[count + 9]
    outs = refs[count + 10 :]
    wholes, (gains, slabs), targets = outs[:count], outs[count : count + 2], outs[count + 2 :]
    targets, scratch = targets[: 2 * micros], targets[2 * micros :]
    gain_send, gain_recv, own_sem, y_send, y_recv, core_send, core_recv, rows_out = scratch[13:21]
    other_slab, slab_send, slab_recv, line_send, line_recv = scratch[21:]
    core, line, half = lax.axis_index("section"), lax.axis_index("fsdp"), lax.axis_index("tp")
    lines = 2 * DEEP

    greet_all()
    across_tp, across_core = (core, line, 1 - half), (1 - core, line, half)

    def send_gain(step):
        return pltpu.make_async_remote_copy(
            src_ref=gain,
            dst_ref=gains.at[core, line],
            send_sem=gain_send.at[step],
            recv_sem=gain_recv.at[step],
            device_id=(core, (line + step) % lines, half),
            device_id_type=MESH,
        )

    for step in range(1, lines):
        send_gain(step).start()

    tokens = own.shape[1] // 2
    mine = pl.ds(pl.multiple_of(core * tokens, tokens), tokens)

    def token_copies(n):
        m = n % micros
        source = rows_out.at[pl.ds(m * tokens, tokens)] if n < micros else cotangent.at[m, mine]
        place = targets[n].at[half, core]
        later = targets[n].at[1 - half, core]
        more = 2 * micros + n
        remote = functools.partial(pltpu.make_async_remote_copy, device_id_type=MESH)
        return (
            pltpu.make_async_copy(source, place, own_sem.at[n]),
            remote(source, place, y_send.at[n], y_recv.at[n], device_id=across_tp),
            remote(source, place, core_send.at[n], core_recv.at[n], device_id=across_core),
            remote(later, later, core_send.at[more], core_recv.at[more], device_id=across_core),
        )

    send_slab = pltpu.make_async_remote_copy(
        src_ref=other_slab,
        dst_ref=slabs.at[core],
        send_sem=slab_send.at[0],
        recv_sem=slab_recv.at[0],
        device_id=across_core,
        device_id_type=MESH,
    )
    send_line = pltpu.make_async_remote_copy(
        src_ref=gains.at[core],
        dst_ref=gains.at[core],
        send_sem=line_send.at[0],
        recv_sem=line_recv.at[0],
        device_id=across_core,
        device_id_type=MESH,
    )

    def write_slab(place, index):
        taps, bias, shared_taps, shared_bias, gate, per_head = (v[...] for v in params)
        channels = spread.shape[1]
        first = index == 0
        cut = lambda v: jnp.where(first, v[:, :channels], v[:, channels:])
        lane = lax.broadcasted_iota(jnp.int32, per_head.shape, 1)
        here = jnp.where(first, per_head, pltpu.roll(per_head, LANES - heads, 1))
        here = jnp.where(lane < heads, here, 0.0)
        skip = expand(here, spread[...], heads)
        decay = jnp.where(lane < heads, -jnp.exp(here), 0.0)
        place[...] = jnp.zeros(place.shape, F32)
        place[0:CONV, :channels] = cut(taps)
        place[0:CONV, channels:] = shared_taps
        place[CONV : CONV + 1, :channels] = cut(bias)
        place[CONV : CONV + 1, channels:] = shared_bias
        place[5:6, :channels] = cut(gate)
        place[5:6, channels : channels + LANES] = here[0:1]
        place[6:7, :channels] = skip[2:3]
        place[6:7, channels : channels + LANES] = decay[1:2]

    def send_tokens(stage):
        if stage == 0:
            send_first()
        elif stage <= 2:
            for n in range((stage - 1) * micros, stage * micros):
                token_copies(n)[1].wait_recv()
                token_copies(n)[3].start()
            if stage == 1:
                for n in range(micros, 2 * micros):
                    for copy in token_copies(n)[:3]:
                        copy.start()

    def send_first():
        write_slab(other_slab, 1 - core)
        send_slab.start()
        write_slab(slabs.at[core], core)
        gains[core, line] = gain[...]
        for step in range(1, lines):
            send_gain(step).wait()
        send_line.start()
        send_line.wait()
        gain_row = jnp.concatenate(
            [gains[0, f, j : j + 1, :] for f in range(lines) for j in range(gain_rows)], axis=1
        )
        for m in range(micros):
            h = own[m, mine].astype(F32)
            scale = lax.rsqrt(jnp.mean(h * h, axis=1, keepdims=True) + EPS)
            rows_out[m * tokens : (m + 1) * tokens] = (h * scale * gain_row).astype(BF16)

        for n in range(micros):
            for copy in token_copies(n)[:3]:
                copy.start()

    gather_steps(shards, wholes, scratch[:13], send_tokens)
    send_slab.wait()
    for n in range(2 * micros):
        own_copy, y_copy, core_copy, core_later = token_copies(n)
        own_copy.wait()
        y_copy.wait_send()
        core_copy.wait()
        core_later.wait()


def start_gather(shards, gain, own, cotangent, params, spread, micros, heads, gain_rows):
    count = len(shards)
    lines = 2 * DEEP
    pairs = pltpu.SemaphoreType.DMA((count, DEEP))
    dma = lambda n: pltpu.SemaphoreType.DMA((n,))
    shape = jax.ShapeDtypeStruct
    anywhere = pl.BlockSpec(memory_space=pl.ANY)
    vmem = pl.BlockSpec(memory_space=pltpu.VMEM)
    rows, width = own.shape[0] * own.shape[1] // 2, own.shape[2]
    slab = (8, spread.shape[1] + params[2].shape[1])
    return pl.pallas_call(
        functools.partial(
            start_kernel, count=count, micros=micros, heads=heads, gain_rows=gain_rows
        ),
        out_shape=[shape((lines,) + v.shape, v.dtype) for v in shards]
        + [
            shape((2, lines) + gain.shape, F32),
            shape((2,) + slab, F32),
        ]
        + [shape((2, 2, rows // micros, width), BF16)] * (2 * micros),
        in_specs=[anywhere] * count + [vmem, vmem, anywhere] + [vmem] * 7,
        out_specs=[anywhere] * count + [vmem, vmem] + [anywhere] * (2 * micros),
        scratch_shapes=[dma(count)]
        + [pairs] * 6
        + [dma(count)] * 2
        + [pairs] * 4
        + [dma(lines)] * 2
        + [dma(2 * micros)] * 3
        + [dma(4 * micros)] * 2
        + [pltpu.VMEM((rows, width), BF16), pltpu.VMEM(slab, F32)]
        + [dma(1)] * 4,
        compiler_params=pltpu.CompilerParams(
            collective_id=1, has_side_effects=True, vmem_limit_bytes=VMEM_LIMIT
        ),
        cost_estimate=pl.CostEstimate(flops=170_000_000_000, bytes_accessed=1000, transcendentals=0),
        name="start_gather",
    )(*shards, gain, own, cotangent, *params, spread)


def add_rows(out, *parts):
    rows = out.shape[0]
    step = 16

    def body(n, _):
        at = pl.ds(pl.multiple_of(n * step, step), step)
        total = parts[0][at].astype(F32)
        for part in parts[1:]:
            total = total + part[at].astype(F32)
        out[at] = total.astype(out.dtype)
        return 0

    lax.fori_loop(0, rows // step, body, 0)


X_ORDER = ((3, 2, 1, 0), (3, 0, 2, 1), (0, 3, 1, 2), (0, 1, 2, 3))


def reduce_kernel(*refs, count):
    parts, small, results = refs[:count], refs[count], refs[count + 1 : 2 * count + 1]
    others = refs[2 * count + 1 : 3 * count + 1]
    own_small, next_small, both_small = refs[3 * count + 1 : 3 * count + 4]
    scratch = refs[3 * count + 4 :]
    held, crossed, from_below, from_above, pairs, pairs_below, pairs_above, side_in = (
        scratch[n * count : (n + 1) * count] for n in range(8)
    )
    sems = scratch[8 * count : -5]
    load_sem, x_send, x_recv, up_send, up_recv, down_send, down_recv = sems[:7]
    pair_sem, pair_up_send, pair_up_recv, pair_down_send, pair_down_recv = sems[7:12]
    side_send, side_recv = sems[12:]
    small_buffer, small_send, small_recv, other_send, other_recv = scratch[-5:]
    main = [result.shape[0] - SIDEWAYS for result in results]
    deep, side, device = place_in_line()
    core, line, half = lax.axis_index("section"), lax.axis_index("fsdp"), lax.axis_index("tp")
    greet_all()
    across_core = (1 - core, line, half)
    partners = [
        device(deep, 1 - side),
        device(deep + 1 - 2 * (deep % 2), side),
        device((deep + 2) % DEEP, side),
        (core, line, 1 - half),
        across_core,
        across_core,
    ]

    def swap_small(n, source, target):
        return pltpu.make_async_remote_copy(
            src_ref=source,
            dst_ref=target,
            send_sem=small_send.at[n],
            recv_sem=small_recv.at[n],
            device_id=partners[n],
            device_id_type=MESH,
        )

    def sum_small():
        for n in range(3):
            copy = swap_small(n, small if n == 0 else small_buffer.at[n - 1], small_buffer.at[3 + n])
            if n > 0:
                copy.start()
            copy.wait()
            value = small[...] if n == 0 else small_buffer[n - 1]
            small_buffer[n] = value + small_buffer[3 + n]

    def spread_small():
        over_tp = swap_small(3, small_buffer.at[2], small_buffer.at[6])
        over_core = swap_small(4, small_buffer.at[2, 1 - core], next_small)
        over_tp.start()
        over_core.start()
        own_small[...] = small_buffer[2, core]
        over_tp.wait()
        small_buffer[7] = small_buffer[2] + small_buffer[6]
        last = swap_small(5, small_buffer.at[7, 1 - core], small_buffer.at[8, 0])
        last.start()
        last.wait()
        both_small[...] = small_buffer[7, core] + small_buffer[8, 0]
        over_core.wait()

    def rows(i, z, x):
        return parts[i].at[z * 2 + x, pl.ds(0, main[i])]

    def load_pair(i, z):
        source = parts[i].at[pl.ds(z * 2, 2), pl.ds(main[i], SIDEWAYS)]
        return pltpu.make_async_copy(source, pairs[i].at[z], pair_sem.at[i, z])

    def pair_along(i, k, z, here, up):
        send, recv = (pair_up_send, pair_up_recv) if up else (pair_down_send, pair_down_recv)
        target = min(here + 1, DEEP - 1) if up else max(here - 1, 0)
        return pltpu.make_async_remote_copy(
            src_ref=pairs[i].at[z],
            dst_ref=(pairs_below if up else pairs_above)[i].at[k - 1],
            send_sem=send.at[i, k - 1],
            recv_sem=recv.at[i, k - 1],
            device_id=device(target, side),
            device_id_type=MESH,
        )

    def sideways(i, here):
        return pltpu.make_async_remote_copy(
            src_ref=pairs[i].at[here, 1 - side],
            dst_ref=side_in[i],
            send_sem=side_send.at[i],
            recv_sem=side_recv.at[i],
            device_id=device(deep, 1 - side),
            device_id_type=MESH,
        )

    def load(i, z):
        return pltpu.make_async_copy(rows(i, z, side), held[i].at[z], load_sem.at[i, z])

    def across(i, z):
        return pltpu.make_async_remote_copy(
            src_ref=rows(i, z, 1 - side),
            dst_ref=crossed[i].at[z],
            send_sem=x_send.at[i, z],
            recv_sem=x_recv.at[i, z],
            device_id=device(deep, 1 - side),
            device_id_type=MESH,
        )

    def upward(i, k, z, here):
        return pltpu.make_async_remote_copy(
            src_ref=held[i].at[z],
            dst_ref=from_below[i].at[k - 1],
            send_sem=up_send.at[i, k - 1],
            recv_sem=up_recv.at[i, k - 1],
            device_id=device(min(here + 1, DEEP - 1), side),
            device_id_type=MESH,
        )

    def downward(i, k, z, here):
        return pltpu.make_async_remote_copy(
            src_ref=held[i].at[z],
            dst_ref=from_above[i].at[k - 1],
            send_sem=down_send.at[i, k - 1],
            recv_sem=down_recv.at[i, k - 1],
            device_id=device(max(here - 1, 0), side),
            device_id_type=MESH,
        )

    def to_other(i):
        return pltpu.make_async_remote_copy(
            src_ref=results[i],
            dst_ref=others[i],
            send_sem=other_send.at[i],
            recv_sem=other_recv.at[i],
            device_id=across_core,
            device_id_type=MESH,
        )

    def at_depth(here):
        order = X_ORDER[here]
        last = DEEP - 1
        started = []

        def send_across(number):
            for i in range(count):
                across(i, order[number]).start()

        def take(number):
            z = order[number]
            for i in range(count):
                across(i, z).wait_recv()
            if number + 2 < DEEP:
                send_across(number + 2)
            for i in range(count):
                load(i, z).wait()
                add_rows(held[i].at[z], held[i].at[z], crossed[i].at[z])

        def relay(k, up):
            z = DEEP - k + here if up else here + k - DEEP
            first = here == 0 if up else here == last
            for i in range(count):
                if not first:
                    make = upward if up else downward
                    back = from_below if up else from_above
                    make(i, k - 1, z, here).wait_recv()
                    add_rows(held[i].at[z], held[i].at[z], back[i].at[k - 2])
                copy = (upward if up else downward)(i, k, z, here)
                copy.start()
                started.append(copy)

        swap_small(0, small, small_buffer.at[3]).start()
        send_across(0)
        send_across(1)
        for number in range(DEEP):
            for i in range(count):
                load_pair(i, order[number]).start()
        for number in range(DEEP):
            for i in range(count):
                load(i, order[number]).start()

        def relay_pair(k, up):
            z = DEEP - k + here if up else here + k - DEEP
            if not 0 <= z < DEEP or z == here or (z < here) == up:
                return
            for i in range(count):
                load_pair(i, z).wait()
                if here != (0 if up else last):
                    pair_along(i, k - 1, z, here, up).wait_recv()
                    back = (pairs_below if up else pairs_above)[i]
                    for x in range(2):
                        add_rows(pairs[i].at[z, x], pairs[i].at[z, x], back.at[k - 2, x])
                copy = pair_along(i, k, z, here, up)
                copy.start()
                started.append(copy)

        for k in range(1, DEEP):
            relay_pair(k, True)
            relay_pair(k, False)
        sum_small()
        for i in range(count):
            load_pair(i, here).wait()
            for x in range(2):
                terms = [pairs[i].at[here, x]]
                if here > 0:
                    if x == 0:
                        pair_along(i, DEEP - 1, here, here, True).wait_recv()
                    terms.append(pairs_below[i].at[DEEP - 2, x])
                if here < last:
                    if x == 0:
                        pair_along(i, DEEP - 1, here, here, False).wait_recv()
                    terms.append(pairs_above[i].at[DEEP - 2, x])
                add_rows(pairs[i].at[here, x], *terms)
            sideways(i, here).start()
        if here in (0, last):
            up = here == 0
            for k in range(1, DEEP):
                take(k - 1)
                relay(k, up)
            spread_small()
            take(DEEP - 1)
        else:
            up = here == 1
            take(0)
            take(1)
            relay(2, up)
            relay(3, not up)
            take(2)
            relay(3, up)
            spread_small()
            take(3)
        for i in range(count):
            terms = [held[i].at[here]]
            if here > 0:
                upward(i, DEEP - 1, here, here).wait_recv()
                terms.append(from_below[i].at[DEEP - 2])
            if here < last:
                downward(i, DEEP - 1, here, here).wait_recv()
                terms.append(from_above[i].at[DEEP - 2])
            add_rows(results[i].at[pl.ds(0, main[i])], *terms)
            sideways(i, here).wait_recv()
            add_rows(
                results[i].at[pl.ds(main[i], SIDEWAYS)], pairs[i].at[here, side], side_in[i]
            )
            to_other(i).start()
        for i in range(count):
            to_other(i).wait()
            sideways(i, here).wait_send()
        for copy in started:
            copy.wait_send()
        for z in range(DEEP):
            for i in range(count):
                across(i, z).wait_send()

    for here in range(DEEP):

        @pl.when(deep == here)
        def _(here=here):
            at_depth(here)


def reduce_line(parts, small, name, collective_id):
    count = len(parts)
    shards = [(p.shape[0] // (2 * DEEP),) + p.shape[1:] for p in parts]
    pairs = pltpu.SemaphoreType.DMA((count, DEEP))
    sizes = sum(p.size for p in parts)
    blocks = lambda n: [pltpu.VMEM((n, shard[0] - SIDEWAYS, shard[1]), BF16) for shard in shards]
    doubles = lambda n: [pltpu.VMEM((n, 2, SIDEWAYS, shard[1]), BF16) for shard in shards]
    split_parts = [p.reshape((2 * DEEP, -1) + p.shape[1:]) for p in parts]
    shape = jax.ShapeDtypeStruct
    vmem = pl.BlockSpec(memory_space=pltpu.VMEM)
    return pl.pallas_call(
        functools.partial(reduce_kernel, count=count),
        out_shape=[shape(shard, BF16) for shard in shards] * 2 + [shape(small.shape[1:], F32)] * 3,
        in_specs=[pl.BlockSpec(memory_space=pl.ANY)] * count + [vmem],
        out_specs=[vmem] * (2 * count + 3),
        scratch_shapes=blocks(DEEP)
        + blocks(DEEP)
        + blocks(DEEP - 1)
        + blocks(DEEP - 1)
        + doubles(DEEP)
        + doubles(DEEP - 1)
        + doubles(DEEP - 1)
        + [pltpu.VMEM((SIDEWAYS, shard[1]), BF16) for shard in shards]
        + [pairs] * 12
        + [pltpu.SemaphoreType.DMA((count,))] * 2
        + [
            pltpu.VMEM((9,) + small.shape, F32),
            pltpu.SemaphoreType.DMA((6,)),
            pltpu.SemaphoreType.DMA((6,)),
            pltpu.SemaphoreType.DMA((count,)),
            pltpu.SemaphoreType.DMA((count,)),
        ],
        compiler_params=pltpu.CompilerParams(
            collective_id=collective_id, has_side_effects=True, vmem_limit_bytes=VMEM_LIMIT
        ),
        cost_estimate=pl.CostEstimate(flops=1000, bytes_accessed=1000, transcendentals=0),
        name=name,
    )(*split_parts, small)


SWAP = [(0, 1), (1, 0)]


def swap_core(value):
    return lax.ppermute(value, "section", SWAP)


def swap_tp(value):
    return lax.ppermute(value, "tp", SWAP)


def by_index(index, own, other):
    first = index == 0
    return jnp.stack([jnp.where(first, own, other), jnp.where(first, other, own)])


def pick(pair, index):
    return lax.dynamic_index_in_dim(pair, index, 0, keepdims=False)


def gather_tokens(own, core, half, beside=()):
    both = by_index(half, own, after(swap_tp(own), *beside))
    whole = by_index(core, both, swap_core(both))
    whole = jnp.moveaxis(whole, 0, 1)
    return whole.reshape((4 * own.shape[0],) + own.shape[1:])


def after(value, *others):
    return lax.optimization_barrier((value,) + others)[0] if others else value


def over_cores(part, core, *beside):
    split_rows = part.reshape((2, 2, part.shape[0] // 4) + part.shape[1:])
    mine = lax.dynamic_index_in_dim(split_rows, core, 1, keepdims=False)
    theirs = lax.dynamic_index_in_dim(split_rows, 1 - core, 1, keepdims=False)
    return mine.astype(F32) + after(swap_core(theirs), *beside).astype(F32)


class Sum:
    def __init__(self, part, core, half, needed=(), beside=()):
        self.half = half
        self.total = over_cores(part, core, *beside)
        sent = after(pick(self.total, 1 - half), *needed)
        self.sent = sent.astype(BF16) if part.ndim > 1 else sent

    def done(self, *beside):
        return pick(self.total, self.half) + after(swap_tp(self.sent), *beside).astype(F32)


def local(
    inputs,
    cotangent,
    norm_gain,
    w_zx,
    w_bc,
    w_dt,
    conv_x,
    conv_xb,
    conv_bc,
    conv_bcb,
    dt_bias,
    a_log,
    d_skip,
    gate_gain,
    w_out,
):
    cores = lax.axis_size("section")
    core = lax.axis_index("section")
    half = lax.axis_index("tp")
    micros = inputs.shape[1]
    rows = inputs.shape[2] // cores
    channels = w_zx.shape[3] // cores
    heads = w_dt.shape[2] // cores
    width = channels // heads
    shared = w_bc.shape[2]
    depth = w_zx.shape[1]
    in_width = 2 * channels + shared + LANES
    def cut(tensor, index, size):
        return lax.dynamic_slice_in_dim(tensor, index * size, size, tensor.ndim - 1)

    def weight_shard(index):
        zx = cut(w_zx[0], index, channels).reshape(depth, 2 * channels)
        steps = jnp.pad(cut(w_dt[0], index, heads), ((0, 0), (0, LANES - heads)))
        return jnp.concatenate([zx, w_bc[0], steps, cut(w_out[0], index, channels)], axis=1)

    def slab_of(index):
        pad = jnp.zeros((LANES - heads,), F32)
        steps = jnp.concatenate([cut(dt_bias[0], index, heads), pad])
        decay = jnp.concatenate([-jnp.exp(cut(a_log[0], index, heads)), pad])
        skip = jnp.repeat(cut(d_skip[0], index, heads), width)
        rest = jnp.zeros((shared - LANES,), F32)
        taps = jnp.concatenate([cut(conv_x[0], index, channels), conv_bc[0]], axis=1)
        bias = jnp.concatenate([cut(conv_xb[0], index, channels), conv_bcb[0]])
        return jnp.concatenate(
            [
                taps,
                bias[None],
                jnp.concatenate([cut(gate_gain[0], index, channels), steps, rest])[None],
                jnp.concatenate([skip, decay, rest])[None],
                jnp.zeros((1, channels + shared), F32),
            ]
        )

    lane = np.arange(LANES)
    head_of = np.arange(channels) // width
    spread = (lane[:, None] % heads == head_of[None, :]) & (lane[:, None] < 2 * heads)
    spread = jnp.asarray(spread.astype(np.float32), BF16)
    gather = jnp.asarray((head_of[:, None] == lane[None, :]).astype(np.float32), BF16)

    own_shard = weight_shard(core)
    got_shard = swap_core(weight_shard(1 - core))
    in_line = lax.axis_size("fsdp") == 2 * DEEP and lax.axis_size("tp") == 2
    over_fsdp = functools.partial(lax.all_gather, axis_name="fsdp", tiled=True)
    def shard_of(layer, begin, end):
        return jnp.where(core == layer, own_shard[:, begin:end], got_shard[:, begin:end])

    def own_rows(tensor):
        return [
            lax.dynamic_slice_in_dim(tensor[0, m], core * rows, rows, 0) for m in range(micros)
        ]

    first, cotangents = own_rows(inputs), own_rows(cotangent)
    if in_line:
        gain_rows = depth // LANES
        packed = jnp.pad(norm_gain.astype(F32).reshape(-1, LANES), ((0, 8 - gain_rows), (0, 0)))
        per_head = jnp.concatenate([dt_bias, a_log, d_skip])
        per_head = jnp.pad(per_head, ((0, 5), (0, LANES - per_head.shape[1])))
        params = (conv_x[0], conv_xb, conv_bc[0], conv_bcb, gate_gain, per_head)
        second_gate, second_back = shard_of(1, 0, channels), shard_of(1, in_width, None)
        w_in, w_back, second_rest, gains, slabs, *tokens = start_gather(
            (shard_of(0, 0, in_width), shard_of(0, in_width, None), shard_of(1, channels, in_width)),
            packed,
            inputs[0],
            cotangent[0],
            params,
            spread,
            micros,
            heads,
            gain_rows,
        )
        slabs = [slabs[0], slabs[1]]
        w_in, w_back, second_rest = (v.reshape(-1, v.shape[2]) for v in (w_in, w_back, second_rest))
        projections = [(w_in, w_back)]
        second = (over_fsdp(after(second_gate, gains), axis=0), second_rest)
        projections.append((second, over_fsdp(after(second_back, gains), axis=0)))
        gains = gains[:, :, :gain_rows].reshape(2, -1)
        tokens = [v.reshape(4 * rows, -1) for v in tokens]
        first_normed, everyones = tokens[:micros], tokens[micros:]
    else:
        own_slab, got_slab = slab_of(core), swap_core(slab_of(1 - core))
        slabs = [jnp.where(core == layer, own_slab, got_slab) for layer in range(2)]
        gain_pair = by_index(core, norm_gain[0], swap_core(norm_gain[0])).astype(F32)
        projections = [
            (
                over_fsdp(shard_of(layer, 0, in_width), axis=0),
                over_fsdp(shard_of(layer, in_width, None), axis=0),
            )
            for layer in range(2)
        ]
        gains = over_fsdp(gain_pair.astype(BF16), axis=1).astype(F32)
        first_normed = None
        everyones = [gather_tokens(v, core, half) for v in cotangents]

    size = channels + shared
    zero_state = jnp.zeros((shared // 2, channels), F32)
    zero_halo = jnp.zeros((HALO, size), F32)
    last = micros - 1

    def scale_of(h):
        return lax.rsqrt(jnp.mean(h * h, axis=1, keepdims=True) + EPS)

    def norm(h, layer):
        return (h * scale_of(h) * gains[layer][None]).astype(BF16)

    hidden = [v.astype(F32) for v in first]
    normed = [None] * micros
    for m in range(micros):
        normed[m] = (
            first_normed[m] if in_line else gather_tokens(norm(hidden[m], 0), core, half)
        )

    hiddens, normeds, kept = [hidden, None], [normed, None], [[None] * micros for _ in range(2)]
    waiting = None

    def finish(pending, *beside):
        m, part, squares = pending
        r = lax.rsqrt(squares.done(*beside) / DI + EPS)[:, None]
        branch = r * part.done(*beside)
        kept[0][m].update(r=r, branch=branch)
        h = hiddens[0][m] + branch
        hiddens[1][m] = h
        return norm(h, 1)

    def spread_out(pending, own, *beside):
        normeds[1][pending[0]] = gather_tokens(own, core, half, beside)

    hiddens[1], normeds[1] = [None] * micros, [None] * micros
    for layer in range(2):
        w_in, w_back = projections[layer]
        state, tail = zero_state, zero_halo
        for m in range(micros):
            tokens = normeds[layer][m]
            if layer == 0 or not in_line:
                w_pair = (w_in[:, :channels], w_in[:, channels:])
            else:
                w_pair = w_in
            if waiting is not None and layer == 1:
                tokens = after(tokens, waiting[1].sent, waiting[2].sent)
            rest = dot_nn(tokens, w_pair[1])
            gate = dot_nn(tokens, w_pair[0])
            mixed_rest = rest
            if waiting is not None and layer == 1:
                own = finish(waiting, rest)
                gate = after(gate, own)
            elif waiting is not None:
                mixed_rest = after(rest, waiting[1].sent, waiting[2].sent)
            u, squares, y, entering, state_out = mixer_forward(
                gate, mixed_rest, tail, state, slabs[layer], spread, heads
            )
            if waiting is not None:
                spread_out(waiting, own if layer == 1 else finish(waiting, u), u)
            kept[layer][m] = dict(
                gate=gate, rest=rest, tail=tail, u=u, y=y, entering=entering, squares=squares
            )
            state, tail = state_out, rest[-HALO:, :size]
            waiting = None
            if layer == 0:
                part = Sum(dot_nt(u, w_back).astype(BF16), core, half)
                waiting = (m, part, Sum(squares[:, 0], core, half))

    over_tokens = (((0,), (0,)), ((), ()))

    def weight_grad(left, right):
        return lax.dot_general(
            jnp.concatenate(left), jnp.concatenate(right), over_tokens, preferred_element_type=F32
        ).astype(BF16)

    reduced, small = [None, None], [None, None]
    grads = [v.astype(F32) for v in cotangents]
    mixers_done = [kept[1][m]["u"] for m in range(micros)]
    w_in, w_back = projections[1]
    if in_line:
        w_in = jnp.concatenate([after(v, *mixers_done) for v in w_in], axis=1)
    w_back = after(w_back, w_in, *mixers_done)
    projections[1] = (w_in, w_back)
    backs, products, factors = list(everyones), [None] * micros, [None] * micros
    pairs = [None] * micros
    for m in reversed(range(micros)):
        k = kept[1][m]
        products[m] = dot_nn(backs[m], w_back)
        dots = jnp.sum(products[m] * k["u"].astype(F32), axis=1)
        pairs[m] = jnp.stack([k["squares"][:, 0], dots])
    pair = jnp.stack(pairs)
    pair = pair + swap_core(pair)
    pair = pair + swap_tp(pair)
    r = lax.rsqrt(pair[:, 0] / DI + EPS)
    factors = [jnp.stack([r[m], r[m] * r[m] * r[m] * pair[m, 1] / DI], axis=1) for m in range(micros)]
    gain_parts = [[], []]

    def finish_back(pending, *beside):
        layer, m, part = pending
        h = hiddens[layer][m]
        scale = scale_of(h)
        g_norm = part.done(*beside)
        gain_parts[layer].append(jnp.sum(g_norm * (h * scale), axis=0))
        g_norm = g_norm * gains[layer][None]
        mean = jnp.mean(g_norm * h, axis=1, keepdims=True)
        g = grads[m] + scale * g_norm - h * (scale * scale * scale) * mean
        grads[m] = g
        if layer == 0:
            return (g,)
        r, branch = kept[0][m]["r"], kept[0][m]["branch"]
        kappa = r * r * jnp.sum(g * branch, axis=1)[:, None] / DI
        return g.astype(BF16), jnp.concatenate([r, kappa], axis=1)

    def spread_back(pending, own, *beside):
        layer, m = pending[:2]
        if layer == 1:
            next_backs[m] = gather_tokens(own[0], core, half, beside)
            next_factors[m] = gather_tokens(own[1], core, half, beside)

    def reduce_rows(part):
        return lax.psum_scatter(part, "fsdp", scatter_dimension=0, tiled=True)

    def small_of(layer, totals):
        gain_rows = sum(gain_parts[layer]).reshape(2, -1)
        return jnp.concatenate(
            [totals[:6], jnp.concatenate([gain_rows, totals[6:, channels:]], axis=1)]
        )

    waiting, outs = None, [None] * micros
    next_backs, next_factors = [None] * micros, [None] * micros
    for layer in (1, 0):
        w_in, w_back = projections[layer]
        state, e_rows = zero_state, zero_halo
        totals = jnp.zeros(slabs[0].shape, F32)
        gpres = [None] * micros
        for m in reversed(range(micros)):
            k = kept[layer][m]
            q = products[m] if layer == 1 else dot_nn(backs[m], w_back)
            if m == last and layer == 1:
                mixed = [
                    (kept[1][j]["u"].astype(F32) * factors[j][:, :1]).astype(BF16)
                    for j in range(micros)
                ]
                reduced_back = weight_grad(backs, mixed)
                q = after(q, reduced_back)
                reduced_back = reduce_rows(reduced_back)
            if waiting is not None and not (layer == 0 and m == 0):
                q = after(q, waiting[2].sent)
            gpre, state, e_rows, sums = mixer_backward(
                q,
                factors[m],
                k["gate"],
                k["rest"],
                k["tail"],
                k["y"],
                k["entering"],
                state,
                e_rows,
                slabs[layer],
                spread,
                gather,
                heads,
                VMEM_LIMIT if layer == 1 and m == last else BACK_VMEM,
            )
            totals = totals + sums
            gpres[m] = gpre
            ready = gpre
            if waiting is not None:
                own = finish_back(waiting, gpre)
                ready = after(gpre, *own)
            if layer == 1 and m == 0:
                grad_in = weight_grad(normeds[1], gpres)
                ready = after(ready, grad_in)
            part = dot_nt(ready, w_in).astype(BF16)
            if waiting is not None:
                spread_back(waiting, own, part)
                if layer == 0 and waiting[0] == 1:
                    backs[0], factors[0] = next_backs[0], next_factors[0]
                    small[1] = small_of(1, above)
            beside = ()
            if layer == 1:
                outs[m] = dot_nt(after(k["u"], part), w_back).astype(BF16)
                beside = (outs[m],)
            waiting = (layer, m, Sum(part, core, half, (), beside))
            if layer == 0 and m == last:
                outs = [Sum(out, core, half, (waiting[2].sent,)) for out in outs]
        if layer == 0:
            grad_in = weight_grad(normeds[0], [after(v, waiting[2].sent) for v in gpres])
        if layer == 1 or not in_line:
            reduced[layer] = (reduce_rows(grad_in), reduced_back)
        if layer == 0:
            mixed = [
                (kept[0][j]["u"].astype(F32) * factors[j][:, :1]).astype(BF16) for j in range(micros)
            ]
            grad_back = weight_grad(backs, mixed)
            if not in_line:
                reduced[0] = (reduced[0][0], reduce_rows(grad_back))
        if layer == 1:
            second_factors, above = factors, totals
            backs, factors = list(next_backs), list(next_factors)
    finish_back(waiting, grad_in)
    small[0] = small_of(0, totals)

    outputs_rows = []
    for m in range(micros):
        r = lax.dynamic_slice_in_dim(second_factors[m], (2 * half + core) * rows, rows, 0)[:, :1]
        outputs_rows.append(hiddens[1][m] + r * outs[m].done(gpres[0]))

    def placed_rows(parts):
        own = jnp.where(core == 0, parts[0], parts[1])
        other = jnp.where(core == 0, parts[1], parts[0])
        return by_index(core, own, swap_core(other)).reshape(1, 1, 2 * rows, -1)

    outputs, input_grads = placed_rows(outputs_rows), placed_rows(grads)

    small_sums = after(jnp.stack(small), outputs, input_grads)
    if in_line:
        *both_parts, own_small, next_small, both_small = reduce_line(
            [grad_in, grad_back], small_sums, "grads_reduce", 2
        )
        first_own, first_other = both_parts[:2], both_parts[2:]
    else:
        small_sums = lax.psum(small_sums, "fsdp")
        own_small = pick(small_sums, core)
        next_small = swap_core(pick(small_sums, 1 - core))
        both_small = own_small + next_small
        both_small = both_small + swap_tp(both_small)
        first_own, first_other = reduced[0], [swap_core(v) for v in reduced[0]]
    low_small = jnp.where(core == 0, own_small, next_small)
    high_small = jnp.where(core == 0, next_small, own_small)
    wide = jnp.concatenate([low_small[:6, :channels], high_small[:6, :channels]], axis=1)
    narrow = jnp.concatenate(
        [v[5:, channels : channels + heads] for v in (low_small, high_small)], axis=1
    )
    conv_sum = both_small[:5, channels:]
    gain_sum = lax.dynamic_slice_in_dim(
        both_small[6:8, :channels].reshape(-1), lax.axis_index("fsdp") * depth, depth, 0
    )

    second_own = [after(v, own_small) for v in reduced[1]]
    second_other = [swap_core(v) for v in second_own]
    either = lambda one, two: jnp.where(core == 0, one.astype(F32), two.astype(F32))
    low_half = [either(first_own[i], second_other[i]) for i in range(2)]
    high_half = [either(first_other[i], second_own[i]) for i in range(2)]

    def joined(begin, end, i=0):
        return jnp.concatenate([low_half[i][:, begin:end], high_half[i][:, begin:end]], axis=1)

    g_zx = join_halves(first_own[0], first_other[0], second_own[0], second_other[0], channels)
    at = 2 * channels
    g_bc = low_half[0][:, at : at + shared] + high_half[0][:, at : at + shared]
    g_bc = g_bc + swap_tp(g_bc)
    g_dt = joined(at + shared, at + shared + heads)
    g_back = joined(0, channels, 1)

    return (
        outputs,
        input_grads,
        gain_sum[None],
        g_zx[None],
        g_bc[None],
        g_dt[None],
        wide[:4][None],
        wide[4][None],
        conv_sum[:4][None],
        conv_sum[4][None],
        narrow[0][None],
        narrow[1][None],
        narrow[2][None],
        wide[5][None],
        g_back[None],
    )


def solution(mesh):
    placed = (
        P("fsdp", None, "tp", None),
        P("fsdp", None, "tp", None),
        P("section", "fsdp"),
        P("section", "fsdp", None, "tp"),
        P("section", "fsdp", None),
        P("section", "fsdp", "tp"),
        P("section", None, "tp"),
        P("section", "tp"),
        P("section", None, None),
        P("section", None),
        P("section", "tp"),
        P("section", "tp"),
        P("section", "tp"),
        P("section", "tp"),
        P("section", "fsdp", "tp"),
    )
    return jax.shard_map(
        local,
        mesh=mesh,
        in_specs=placed,
        out_specs=(
            P("fsdp", "section", "tp", None),
            P("fsdp", "section", "tp", None),
        )
        + placed[2:],
        check_vma=False,
    )
```

```python
import functools

import jax
import jax.numpy as jnp
import numpy as np
from jax import lax
from jax.experimental import pallas as pl
from jax.experimental.pallas import tpu as pltpu
from jax.sharding import PartitionSpec as P

CONV = 4
DI = 4096
EPS = 1e-05
CHUNK = 128
LANES = 128
HALO = 8
NEG = -10000.0
F32 = jnp.float32
BF16 = jnp.bfloat16
VMEM_LIMIT = 56 * 1024 * 1024
MIXER_VMEM = 24 * 1024 * 1024
BACK_VMEM = 40 * 1024 * 1024


def sigmoid(v):
    return 0.5 * jnp.tanh(0.5 * v) + 0.5


def dot_nn(a, b):
    return lax.dot_general(a, b, (((1,), (0,)), ((), ())), preferred_element_type=F32)


def dot_nt(a, b):
    return lax.dot_general(a, b, (((1,), (1,)), ((), ())), preferred_element_type=F32)


def dot_sums(ones, columns, heads):
    high = columns.astype(BF16).astype(F32)
    middle = (columns - high).astype(BF16).astype(F32)
    low = columns - high - middle
    packed = high + pltpu.roll(middle, heads, 1) + pltpu.roll(low, 2 * heads, 1)
    sums = dot_nn(ones.astype(BF16), packed.astype(BF16))
    return sums + pltpu.roll(sums, LANES - heads, 1) + pltpu.roll(sums, LANES - 2 * heads, 1)


def split(a):
    high = a.astype(BF16)
    return high, (a - high.astype(F32)).astype(BF16)


def dot3(a, b, dot=dot_nn):
    return dot(a[0], b[0]) + (dot(a[1], b[0]) + dot(a[0], b[1]))


def tri(shape, keep):
    rows = lax.broadcasted_iota(jnp.int32, shape, 0)
    cols = lax.broadcasted_iota(jnp.int32, shape, 1)
    return keep(rows, cols)


def expand(columns, spread, heads):
    high = columns.astype(BF16).astype(F32)
    rest = columns - high
    packed = high + pltpu.roll(rest, heads, 1)
    return dot_nn(packed.astype(BF16), spread)


def step_terms(pre_dt, slab, channels, heads, spread):
    lane = lax.broadcasted_iota(jnp.int32, pre_dt.shape, 1)
    live = lane < heads
    arg = pre_dt + slab[5:6, channels : channels + LANES]
    dt = jnp.where(live, jnp.maximum(arg, 0.0) + jnp.log1p(jnp.exp(-jnp.abs(arg))), 0.0)
    decay = slab[6:7, channels : channels + LANES]
    lower = tri((CHUNK, CHUNK), lambda r, c: r >= c).astype(F32)
    cum = dot_sums(lower, dt * decay, heads)
    last = cum[CHUNK - 1 : CHUNK, :]
    grown = jnp.where(live, jnp.exp(cum), 0.0)
    left = jnp.where(live, jnp.exp(last - cum), 0.0)
    wide = expand(jnp.concatenate([dt, grown, left], axis=0), spread, heads)
    return arg, dt, decay, cum, wide[:CHUNK], wide[CHUNK : 2 * CHUNK], wide[2 * CHUNK :]


def conv_rows(buffer, slab):
    out = slab[4:5, :] + slab[CONV - 1 : CONV, :] * buffer[HALO : HALO + CHUNK, :]
    for k in range(CONV - 1):
        first = HALO - (CONV - 1) + k
        out = out + slab[k : k + 1, :] * buffer[first : first + CHUNK, :]
    return out


def forward_kernel(
    gate, rest, tail, start, slab, spread, u, sq, y, entering, leaving, state, buffer, *, channels, heads
):
    step = pl.program_id(0)
    size = channels + 2 * LANES

    @pl.when(step == 0)
    def _():
        state[...] = start[...]
        buffer[0:HALO, :] = tail[...]

    @pl.when(step > 0)
    def _():
        buffer[0:HALO, :] = buffer[CHUNK : CHUNK + HALO, :]

    buffer[HALO:, :] = rest[:, :size]
    entering[0] = state[...]
    conv = conv_rows(buffer, slab)
    act = conv * sigmoid(conv)
    xs = act[:, :channels]
    in_map = act[:, channels : channels + LANES]
    out_map = act[:, channels + LANES :]
    arg, dt, decay, cum, dt_w, grown_w, left_w = step_terms(
        rest[:, size:], slab, channels, heads, spread[...]
    )
    cum_t = cum.T
    xt = xs * dt_w
    xt_s = split(xt)
    out_s = split(out_map)
    scores = dot3(out_s, split(in_map), dot_nt)
    held = state[...]
    base = grown_w * dot3(out_s, split(held)) + slab[6:7, :channels] * xs
    state[...] = held * grown_w[CHUNK - 1 : CHUNK, :] + dot3(
        split(in_map.T), split(xt * left_w)
    )
    causal = tri((CHUNK, CHUNK), lambda r, c: r >= c)
    first_half = lax.broadcasted_iota(jnp.int32, (CHUNK, LANES), 1) < LANES // 2
    zero = jnp.zeros((CHUNK, LANES), BF16)
    for pair in range(channels // LANES):
        cols = slice(pair * LANES, (pair + 1) * LANES)
        mats = []
        for h in (2 * pair, 2 * pair + 1):
            gap = cum[:, h : h + 1] - cum_t[h : h + 1, :]
            mats.append(scores * jnp.exp(jnp.where(causal, gap, NEG)))
        stacked = tuple(
            jnp.concatenate(
                [jnp.where(first_half, xp[:, cols], zero), jnp.where(first_half, zero, xp[:, cols])],
                axis=0,
            )
            for xp in xt_s
        )
        y[:, cols] = base[:, cols] + dot3(split(jnp.concatenate(mats, axis=1)), stacked)
    z = gate[...]
    gated = y[...] * (z * sigmoid(z))
    sq[...] = jnp.sum(gated * gated, axis=1, keepdims=True)
    u[...] = (gated * slab[5:6, :channels]).astype(BF16)

    @pl.when(step == pl.num_programs(0) - 1)
    def _():
        leaving[...] = state[...]


def backward_kernel(
    q,
    factor,
    gate,
    rest,
    before,
    tail,
    y,
    entering,
    grad_start,
    e_start,
    slab,
    spread,
    gather,
    gpre,
    grad_leaving,
    e_leaving,
    sums,
    grad,
    buffer,
    e_buffer,
    *,
    channels,
    heads,
):
    step = pl.program_id(0)
    steps = pl.num_programs(0)
    size = channels + 2 * LANES

    @pl.when(step == 0)
    def _():
        grad[...] = grad_start[...]
        e_buffer[CHUNK:, :] = e_start[...]
        sums[...] = jnp.zeros_like(sums)

    @pl.when(step > 0)
    def _():
        e_buffer[CHUNK:, :] = e_buffer[0:HALO, :]

    @pl.when(step == steps - 1)
    def _():
        buffer[0:HALO, :] = tail[...]

    @pl.when(step < steps - 1)
    def _():
        buffer[0:HALO, :] = before[:, :size]

    buffer[HALO:, :] = rest[:, :size]
    conv = conv_rows(buffer, slab)
    sig = sigmoid(conv)
    act = conv * sig
    d_act = sig * (1.0 + conv * (1.0 - sig))
    xs = act[:, :channels]
    in_map = act[:, channels : channels + LANES]
    out_map = act[:, channels + LANES :]
    arg, dt, decay, cum, dt_w, grown_w, left_w = step_terms(
        rest[:, size:], slab, channels, heads, spread[...]
    )
    cum_t = cum.T

    z = gate[...]
    sig_z = sigmoid(z)
    silu_z = z * sig_z
    yv = y[...]
    gated = yv * silu_z
    qv = q[...] * factor[:, 0:1]
    sums[5:6, :channels] += jnp.sum(qv * gated, axis=0, keepdims=True)
    g_gated = qv * slab[5:6, :channels] - gated * factor[:, 1:2]
    gpre[:, :channels] = (g_gated * yv * (sig_z * (1.0 + z * (1.0 - sig_z)))).astype(BF16)
    gy = g_gated * silu_z
    gy_b = gy.astype(BF16)
    skip_row = jnp.sum(gy * xs, axis=0, keepdims=True)

    xt = xs * dt_w
    xt_b = xt.astype(BF16)
    in_b = in_map.astype(BF16)
    out_b = out_map.astype(BF16)
    held = entering[0]
    held_b = held.astype(BF16)
    g_state = grad[...]
    g_state_b = g_state.astype(BF16)
    grown_last = grown_w[CHUNK - 1 : CHUNK, :]

    from_state = grown_w * dot_nn(out_b, held_b)
    ge_b = (grown_w * gy).astype(BF16)
    g_out_map = dot_nt(ge_b, held_b)
    g_xt = left_w * dot_nn(in_b, g_state_b)
    g_in_map = dot_nt((xt * left_w).astype(BF16), g_state_b)
    through = jnp.sum(g_state * held, axis=0, keepdims=True) * grown_last
    grad[...] = g_state * grown_last + dot_nn(out_map.T.astype(BF16), ge_b)
    row_terms = gy * from_state
    col_terms = xt * g_xt

    scores_t = dot3(split(in_map), split(out_map), dot_nt)
    later = tri((CHUNK, CHUNK), lambda r, c: c >= r)
    first_half = lax.broadcasted_iota(jnp.int32, (CHUNK, LANES), 1) < LANES // 2
    lane = lax.broadcasted_iota(jnp.int32, (CHUNK, LANES), 1)
    zero = jnp.zeros((CHUNK, LANES), BF16)
    g_scores_t = jnp.zeros((CHUNK, CHUNK), F32)
    gap_rows = []
    gap_cols = jnp.zeros((CHUNK, LANES), F32)
    g_xt_parts = []
    for pair in range(channels // LANES):
        cols = slice(pair * LANES, (pair + 1) * LANES)
        gp = gy_b[:, cols]
        stacked = jnp.concatenate(
            [jnp.where(first_half, gp, zero), jnp.where(first_half, zero, gp)], axis=0
        )
        g_mats = dot_nt(xt_b[:, cols], stacked)
        mats = []
        for number in range(2):
            h = 2 * pair + number
            gap = cum_t[h : h + 1, :] - cum[:, h : h + 1]
            weight = jnp.exp(jnp.where(later, gap, NEG))
            mats.append((scores_t * weight).astype(BF16))
            g_score = g_mats[:, number * CHUNK : (number + 1) * CHUNK] * weight
            g_scores_t = g_scores_t + g_score
            g_gap = g_score * scores_t
            gap_rows.append(jnp.sum(g_gap, axis=0, keepdims=True))
            gap_cols = jnp.where(lane == h, jnp.sum(g_gap, axis=1, keepdims=True), gap_cols)
        g_xt_parts.append(g_xt[:, cols] + dot_nn(jnp.concatenate(mats, axis=1), stacked))
    g_xt = jnp.concatenate(g_xt_parts, axis=1)
    g_scores_b = g_scores_t.astype(BF16)
    g_in_map = g_in_map + dot_nn(g_scores_b, out_b)
    g_out_map = g_out_map + dot_nn(g_scores_t.T.astype(BF16), in_b)
    g_xs = slab[6:7, :channels] * gy + dt_w * g_xt

    pad = jnp.zeros((CHUNK - heads, CHUNK), F32)
    gap_rows_t = jnp.concatenate(gap_rows + [pad], axis=0).T
    packed = jnp.concatenate(
        [
            xs * g_xt,
            row_terms,
            col_terms,
            jnp.broadcast_to(through, (HALO, channels)),
            jnp.broadcast_to(skip_row, (HALO, channels)),
        ],
        axis=0,
    )
    high, rest = split(packed)
    grouped = dot_nn(high, gather[...]) + dot_nn(rest, gather[...])
    direct = grouped[:CHUNK]
    row_sum = grouped[CHUNK : 2 * CHUNK]
    col_sum = grouped[2 * CHUNK : 3 * CHUNK]
    through_sum = grouped[3 * CHUNK : 3 * CHUNK + 1]
    sums[7:8, channels : channels + LANES] += grouped[3 * CHUNK + HALO : 3 * CHUNK + HALO + 1]
    upper = tri((CHUNK, CHUNK), lambda r, c: c >= r).astype(F32)
    below = tri((CHUNK, CHUNK), lambda r, c: r > c).astype(F32)
    g_log = (
        dot_sums(upper, gap_rows_t - gap_cols + row_sum, heads)
        + dot_sums(below, col_sum, heads)
        + through_sum
    )
    g_dt = direct + g_log * decay
    g_dtin = jnp.where(lane < heads, g_dt * sigmoid(arg), 0.0)
    sums[5:6, channels : channels + LANES] += jnp.sum(g_dtin, axis=0, keepdims=True)
    sums[6:7, channels : channels + LANES] += decay * jnp.sum(dt * g_log, axis=0, keepdims=True)

    e = jnp.concatenate([g_xs, g_in_map, g_out_map], axis=1) * d_act
    e_buffer[0:CHUNK, :] = e
    sums[4:5, :] += jnp.sum(e, axis=0, keepdims=True)
    for k in range(CONV):
        first = HALO - (CONV - 1) + k
        sums[k : k + 1, :] += jnp.sum(e * buffer[first : first + CHUNK, :], axis=0, keepdims=True)
    g_pre = slab[CONV - 1 : CONV, :] * e
    for k in range(CONV - 1):
        first = CONV - 1 - k
        g_pre = g_pre + slab[k : k + 1, :] * e_buffer[first : first + CHUNK, :]
    gpre[:, channels : channels + size] = g_pre.astype(BF16)
    gpre[:, channels + size :] = g_dtin.astype(BF16)

    @pl.when(step == steps - 1)
    def _():
        grad_leaving[...] = grad[...]
        e_leaving[...] = e_buffer[0:HALO, :]


def fixed(shape):
    return pl.BlockSpec(shape, lambda i: (0,) * len(shape))


def mixer_forward(gate, rest, tail, start, slab, spread, heads):
    rows, width = rest.shape
    state_size, channels = start.shape
    size = channels + 2 * LANES
    steps = rows // CHUNK
    by_row = lambda cols: pl.BlockSpec((CHUNK, cols), lambda i: (i, 0))
    shape = jax.ShapeDtypeStruct

    def body(*refs):
        forward_kernel(*refs, channels=channels, heads=heads)

    return pl.pallas_call(
        body,
        grid=(steps,),
        in_specs=[
            by_row(channels),
            by_row(width),
            fixed((HALO, size)),
            fixed(start.shape),
            fixed(slab.shape),
            fixed(spread.shape),
        ],
        out_specs=[
            by_row(channels),
            by_row(1),
            by_row(channels),
            pl.BlockSpec((1, state_size, channels), lambda i: (i, 0, 0)),
            fixed(start.shape),
        ],
        out_shape=[
            shape((rows, channels), BF16),
            shape((rows, 1), F32),
            shape((rows, channels), F32),
            shape((steps, state_size, channels), F32),
            shape(start.shape, F32),
        ],
        scratch_shapes=[
            pltpu.VMEM((state_size, channels), F32),
            pltpu.VMEM((CHUNK + HALO, size), F32),
        ],
        compiler_params=pltpu.CompilerParams(
            dimension_semantics=("arbitrary",), vmem_limit_bytes=MIXER_VMEM
        ),
        cost_estimate=pl.CostEstimate(flops=1000, bytes_accessed=1000, transcendentals=0),
        name="mixer_forward",
    )(gate, rest, tail, start, slab, spread)


def mixer_backward(
    q, factor, gate, rest, tail, y, entering, grad, e_rows, slab, spread, gather, heads, grant
):
    rows, width = rest.shape
    state_size, channels = grad.shape
    size = channels + 2 * LANES
    steps = rows // CHUNK
    by_row = lambda cols: pl.BlockSpec((CHUNK, cols), lambda i: (steps - 1 - i, 0))
    shape = jax.ShapeDtypeStruct
    groups = CHUNK // HALO

    def body(*refs):
        backward_kernel(*refs, channels=channels, heads=heads)

    return pl.pallas_call(
        body,
        grid=(steps,),
        in_specs=[
            by_row(channels),
            by_row(2),
            by_row(channels),
            by_row(width),
            pl.BlockSpec(
                (HALO, width), lambda i: (jnp.maximum((steps - 1 - i) * groups - 1, 0), 0)
            ),
            fixed((HALO, size)),
            by_row(channels),
            pl.BlockSpec((1, state_size, channels), lambda i: (steps - 1 - i, 0, 0)),
            fixed(grad.shape),
            fixed(e_rows.shape),
            fixed(slab.shape),
            fixed(spread.shape),
            fixed(gather.shape),
        ],
        out_specs=[
            by_row(channels + width),
            fixed(grad.shape),
            fixed(e_rows.shape),
            fixed(slab.shape),
        ],
        out_shape=[
            shape((rows, channels + width), BF16),
            shape(grad.shape, F32),
            shape(e_rows.shape, F32),
            shape(slab.shape, F32),
        ],
        scratch_shapes=[
            pltpu.VMEM((state_size, channels), F32),
            pltpu.VMEM((CHUNK + HALO, size), F32),
            pltpu.VMEM((CHUNK + HALO, size), F32),
        ],
        compiler_params=pltpu.CompilerParams(
            dimension_semantics=("arbitrary",), vmem_limit_bytes=grant
        ),
        cost_estimate=pl.CostEstimate(flops=1000, bytes_accessed=1000, transcendentals=0),
        name="mixer_backward",
    )(q, factor, gate, rest, rest, tail, y, entering, grad, e_rows, slab, spread, gather)


def finish_kernel(first_own, first_other, second_own, second_other, gates, *, channels):
    core = lax.axis_index("section")

    def write(low, high):
        for half, source in enumerate((low, high)):
            value = source[...].astype(F32)
            for k in range(2):
                gates[:, k, half * channels : (half + 1) * channels] = value[
                    :, k * channels : (k + 1) * channels
                ]

    @pl.when(core == 0)
    def _():
        write(first_own, first_other)

    @pl.when(core == 1)
    def _():
        write(second_other, second_own)


def join_halves(first_own, first_other, second_own, second_other, channels):
    rows = first_own.shape[0]
    step = 32
    block = pl.BlockSpec((step, 2 * channels), lambda i: (i, 0))
    return pl.pallas_call(
        functools.partial(finish_kernel, channels=channels),
        grid=(rows // step,),
        in_specs=[block] * 4,
        out_specs=pl.BlockSpec((step, 2, 2 * channels), lambda i: (i, 0, 0)),
        out_shape=jax.ShapeDtypeStruct((rows, 2, 2 * channels), F32),
        compiler_params=pltpu.CompilerParams(
            dimension_semantics=("arbitrary",), vmem_limit_bytes=MIXER_VMEM
        ),
        cost_estimate=pl.CostEstimate(flops=1000, bytes_accessed=1000, transcendentals=0),
        name="join_halves",
    )(first_own, first_other, second_own, second_other)


MESH = pl.DeviceIdType.MESH
DEEP = 4
SIDEWAYS = 32
SIDE_ROWS = 48


def place_in_line():
    core, line, half = lax.axis_index("section"), lax.axis_index("fsdp"), lax.axis_index("tp")
    deep, side = line // 2, line % 2

    def device(z, x):
        return (core, z * 2 + x, half)

    return deep, side, device


def greet_all():
    core, line, half = lax.axis_index("section"), lax.axis_index("fsdp"), lax.axis_index("tp")
    barrier = pltpu.get_barrier_semaphore()

    def greet(target):
        pl.semaphore_signal(barrier, inc=1, device_id=target, device_id_type=MESH)

    greet((core, line, 1 - half))
    greet((1 - core, line, half))
    for step in range(1, 2 * DEEP):
        greet((core, (line + step) % (2 * DEEP), half))
    pl.semaphore_wait(barrier, 2 * DEEP + 1)


def gather_steps(shards, wholes, sems, beside):
    count = len(shards)
    local_sem, x_send, x_recv, up_send, up_recv, down_send, down_recv = sems[:7]
    side_send, side_recv, pair_up_send, pair_up_recv, pair_down_send, pair_down_recv = sems[7:]
    deep, side, device = place_in_line()
    above, below = jnp.minimum(deep + 1, DEEP - 1), jnp.maximum(deep - 1, 0)
    has_above, has_below = deep < DEEP - 1, deep > 0
    main = [pl.ds(0, shard.shape[0] - SIDE_ROWS) for shard in shards]
    rest = [pl.ds(shard.shape[0] - SIDE_ROWS, SIDE_ROWS) for shard in shards]

    def remote(source, place, send, recv, target):
        return pltpu.make_async_remote_copy(
            src_ref=source,
            dst_ref=place,
            send_sem=send,
            recv_sem=recv,
            device_id=target,
            device_id_type=MESH,
        )

    def own(i):
        return pltpu.make_async_copy(shards[i], wholes[i].at[deep * 2 + side], local_sem.at[i])

    def block(i, z, x=None):
        return wholes[i].at[z * 2 + (side if x is None else x), main[i]]

    def across(i, z, source=None):
        source = block(i, z) if source is None else source
        target = device(deep, 1 - side)
        return remote(source, block(i, z), x_send.at[i, z], x_recv.at[i, z], target)

    def upward(i, k, source=None):
        place = block(i, deep - k)
        source = place if source is None else source
        return remote(source, place, up_send.at[i, k], up_recv.at[i, k], device(above, side))

    def downward(i, k, source=None):
        place = block(i, deep + k)
        source = place if source is None else source
        return remote(source, place, down_send.at[i, k], down_recv.at[i, k], device(below, side))

    def sideways(i, x):
        place = wholes[i].at[deep * 2 + x, rest[i]]
        source = shards[i].at[rest[i]]
        return remote(source, place, side_send.at[i], side_recv.at[i], device(deep, 1 - side))

    def pair(i, z):
        return wholes[i].at[pl.ds(z * 2, 2), rest[i]]

    def pair_up(i, k):
        place = pair(i, deep - k)
        return remote(place, place, pair_up_send.at[i, k], pair_up_recv.at[i, k], device(above, side))

    def pair_down(i, k):
        place = pair(i, deep + k)
        return remote(
            place, place, pair_down_send.at[i, k], pair_down_recv.at[i, k], device(below, side)
        )

    for i in range(count):
        own(i).start()
        sideways(i, side).start()
    for i in range(count):
        source = shards[i].at[main[i]]

        @pl.when(has_above)
        def _(i=i, source=source):
            upward(i, 0, source).start()

        @pl.when(has_below)
        def _(i=i, source=source):
            downward(i, 0, source).start()

        across(i, deep, source).start()
    beside(0)
    here = device(deep, side)
    for k in range(1, DEEP):
        for i in range(count):

            @pl.when(deep >= k)
            def _(i=i, k=k):
                place = block(i, deep - k)
                remote(place, place, up_send.at[i, k - 1], up_recv.at[i, k - 1], here).wait_recv()

                @pl.when(has_above)
                def _():
                    upward(i, k).start()

                across(i, deep - k).start()

            @pl.when(deep + k <= DEEP - 1)
            def _(i=i, k=k):
                place = block(i, deep + k)
                remote(place, place, down_send.at[i, k - 1], down_recv.at[i, k - 1], here).wait_recv()

                @pl.when(has_below)
                def _():
                    downward(i, k).start()

                across(i, deep + k).start()

        if k == DEEP - 2:
            for i in range(count):
                own(i).wait()
                sideways(i, 1 - side).wait_recv()

                @pl.when(has_above)
                def _(i=i):
                    pair_up(i, 0).start()

                @pl.when(has_below)
                def _(i=i):
                    pair_down(i, 0).start()

        beside(k)

    for k in range(1, DEEP):
        for i in range(count):

            @pl.when(deep >= k)
            def _(i=i, k=k):
                place = pair(i, deep - k)
                remote(
                    place, place, pair_up_send.at[i, k - 1], pair_up_recv.at[i, k - 1], here
                ).wait_recv()

                @pl.when(has_above)
                def _():
                    pair_up(i, k).start()

            @pl.when(deep + k <= DEEP - 1)
            def _(i=i, k=k):
                place = pair(i, deep + k)
                remote(
                    place, place, pair_down_send.at[i, k - 1], pair_down_recv.at[i, k - 1], here
                ).wait_recv()

                @pl.when(has_below)
                def _():
                    pair_down(i, k).start()

    for i in range(count):
        sideways(i, side).wait_send()
        for z in range(DEEP):
            other = remote(
                block(i, z), block(i, z, 1 - side), x_send.at[i, z], x_recv.at[i, z], here
            )
            other.wait_send()
            other.wait_recv()
        for k in range(DEEP - 1):

            @pl.when(has_above & (deep >= k))
            def _(i=i, k=k):
                upward(i, k).wait_send()
                pair_up(i, k).wait_send()

            @pl.when(has_below & (deep + k <= DEEP - 1))
            def _(i=i, k=k):
                downward(i, k).wait_send()
                pair_down(i, k).wait_send()


def start_kernel(*refs, count, micros, heads, gain_rows):
    shards, (gain, own, cotangent) = refs[:count], refs[count : count + 3]
    params, spread = refs[count + 3 : count + 9], refs[count + 9]
    outs = refs[count + 10 :]
    wholes, (gains, slabs), targets = outs[:count], outs[count : count + 2], outs[count + 2 :]
    targets, scratch = targets[: 2 * micros], targets[2 * micros :]
    gain_send, gain_recv, own_sem, y_send, y_recv, core_send, core_recv, rows_out = scratch[13:21]
    other_slab, slab_send, slab_recv, line_send, line_recv = scratch[21:]
    core, line, half = lax.axis_index("section"), lax.axis_index("fsdp"), lax.axis_index("tp")
    lines = 2 * DEEP

    greet_all()
    across_tp, across_core = (core, line, 1 - half), (1 - core, line, half)

    def send_gain(step):
        return pltpu.make_async_remote_copy(
            src_ref=gain,
            dst_ref=gains.at[core, line],
            send_sem=gain_send.at[step],
            recv_sem=gain_recv.at[step],
            device_id=(core, (line + step) % lines, half),
            device_id_type=MESH,
        )

    for step in range(1, lines):
        send_gain(step).start()

    tokens = own.shape[1] // 2
    mine = pl.ds(pl.multiple_of(core * tokens, tokens), tokens)

    def token_copies(n):
        m = n % micros
        source = rows_out.at[pl.ds(m * tokens, tokens)] if n < micros else cotangent.at[m, mine]
        place = targets[n].at[half, core]
        later = targets[n].at[1 - half, core]
        more = 2 * micros + n
        remote = functools.partial(pltpu.make_async_remote_copy, device_id_type=MESH)
        return (
            pltpu.make_async_copy(source, place, own_sem.at[n]),
            remote(source, place, y_send.at[n], y_recv.at[n], device_id=across_tp),
            remote(source, place, core_send.at[n], core_recv.at[n], device_id=across_core),
            remote(later, later, core_send.at[more], core_recv.at[more], device_id=across_core),
        )

    send_slab = pltpu.make_async_remote_copy(
        src_ref=other_slab,
        dst_ref=slabs.at[core],
        send_sem=slab_send.at[0],
        recv_sem=slab_recv.at[0],
        device_id=across_core,
        device_id_type=MESH,
    )
    send_line = pltpu.make_async_remote_copy(
        src_ref=gains.at[core],
        dst_ref=gains.at[core],
        send_sem=line_send.at[0],
        recv_sem=line_recv.at[0],
        device_id=across_core,
        device_id_type=MESH,
    )

    def write_slab(place, index):
        taps, bias, shared_taps, shared_bias, gate, per_head = (v[...] for v in params)
        channels = spread.shape[1]
        first = index == 0
        cut = lambda v: jnp.where(first, v[:, :channels], v[:, channels:])
        lane = lax.broadcasted_iota(jnp.int32, per_head.shape, 1)
        here = jnp.where(first, per_head, pltpu.roll(per_head, LANES - heads, 1))
        here = jnp.where(lane < heads, here, 0.0)
        skip = expand(here, spread[...], heads)
        decay = jnp.where(lane < heads, -jnp.exp(here), 0.0)
        place[...] = jnp.zeros(place.shape, F32)
        place[0:CONV, :channels] = cut(taps)
        place[0:CONV, channels:] = shared_taps
        place[CONV : CONV + 1, :channels] = cut(bias)
        place[CONV : CONV + 1, channels:] = shared_bias
        place[5:6, :channels] = cut(gate)
        place[5:6, channels : channels + LANES] = here[0:1]
        place[6:7, :channels] = skip[2:3]
        place[6:7, channels : channels + LANES] = decay[1:2]

    def send_tokens(stage):
        if stage == 0:
            send_first()
        elif stage <= 2:
            for n in range((stage - 1) * micros, stage * micros):
                token_copies(n)[1].wait_recv()
                token_copies(n)[3].start()
            if stage == 1:
                for n in range(micros, 2 * micros):
                    for copy in token_copies(n)[:3]:
                        copy.start()

    def send_first():
        write_slab(other_slab, 1 - core)
        send_slab.start()
        write_slab(slabs.at[core], core)
        gains[core, line] = gain[...]
        for step in range(1, lines):
            send_gain(step).wait()
        send_line.start()
        send_line.wait()
        gain_row = jnp.concatenate(
            [gains[0, f, j : j + 1, :] for f in range(lines) for j in range(gain_rows)], axis=1
        )
        for m in range(micros):
            h = own[m, mine].astype(F32)
            scale = lax.rsqrt(jnp.mean(h * h, axis=1, keepdims=True) + EPS)
            rows_out[m * tokens : (m + 1) * tokens] = (h * scale * gain_row).astype(BF16)

        for n in range(micros):
            for copy in token_copies(n)[:3]:
                copy.start()

    gather_steps(shards, wholes, scratch[:13], send_tokens)
    send_slab.wait()
    for n in range(2 * micros):
        own_copy, y_copy, core_copy, core_later = token_copies(n)
        own_copy.wait()
        y_copy.wait_send()
        core_copy.wait()
        core_later.wait()


def start_gather(shards, gain, own, cotangent, params, spread, micros, heads, gain_rows):
    count = len(shards)
    lines = 2 * DEEP
    pairs = pltpu.SemaphoreType.DMA((count, DEEP))
    dma = lambda n: pltpu.SemaphoreType.DMA((n,))
    shape = jax.ShapeDtypeStruct
    anywhere = pl.BlockSpec(memory_space=pl.ANY)
    vmem = pl.BlockSpec(memory_space=pltpu.VMEM)
    rows, width = own.shape[0] * own.shape[1] // 2, own.shape[2]
    slab = (8, spread.shape[1] + params[2].shape[1])
    return pl.pallas_call(
        functools.partial(
            start_kernel, count=count, micros=micros, heads=heads, gain_rows=gain_rows
        ),
        out_shape=[shape((lines,) + v.shape, v.dtype) for v in shards]
        + [
            shape((2, lines) + gain.shape, F32),
            shape((2,) + slab, F32),
        ]
        + [shape((2, 2, rows // micros, width), BF16)] * (2 * micros),
        in_specs=[anywhere] * count + [vmem, vmem, anywhere] + [vmem] * 7,
        out_specs=[anywhere] * count + [vmem, vmem] + [anywhere] * (2 * micros),
        scratch_shapes=[dma(count)]
        + [pairs] * 6
        + [dma(count)] * 2
        + [pairs] * 4
        + [dma(lines)] * 2
        + [dma(2 * micros)] * 3
        + [dma(4 * micros)] * 2
        + [pltpu.VMEM((rows, width), BF16), pltpu.VMEM(slab, F32)]
        + [dma(1)] * 4,
        compiler_params=pltpu.CompilerParams(
            collective_id=1, has_side_effects=True, vmem_limit_bytes=VMEM_LIMIT
        ),
        cost_estimate=pl.CostEstimate(flops=170_000_000_000, bytes_accessed=1000, transcendentals=0),
        name="start_gather",
    )(*shards, gain, own, cotangent, *params, spread)


def add_rows(out, *parts):
    rows = out.shape[0]
    step = 16

    def body(n, _):
        at = pl.ds(pl.multiple_of(n * step, step), step)
        total = parts[0][at].astype(F32)
        for part in parts[1:]:
            total = total + part[at].astype(F32)
        out[at] = total.astype(out.dtype)
        return 0

    lax.fori_loop(0, rows // step, body, 0)


X_ORDER = ((3, 2, 1, 0), (3, 0, 2, 1), (0, 3, 1, 2), (0, 1, 2, 3))


def reduce_kernel(*refs, count):
    parts, small, results = refs[:count], refs[count], refs[count + 1 : 2 * count + 1]
    others = refs[2 * count + 1 : 3 * count + 1]
    own_small, next_small, both_small = refs[3 * count + 1 : 3 * count + 4]
    scratch = refs[3 * count + 4 :]
    held, crossed, from_below, from_above, pairs, pairs_below, pairs_above, side_in = (
        scratch[n * count : (n + 1) * count] for n in range(8)
    )
    sems = scratch[8 * count : -5]
    load_sem, x_send, x_recv, up_send, up_recv, down_send, down_recv = sems[:7]
    pair_sem, pair_up_send, pair_up_recv, pair_down_send, pair_down_recv = sems[7:12]
    side_send, side_recv = sems[12:]
    small_buffer, small_send, small_recv, other_send, other_recv = scratch[-5:]
    main = [result.shape[0] - SIDEWAYS for result in results]
    deep, side, device = place_in_line()
    core, line, half = lax.axis_index("section"), lax.axis_index("fsdp"), lax.axis_index("tp")
    greet_all()
    across_core = (1 - core, line, half)
    partners = [
        device(deep, 1 - side),
        device(deep + 1 - 2 * (deep % 2), side),
        device((deep + 2) % DEEP, side),
        (core, line, 1 - half),
        across_core,
        across_core,
    ]

    def swap_small(n, source, target):
        return pltpu.make_async_remote_copy(
            src_ref=source,
            dst_ref=target,
            send_sem=small_send.at[n],
            recv_sem=small_recv.at[n],
            device_id=partners[n],
            device_id_type=MESH,
        )

    def sum_small():
        for n in range(3):
            copy = swap_small(n, small if n == 0 else small_buffer.at[n - 1], small_buffer.at[3 + n])
            if n > 0:
                copy.start()
            copy.wait()
            value = small[...] if n == 0 else small_buffer[n - 1]
            small_buffer[n] = value + small_buffer[3 + n]

    def spread_small():
        over_tp = swap_small(3, small_buffer.at[2], small_buffer.at[6])
        over_core = swap_small(4, small_buffer.at[2, 1 - core], next_small)
        over_tp.start()
        over_core.start()
        own_small[...] = small_buffer[2, core]
        over_tp.wait()
        small_buffer[7] = small_buffer[2] + small_buffer[6]
        last = swap_small(5, small_buffer.at[7, 1 - core], small_buffer.at[8, 0])
        last.start()
        last.wait()
        both_small[...] = small_buffer[7, core] + small_buffer[8, 0]
        over_core.wait()

    def rows(i, z, x):
        return parts[i].at[z * 2 + x, pl.ds(0, main[i])]

    def load_pair(i, z):
        source = parts[i].at[pl.ds(z * 2, 2), pl.ds(main[i], SIDEWAYS)]
        return pltpu.make_async_copy(source, pairs[i].at[z], pair_sem.at[i, z])

    def pair_along(i, k, z, here, up):
        send, recv = (pair_up_send, pair_up_recv) if up else (pair_down_send, pair_down_recv)
        target = min(here + 1, DEEP - 1) if up else max(here - 1, 0)
        return pltpu.make_async_remote_copy(
            src_ref=pairs[i].at[z],
            dst_ref=(pairs_below if up else pairs_above)[i].at[k - 1],
            send_sem=send.at[i, k - 1],
            recv_sem=recv.at[i, k - 1],
            device_id=device(target, side),
            device_id_type=MESH,
        )

    def sideways(i, here):
        return pltpu.make_async_remote_copy(
            src_ref=pairs[i].at[here, 1 - side],
            dst_ref=side_in[i],
            send_sem=side_send.at[i],
            recv_sem=side_recv.at[i],
            device_id=device(deep, 1 - side),
            device_id_type=MESH,
        )

    def load(i, z):
        return pltpu.make_async_copy(rows(i, z, side), held[i].at[z], load_sem.at[i, z])

    def across(i, z):
        return pltpu.make_async_remote_copy(
            src_ref=rows(i, z, 1 - side),
            dst_ref=crossed[i].at[z],
            send_sem=x_send.at[i, z],
            recv_sem=x_recv.at[i, z],
            device_id=device(deep, 1 - side),
            device_id_type=MESH,
        )

    def upward(i, k, z, here):
        return pltpu.make_async_remote_copy(
            src_ref=held[i].at[z],
            dst_ref=from_below[i].at[k - 1],
            send_sem=up_send.at[i, k - 1],
            recv_sem=up_recv.at[i, k - 1],
            device_id=device(min(here + 1, DEEP - 1), side),
            device_id_type=MESH,
        )

    def downward(i, k, z, here):
        return pltpu.make_async_remote_copy(
            src_ref=held[i].at[z],
            dst_ref=from_above[i].at[k - 1],
            send_sem=down_send.at[i, k - 1],
            recv_sem=down_recv.at[i, k - 1],
            device_id=device(max(here - 1, 0), side),
            device_id_type=MESH,
        )

    def to_other(i):
        return pltpu.make_async_remote_copy(
            src_ref=results[i],
            dst_ref=others[i],
            send_sem=other_send.at[i],
            recv_sem=other_recv.at[i],
            device_id=across_core,
            device_id_type=MESH,
        )

    def at_depth(here):
        order = X_ORDER[here]
        last = DEEP - 1
        started = []

        def send_across(number):
            for i in range(count):
                across(i, order[number]).start()

        def take(number):
            z = order[number]
            for i in range(count):
                across(i, z).wait_recv()
            if number + 2 < DEEP:
                send_across(number + 2)
            for i in range(count):
                load(i, z).wait()
                add_rows(held[i].at[z], held[i].at[z], crossed[i].at[z])

        def relay(k, up):
            z = DEEP - k + here if up else here + k - DEEP
            first = here == 0 if up else here == last
            for i in range(count):
                if not first:
                    make = upward if up else downward
                    back = from_below if up else from_above
                    make(i, k - 1, z, here).wait_recv()
                    add_rows(held[i].at[z], held[i].at[z], back[i].at[k - 2])
                copy = (upward if up else downward)(i, k, z, here)
                copy.start()
                started.append(copy)

        swap_small(0, small, small_buffer.at[3]).start()
        send_across(0)
        send_across(1)
        for number in range(DEEP):
            for i in range(count):
                load_pair(i, order[number]).start()
        for number in range(DEEP):
            for i in range(count):
                load(i, order[number]).start()

        def relay_pair(k, up):
            z = DEEP - k + here if up else here + k - DEEP
            if not 0 <= z < DEEP or z == here or (z < here) == up:
                return
            for i in range(count):
                load_pair(i, z).wait()
                if here != (0 if up else last):
                    pair_along(i, k - 1, z, here, up).wait_recv()
                    back = (pairs_below if up else pairs_above)[i]
                    for x in range(2):
                        add_rows(pairs[i].at[z, x], pairs[i].at[z, x], back.at[k - 2, x])
                copy = pair_along(i, k, z, here, up)
                copy.start()
                started.append(copy)

        for k in range(1, DEEP):
            relay_pair(k, True)
            relay_pair(k, False)
            if k == 1:
                sum_small()
        for i in range(count):
            load_pair(i, here).wait()
            for x in range(2):
                terms = [pairs[i].at[here, x]]
                if here > 0:
                    if x == 0:
                        pair_along(i, DEEP - 1, here, here, True).wait_recv()
                    terms.append(pairs_below[i].at[DEEP - 2, x])
                if here < last:
                    if x == 0:
                        pair_along(i, DEEP - 1, here, here, False).wait_recv()
                    terms.append(pairs_above[i].at[DEEP - 2, x])
                add_rows(pairs[i].at[here, x], *terms)
            sideways(i, here).start()
        if here in (0, last):
            up = here == 0
            for k in range(1, DEEP):
                take(k - 1)
                relay(k, up)
            spread_small()
            take(DEEP - 1)
        else:
            up = here == 1
            take(0)
            take(1)
            relay(2, up)
            relay(3, not up)
            take(2)
            relay(3, up)
            spread_small()
            take(3)
        for i in range(count):
            terms = [held[i].at[here]]
            if here > 0:
                upward(i, DEEP - 1, here, here).wait_recv()
                terms.append(from_below[i].at[DEEP - 2])
            if here < last:
                downward(i, DEEP - 1, here, here).wait_recv()
                terms.append(from_above[i].at[DEEP - 2])
            add_rows(results[i].at[pl.ds(0, main[i])], *terms)
            sideways(i, here).wait_recv()
            add_rows(
                results[i].at[pl.ds(main[i], SIDEWAYS)], pairs[i].at[here, side], side_in[i]
            )
            to_other(i).start()
        for i in range(count):
            to_other(i).wait()
            sideways(i, here).wait_send()
        for copy in started:
            copy.wait_send()
        for z in range(DEEP):
            for i in range(count):
                across(i, z).wait_send()

    for here in range(DEEP):

        @pl.when(deep == here)
        def _(here=here):
            at_depth(here)


def reduce_line(parts, small, name, collective_id):
    count = len(parts)
    shards = [(p.shape[0] // (2 * DEEP),) + p.shape[1:] for p in parts]
    pairs = pltpu.SemaphoreType.DMA((count, DEEP))
    sizes = sum(p.size for p in parts)
    blocks = lambda n: [pltpu.VMEM((n, shard[0] - SIDEWAYS, shard[1]), BF16) for shard in shards]
    doubles = lambda n: [pltpu.VMEM((n, 2, SIDEWAYS, shard[1]), BF16) for shard in shards]
    split_parts = [p.reshape((2 * DEEP, -1) + p.shape[1:]) for p in parts]
    shape = jax.ShapeDtypeStruct
    vmem = pl.BlockSpec(memory_space=pltpu.VMEM)
    return pl.pallas_call(
        functools.partial(reduce_kernel, count=count),
        out_shape=[shape(shard, BF16) for shard in shards] * 2 + [shape(small.shape[1:], F32)] * 3,
        in_specs=[pl.BlockSpec(memory_space=pl.ANY)] * count + [vmem],
        out_specs=[vmem] * (2 * count + 3),
        scratch_shapes=blocks(DEEP)
        + blocks(DEEP)
        + blocks(DEEP - 1)
        + blocks(DEEP - 1)
        + doubles(DEEP)
        + doubles(DEEP - 1)
        + doubles(DEEP - 1)
        + [pltpu.VMEM((SIDEWAYS, shard[1]), BF16) for shard in shards]
        + [pairs] * 12
        + [pltpu.SemaphoreType.DMA((count,))] * 2
        + [
            pltpu.VMEM((9,) + small.shape, F32),
            pltpu.SemaphoreType.DMA((6,)),
            pltpu.SemaphoreType.DMA((6,)),
            pltpu.SemaphoreType.DMA((count,)),
            pltpu.SemaphoreType.DMA((count,)),
        ],
        compiler_params=pltpu.CompilerParams(
            collective_id=collective_id, has_side_effects=True, vmem_limit_bytes=VMEM_LIMIT
        ),
        cost_estimate=pl.CostEstimate(flops=1000, bytes_accessed=1000, transcendentals=0),
        name=name,
    )(*split_parts, small)


SWAP = [(0, 1), (1, 0)]


def swap_core(value):
    return lax.ppermute(value, "section", SWAP)


def swap_tp(value):
    return lax.ppermute(value, "tp", SWAP)


def by_index(index, own, other):
    first = index == 0
    return jnp.stack([jnp.where(first, own, other), jnp.where(first, other, own)])


def pick(pair, index):
    return lax.dynamic_index_in_dim(pair, index, 0, keepdims=False)


def gather_tokens(own, core, half, beside=()):
    both = by_index(half, own, after(swap_tp(own), *beside))
    whole = by_index(core, both, swap_core(both))
    whole = jnp.moveaxis(whole, 0, 1)
    return whole.reshape((4 * own.shape[0],) + own.shape[1:])


def after(value, *others):
    return lax.optimization_barrier((value,) + others)[0] if others else value


def over_cores(part, core, *beside):
    split_rows = part.reshape((2, 2, part.shape[0] // 4) + part.shape[1:])
    mine = lax.dynamic_index_in_dim(split_rows, core, 1, keepdims=False)
    theirs = lax.dynamic_index_in_dim(split_rows, 1 - core, 1, keepdims=False)
    return mine.astype(F32) + after(swap_core(theirs), *beside).astype(F32)


class Sum:
    def __init__(self, part, core, half, needed=(), beside=()):
        self.half = half
        self.total = over_cores(part, core, *beside)
        sent = after(pick(self.total, 1 - half), *needed)
        self.sent = sent.astype(BF16) if part.ndim > 1 else sent

    def done(self, *beside):
        return pick(self.total, self.half) + after(swap_tp(self.sent), *beside).astype(F32)


def local(
    inputs,
    cotangent,
    norm_gain,
    w_zx,
    w_bc,
    w_dt,
    conv_x,
    conv_xb,
    conv_bc,
    conv_bcb,
    dt_bias,
    a_log,
    d_skip,
    gate_gain,
    w_out,
):
    cores = lax.axis_size("section")
    core = lax.axis_index("section")
    half = lax.axis_index("tp")
    micros = inputs.shape[1]
    rows = inputs.shape[2] // cores
    channels = w_zx.shape[3] // cores
    heads = w_dt.shape[2] // cores
    width = channels // heads
    shared = w_bc.shape[2]
    depth = w_zx.shape[1]
    in_width = 2 * channels + shared + LANES
    def cut(tensor, index, size):
        return lax.dynamic_slice_in_dim(tensor, index * size, size, tensor.ndim - 1)

    def weight_shard(index):
        zx = cut(w_zx[0], index, channels).reshape(depth, 2 * channels)
        steps = jnp.pad(cut(w_dt[0], index, heads), ((0, 0), (0, LANES - heads)))
        return jnp.concatenate([zx, w_bc[0], steps, cut(w_out[0], index, channels)], axis=1)

    def slab_of(index):
        pad = jnp.zeros((LANES - heads,), F32)
        steps = jnp.concatenate([cut(dt_bias[0], index, heads), pad])
        decay = jnp.concatenate([-jnp.exp(cut(a_log[0], index, heads)), pad])
        skip = jnp.repeat(cut(d_skip[0], index, heads), width)
        rest = jnp.zeros((shared - LANES,), F32)
        taps = jnp.concatenate([cut(conv_x[0], index, channels), conv_bc[0]], axis=1)
        bias = jnp.concatenate([cut(conv_xb[0], index, channels), conv_bcb[0]])
        return jnp.concatenate(
            [
                taps,
                bias[None],
                jnp.concatenate([cut(gate_gain[0], index, channels), steps, rest])[None],
                jnp.concatenate([skip, decay, rest])[None],
                jnp.zeros((1, channels + shared), F32),
            ]
        )

    lane = np.arange(LANES)
    head_of = np.arange(channels) // width
    spread = (lane[:, None] % heads == head_of[None, :]) & (lane[:, None] < 2 * heads)
    spread = jnp.asarray(spread.astype(np.float32), BF16)
    gather = jnp.asarray((head_of[:, None] == lane[None, :]).astype(np.float32), BF16)

    own_shard = weight_shard(core)
    got_shard = swap_core(weight_shard(1 - core))
    in_line = lax.axis_size("fsdp") == 2 * DEEP and lax.axis_size("tp") == 2
    over_fsdp = functools.partial(lax.all_gather, axis_name="fsdp", tiled=True)
    def shard_of(layer, begin, end):
        return jnp.where(core == layer, own_shard[:, begin:end], got_shard[:, begin:end])

    def own_rows(tensor):
        return [
            lax.dynamic_slice_in_dim(tensor[0, m], core * rows, rows, 0) for m in range(micros)
        ]

    first, cotangents = own_rows(inputs), own_rows(cotangent)
    if in_line:
        gain_rows = depth // LANES
        packed = jnp.pad(norm_gain.astype(F32).reshape(-1, LANES), ((0, 8 - gain_rows), (0, 0)))
        per_head = jnp.concatenate([dt_bias, a_log, d_skip])
        per_head = jnp.pad(per_head, ((0, 5), (0, LANES - per_head.shape[1])))
        params = (conv_x[0], conv_xb, conv_bc[0], conv_bcb, gate_gain, per_head)
        second_gate, second_back = shard_of(1, 0, channels), shard_of(1, in_width, None)
        w_in, w_back, second_rest, gains, slabs, *tokens = start_gather(
            (shard_of(0, 0, in_width), shard_of(0, in_width, None), shard_of(1, channels, in_width)),
            packed,
            inputs[0],
            cotangent[0],
            params,
            spread,
            micros,
            heads,
            gain_rows,
        )
        slabs = [slabs[0], slabs[1]]
        w_in, w_back, second_rest = (v.reshape(-1, v.shape[2]) for v in (w_in, w_back, second_rest))
        projections = [(w_in, w_back)]
        second = (over_fsdp(after(second_gate, gains), axis=0), second_rest)
        projections.append((second, over_fsdp(after(second_back, gains), axis=0)))
        gains = gains[:, :, :gain_rows].reshape(2, -1)
        tokens = [v.reshape(4 * rows, -1) for v in tokens]
        first_normed, everyones = tokens[:micros], tokens[micros:]
    else:
        own_slab, got_slab = slab_of(core), swap_core(slab_of(1 - core))
        slabs = [jnp.where(core == layer, own_slab, got_slab) for layer in range(2)]
        gain_pair = by_index(core, norm_gain[0], swap_core(norm_gain[0])).astype(F32)
        projections = [
            (
                over_fsdp(shard_of(layer, 0, in_width), axis=0),
                over_fsdp(shard_of(layer, in_width, None), axis=0),
            )
            for layer in range(2)
        ]
        gains = over_fsdp(gain_pair.astype(BF16), axis=1).astype(F32)
        first_normed = None
        everyones = [gather_tokens(v, core, half) for v in cotangents]

    size = channels + shared
    zero_state = jnp.zeros((shared // 2, channels), F32)
    zero_halo = jnp.zeros((HALO, size), F32)
    last = micros - 1

    def scale_of(h):
        return lax.rsqrt(jnp.mean(h * h, axis=1, keepdims=True) + EPS)

    def norm(h, layer):
        return (h * scale_of(h) * gains[layer][None]).astype(BF16)

    hidden = [v.astype(F32) for v in first]
    normed = [None] * micros
    for m in range(micros):
        normed[m] = (
            first_normed[m] if in_line else gather_tokens(norm(hidden[m], 0), core, half)
        )

    hiddens, normeds, kept = [hidden, None], [normed, None], [[None] * micros for _ in range(2)]
    waiting = None

    def finish(pending, *beside):
        m, part, squares = pending
        r = lax.rsqrt(squares.done(*beside) / DI + EPS)[:, None]
        branch = r * part.done(*beside)
        kept[0][m].update(r=r, branch=branch)
        h = hiddens[0][m] + branch
        hiddens[1][m] = h
        return norm(h, 1)

    def spread_out(pending, own, *beside):
        normeds[1][pending[0]] = gather_tokens(own, core, half, beside)

    hiddens[1], normeds[1] = [None] * micros, [None] * micros
    for layer in range(2):
        w_in, w_back = projections[layer]
        state, tail = zero_state, zero_halo
        for m in range(micros):
            tokens = normeds[layer][m]
            if layer == 0 or not in_line:
                w_pair = (w_in[:, :channels], w_in[:, channels:])
            else:
                w_pair = w_in
            if waiting is not None and layer == 1:
                tokens = after(tokens, waiting[1].sent, waiting[2].sent)
            rest = dot_nn(tokens, w_pair[1])
            gate = dot_nn(tokens, w_pair[0])
            mixed_rest = rest
            if waiting is not None and layer == 1:
                own = finish(waiting, rest)
                gate = after(gate, own)
            elif waiting is not None:
                mixed_rest = after(rest, waiting[1].sent, waiting[2].sent)
            u, squares, y, entering, state_out = mixer_forward(
                gate, mixed_rest, tail, state, slabs[layer], spread, heads
            )
            if waiting is not None:
                spread_out(waiting, own if layer == 1 else finish(waiting, u), u)
            kept[layer][m] = dict(
                gate=gate, rest=rest, tail=tail, u=u, y=y, entering=entering, squares=squares
            )
            state, tail = state_out, rest[-HALO:, :size]
            waiting = None
            if layer == 0:
                part = Sum(dot_nt(u, w_back).astype(BF16), core, half)
                waiting = (m, part, Sum(squares[:, 0], core, half))

    over_tokens = (((0,), (0,)), ((), ()))

    def weight_grad(left, right):
        return lax.dot_general(
            jnp.concatenate(left), jnp.concatenate(right), over_tokens, preferred_element_type=F32
        ).astype(BF16)

    reduced, small = [None, None], [None, None]
    grads = [v.astype(F32) for v in cotangents]
    mixers_done = [kept[1][m]["u"] for m in range(micros)]
    w_in, w_back = projections[1]
    if in_line:
        w_in = jnp.concatenate([after(v, *mixers_done) for v in w_in], axis=1)
    w_back = after(w_back, w_in, *mixers_done)
    projections[1] = (w_in, w_back)
    backs, products, factors = list(everyones), [None] * micros, [None] * micros
    pairs = [None] * micros
    for m in reversed(range(micros)):
        k = kept[1][m]
        products[m] = dot_nn(backs[m], w_back)
        dots = jnp.sum(products[m] * k["u"].astype(F32), axis=1)
        pairs[m] = jnp.stack([k["squares"][:, 0], dots])
    pair = jnp.stack(pairs)
    pair = pair + swap_core(pair)
    pair = pair + swap_tp(pair)
    r = lax.rsqrt(pair[:, 0] / DI + EPS)
    factors = [jnp.stack([r[m], r[m] * r[m] * r[m] * pair[m, 1] / DI], axis=1) for m in range(micros)]
    gain_parts = [[], []]

    def finish_back(pending, *beside):
        layer, m, part = pending
        h = hiddens[layer][m]
        scale = scale_of(h)
        g_norm = part.done(*beside)
        gain_parts[layer].append(jnp.sum(g_norm * (h * scale), axis=0))
        g_norm = g_norm * gains[layer][None]
        mean = jnp.mean(g_norm * h, axis=1, keepdims=True)
        g = grads[m] + scale * g_norm - h * (scale * scale * scale) * mean
        grads[m] = g
        if layer == 0:
            return (g,)
        r, branch = kept[0][m]["r"], kept[0][m]["branch"]
        kappa = r * r * jnp.sum(g * branch, axis=1)[:, None] / DI
        return g.astype(BF16), jnp.concatenate([r, kappa], axis=1)

    def spread_back(pending, own, *beside):
        layer, m = pending[:2]
        if layer == 1:
            next_backs[m] = gather_tokens(own[0], core, half, beside)
            next_factors[m] = gather_tokens(own[1], core, half, beside)

    def reduce_rows(part):
        return lax.psum_scatter(part, "fsdp", scatter_dimension=0, tiled=True)

    def small_of(layer, totals):
        gain_rows = sum(gain_parts[layer]).reshape(2, -1)
        return jnp.concatenate(
            [totals[:6], jnp.concatenate([gain_rows, totals[6:, channels:]], axis=1)]
        )

    waiting, outs = None, [None] * micros
    next_backs, next_factors = [None] * micros, [None] * micros
    for layer in (1, 0):
        w_in, w_back = projections[layer]
        state, e_rows = zero_state, zero_halo
        totals = jnp.zeros(slabs[0].shape, F32)
        gpres = [None] * micros
        for m in reversed(range(micros)):
            k = kept[layer][m]
            q = products[m] if layer == 1 else dot_nn(backs[m], w_back)
            if m == last and layer == 1:
                mixed = [
                    (kept[1][j]["u"].astype(F32) * factors[j][:, :1]).astype(BF16)
                    for j in range(micros)
                ]
                reduced_back = weight_grad(backs, mixed)
                q = after(q, reduced_back)
                reduced_back = reduce_rows(reduced_back)
            if waiting is not None and not (layer == 0 and m == 0):
                q = after(q, waiting[2].sent)
            gpre, state, e_rows, sums = mixer_backward(
                q,
                factors[m],
                k["gate"],
                k["rest"],
                k["tail"],
                k["y"],
                k["entering"],
                state,
                e_rows,
                slabs[layer],
                spread,
                gather,
                heads,
                VMEM_LIMIT if layer == 1 and m == last else BACK_VMEM,
            )
            totals = totals + sums
            gpres[m] = gpre
            ready = gpre
            if waiting is not None:
                own = finish_back(waiting, gpre)
                ready = after(gpre, *own)
            if layer == 1 and m == 0:
                grad_in = weight_grad(normeds[1], gpres)
                ready = after(ready, grad_in)
            part = dot_nt(ready, w_in).astype(BF16)
            if waiting is not None:
                spread_back(waiting, own, part)
                if layer == 0 and waiting[0] == 1:
                    backs[0], factors[0] = next_backs[0], next_factors[0]
                    small[1] = small_of(1, above)
            beside = ()
            if layer == 1:
                outs[m] = dot_nt(after(k["u"], part), w_back).astype(BF16)
                beside = (outs[m],)
            waiting = (layer, m, Sum(part, core, half, (), beside))
            if layer == 0 and m == last:
                outs = [Sum(out, core, half, (waiting[2].sent,)) for out in outs]
        if layer == 0:
            grad_in = weight_grad(normeds[0], [after(v, waiting[2].sent) for v in gpres])
        if layer == 1 or not in_line:
            reduced[layer] = (reduce_rows(grad_in), reduced_back)
        if layer == 0:
            mixed = [
                (kept[0][j]["u"].astype(F32) * factors[j][:, :1]).astype(BF16) for j in range(micros)
            ]
            grad_back = weight_grad(backs, mixed)
            if not in_line:
                reduced[0] = (reduced[0][0], reduce_rows(grad_back))
        if layer == 1:
            second_factors, above = factors, totals
            backs, factors = list(next_backs), list(next_factors)
    finish_back(waiting, grad_in)
    small[0] = small_of(0, totals)

    outputs_rows = []
    for m in range(micros):
        r = lax.dynamic_slice_in_dim(second_factors[m], (2 * half + core) * rows, rows, 0)[:, :1]
        outputs_rows.append(hiddens[1][m] + r * outs[m].done(gpres[0]))

    def placed_rows(parts):
        own = jnp.where(core == 0, parts[0], parts[1])
        other = jnp.where(core == 0, parts[1], parts[0])
        return by_index(core, own, swap_core(other)).reshape(1, 1, 2 * rows, -1)

    outputs, input_grads = placed_rows(outputs_rows), placed_rows(grads)

    small_sums = after(jnp.stack(small), outputs, input_grads)
    if in_line:
        *both_parts, own_small, next_small, both_small = reduce_line(
            [grad_in, grad_back], small_sums, "grads_reduce", 2
        )
        first_own, first_other = both_parts[:2], both_parts[2:]
    else:
        small_sums = lax.psum(small_sums, "fsdp")
        own_small = pick(small_sums, core)
        next_small = swap_core(pick(small_sums, 1 - core))
        both_small = own_small + next_small
        both_small = both_small + swap_tp(both_small)
        first_own, first_other = reduced[0], [swap_core(v) for v in reduced[0]]
    low_small = jnp.where(core == 0, own_small, next_small)
    high_small = jnp.where(core == 0, next_small, own_small)
    wide = jnp.concatenate([low_small[:6, :channels], high_small[:6, :channels]], axis=1)
    narrow = jnp.concatenate(
        [v[5:, channels : channels + heads] for v in (low_small, high_small)], axis=1
    )
    conv_sum = both_small[:5, channels:]
    gain_sum = lax.dynamic_slice_in_dim(
        both_small[6:8, :channels].reshape(-1), lax.axis_index("fsdp") * depth, depth, 0
    )

    second_own = [after(v, own_small) for v in reduced[1]]
    second_other = [swap_core(v) for v in second_own]
    either = lambda one, two: jnp.where(core == 0, one.astype(F32), two.astype(F32))
    low_half = [either(first_own[i], second_other[i]) for i in range(2)]
    high_half = [either(first_other[i], second_own[i]) for i in range(2)]

    def joined(begin, end, i=0):
        return jnp.concatenate([low_half[i][:, begin:end], high_half[i][:, begin:end]], axis=1)

    g_zx = join_halves(first_own[0], first_other[0], second_own[0], second_other[0], channels)
    at = 2 * channels
    g_bc = low_half[0][:, at : at + shared] + high_half[0][:, at : at + shared]
    g_bc = g_bc + swap_tp(g_bc)
    g_dt = joined(at + shared, at + shared + heads)
    g_back = joined(0, channels, 1)

    return (
        outputs,
        input_grads,
        gain_sum[None],
        g_zx[None],
        g_bc[None],
        g_dt[None],
        wide[:4][None],
        wide[4][None],
        conv_sum[:4][None],
        conv_sum[4][None],
        narrow[0][None],
        narrow[1][None],
        narrow[2][None],
        wide[5][None],
        g_back[None],
    )


def solution(mesh):
    placed = (
        P("fsdp", None, "tp", None),
        P("fsdp", None, "tp", None),
        P("section", "fsdp"),
        P("section", "fsdp", None, "tp"),
        P("section", "fsdp", None),
        P("section", "fsdp", "tp"),
        P("section", None, "tp"),
        P("section", "tp"),
        P("section", None, None),
        P("section", None),
        P("section", "tp"),
        P("section", "tp"),
        P("section", "tp"),
        P("section", "tp"),
        P("section", "fsdp", "tp"),
    )
    return jax.shard_map(
        local,
        mesh=mesh,
        in_specs=placed,
        out_specs=(
            P("fsdp", "section", "tp", None),
            P("fsdp", "section", "tp", None),
        )
        + placed[2:],
        check_vma=False,
    )
```
